128 devices in a mesh: batch: 2 (over core), sx: 8 (over y, x_lo), sy: 8 (over x_hi, z).
Axes of the slice: x: 4 (x_hi: 2, x_lo: 2; x = x_hi * 2 + x_lo), y: 4, z: 4, core: 2. Of those that a mesh axis runs over, the one named last changes fastest.
Arguments:
- features: bfloat16 [2, 32, 32, 64, 128], P('batch', None, 'sx', 'sy'), may hold values from -6 to 6
- labels: int32 [2, 32, 64, 128], P('batch', 'sx', 'sy'), may hold values from 0 to 3
- w_enc: bfloat16 [3, 3, 3, 32, 32], replicated, may hold values from -0.21875 to 0.21875
- w_mid: bfloat16 [3, 3, 3, 64, 32], replicated, may hold values from -0.21875 to 0.21875
- w_dec: bfloat16 [3, 3, 3, 32, 96], replicated, may hold values from -0.125 to 0.125
- w_out: bfloat16 [4, 32], replicated, may hold values from -1 to 1
Outputs:
- feature_grad: bfloat16 [2, 32, 32, 64, 128], P('batch', None, 'sx', 'sy')
- grad_enc: float32 [3, 3, 3, 32, 32], replicated
- grad_mid: float32 [3, 3, 3, 64, 32], replicated
- grad_dec: float32 [3, 3, 3, 32, 96], replicated
- grad_out: float32 [4, 32], replicated
The draws below stay inside these ranges and needn't reach their ends.
All inputs are finite; a program needn't handle non-finite values.
Results may differ from the reference program's by a relative error of at most 0.012.
Values may be sent and summed in bfloat16 or wider, within the bound.
A program may use at most 128 MiB of HBM per device.

```python
import jax
import jax.numpy as jnp
from jax import lax

C1 = 32
C2 = 64
K = 4
Z = 128
VOLS = 2
NX = 32
NY = 64


def draw_features(key, part):
    key = jax.random.fold_in(key, 11)
    shape = (VOLS, C1, NX, NY, Z)
    place_x = lax.broadcasted_iota(jnp.float32, (VOLS, 1, NX, 1, 1), 0) * NX + lax.broadcasted_iota(jnp.float32, (VOLS, 1, NX, 1, 1), 2)
    ramp = 0.5 + place_x / max(VOLS * NX - 1, 1)
    values = jnp.clip(jax.random.normal(key, shape, jnp.float32), -4.0, 4.0) * ramp
    return values.astype(jnp.bfloat16)


def plant(values, rng, least, top_value):
    longest = values.shape.index(max(values.shape))
    spots = []
    for shift in (0, 1):
        where = [jax.random.randint(jax.random.fold_in(rng, axis), (), 0, length) for axis, length in enumerate(values.shape)]
        where[longest] = (where[longest] + shift) % values.shape[longest]
        spots.append(tuple(where))
    return values.at[spots[0]].set(least).at[spots[1]].set(top_value)


def gaussian(own_key, extent, spread, bound, held_as=jnp.bfloat16):
    drawn = spread * jax.random.normal(own_key, extent, jnp.float32)
    return jnp.clip(drawn, min=-bound, max=bound).astype(held_as)


def setup_inputs(seed: int = 0) -> dict:
    key_list = jax.random.split(jax.random.key(seed), 7)
    return {
        "features": draw_features(jax.random.fold_in(key_list[6], 71), 0),
        "labels": plant(jax.random.randint(key_list[1], (VOLS, NX, NY, Z), 0, K), jax.random.fold_in(key_list[1], 1), 0, K - 1).astype(jnp.int32),
        "w_enc": gaussian(key_list[2], (3, 3, 3, C1, C1), (27 * C1) ** -0.5, 0.21875),
        "w_mid": gaussian(key_list[3], (3, 3, 3, C2, C1), (27 * C1) ** -0.5, 0.21875),
        "w_dec": gaussian(key_list[4], (3, 3, 3, C1, C2 + C1), (27 * (C1 + C2)) ** -0.5, 0.125),
        "w_out": gaussian(key_list[5], (K, C1), C1 ** -0.5, 1.0),
    }


loss_scale = 32.0

def conv_same(values, weight):
    left = values.astype(jnp.float32)[None]
    kernel = jnp.transpose(weight.astype(jnp.float32), (3, 4, 0, 1, 2))
    result = lax.conv_general_dilated(left, kernel, (1, 1, 1), ((1, 1), (1, 1), (1, 1)), dimension_numbers=('NCDHW', 'OIDHW', 'NCDHW'), precision=lax.Precision.HIGHEST)
    return result[0]

def conv_back(grads, weight):
    flipped = jnp.swapaxes(jnp.flip(weight, (0, 1, 2)), 3, 4)
    return conv_same(grads, flipped)

def weight_grad(values, grads):
    padded = jnp.pad(values.astype(jnp.float32), ((0, 0), (1, 1), (1, 1), (1, 1)))
    grads_wide = grads.astype(jnp.float32)
    size_x, size_y, size_z = (values.shape[1], values.shape[2], values.shape[3])
    pieces = []
    for shift_a in range(3):
        for shift_b in range(3):
            for shift_c in range(3):
                window = padded[:, shift_a:shift_a + size_x, shift_b:shift_b + size_y, shift_c:shift_c + size_z]
                pieces.append(jnp.einsum('oxyz,ixyz->oi', grads_wide, window, precision=lax.Precision.HIGHEST))
    stacked = jnp.stack(pieces)
    return stacked.reshape(3, 3, 3, stacked.shape[1], stacked.shape[2])

def grow(values):
    return jnp.repeat(jnp.repeat(jnp.repeat(values, 2, axis=1), 2, axis=2), 2, axis=3)

def blocks_of(values):
    chans, size_x, size_y, size_z = values.shape
    return values.astype(jnp.float32).reshape(chans, size_x // 2, 2, size_y // 2, 2, size_z // 2, 2)

def silu_slope(pre_act):
    sigmoid = jax.nn.sigmoid(pre_act)
    return sigmoid * (1.0 + pre_act * (1.0 - sigmoid))

def reference(features, labels, w_enc, w_mid, w_dec, w_out):
    classes = w_out.shape[0]
    chans_mid = w_mid.shape[3]
    total_enc = jnp.zeros(w_enc.shape, jnp.float32)
    total_mid = jnp.zeros(w_mid.shape, jnp.float32)
    total_dec = jnp.zeros(w_dec.shape, jnp.float32)
    total_out = jnp.zeros(w_out.shape, jnp.float32)
    feature_grads = []
    for volume in range(features.shape[0]):
        source = features[volume]
        enc_pre = conv_same(source, w_enc)
        enc_act = jax.nn.silu(enc_pre).astype(jnp.bfloat16)
        pooled = lax.optimization_barrier(jnp.mean(blocks_of(enc_act), axis=(2, 4, 6))).astype(jnp.bfloat16)
        mid_pre = conv_same(pooled, w_mid)
        mid_act = jax.nn.silu(mid_pre).astype(jnp.bfloat16)
        joined = jnp.concatenate([grow(mid_act), enc_act], axis=0)
        dec_pre = conv_same(joined, w_dec)
        dec_act = jax.nn.silu(dec_pre).astype(jnp.bfloat16)
        logits = jnp.einsum('kc,cxyz->kxyz', w_out.astype(jnp.float32), dec_act.astype(jnp.float32), precision=lax.Precision.HIGHEST)
        expo = jnp.exp(logits)
        prob = expo / lax.optimization_barrier(jnp.sum(expo, axis=0, keepdims=True))
        onehot = (labels[volume][None] == jnp.arange(classes, dtype=jnp.int32)[:, None, None, None]).astype(jnp.float32)
        logit_grad = (loss_scale * (prob - onehot)).astype(jnp.bfloat16)
        total_out = total_out + jnp.einsum('kxyz,cxyz->kc', logit_grad.astype(jnp.float32), dec_act.astype(jnp.float32), precision=lax.Precision.HIGHEST)
        act_grad = jnp.einsum('kc,kxyz->cxyz', w_out.astype(jnp.float32), logit_grad.astype(jnp.float32), precision=lax.Precision.HIGHEST)
        dec_grad = (act_grad * silu_slope(dec_pre)).astype(jnp.bfloat16)
        total_dec = total_dec + weight_grad(joined, dec_grad)
        joined_grad = conv_back(dec_grad, w_dec)
        up_grad = joined_grad[:chans_mid]
        skip_grad = joined_grad[chans_mid:]
        mid_grad = (lax.optimization_barrier(jnp.sum(blocks_of(up_grad), axis=(2, 4, 6))) * silu_slope(mid_pre)).astype(jnp.bfloat16)
        total_mid = total_mid + weight_grad(pooled, mid_grad)
        pooled_grad = conv_back(mid_grad, w_mid)
        enc_grad = ((skip_grad + grow(pooled_grad) * 0.125) * silu_slope(enc_pre)).astype(jnp.bfloat16)
        total_enc = total_enc + weight_grad(source, enc_grad)
        feature_grads.append(conv_back(enc_grad, w_enc).astype(jnp.bfloat16))
    scale = 1.0 / (features.shape[0] * features.shape[2] * features.shape[3] * features.shape[4])
    return (jnp.stack(feature_grads), total_enc * scale, total_mid * scale, total_dec * scale, total_out * scale)
```

```python
import functools

import jax
import jax.numpy as jnp
from jax import lax
from jax.experimental import pallas as pl
from jax.experimental.pallas import tpu as pltpu
from jax.sharding import PartitionSpec as P

loss_scale = 32.0
LANES = 128
MESH = pl.DeviceIdType.MESH
f32 = jnp.float32
bf16 = jnp.bfloat16

DIRS = [(dx, dy) for dx in (-1, 0, 1) for dy in (-1, 0, 1) if (dx, dy) != (0, 0)]
FEAT, POOL, SKIP, MID, DECG, MIDG, ENCG = range(7)
DEC, MIDW, ENC = range(3)


def lane_tile(y, count=1):
    if isinstance(y, int):
        return pl.ds(y * LANES, count * LANES)
    return pl.ds(pl.multiple_of(y * LANES, LANES), count * LANES)


def sigmoid(u):
    return 1.0 / (1.0 + jnp.exp(-u))


def shifted(tile, shift):
    lane = lax.broadcasted_iota(jnp.int32, tile.shape, 1)
    before = jnp.where(lane >= shift, pltpu.roll(tile, shift, axis=1), 0.0)
    after = jnp.where(lane < LANES - shift, pltpu.roll(tile, LANES - shift, axis=1), 0.0)
    return before.astype(bf16), after.astype(bf16)


def pair_sum(tile):
    lane = lax.broadcasted_iota(jnp.int32, tile.shape, 1)
    other = jnp.where(
        lane % 2 == 0, pltpu.roll(tile, LANES - 1, axis=1), pltpu.roll(tile, 1, axis=1)
    )
    return tile + other


def put_stack(buf, x, y, tile, period, offset, shift):
    chans = tile.shape[0]
    before, after = shifted(tile, shift)
    lanes = lane_tile(y)
    buf[x, offset : offset + chans, lanes] = before
    buf[x, period + offset : period + offset + chans, lanes] = tile.astype(bf16)
    buf[x, 2 * period + offset : 2 * period + offset + chans, lanes] = after


def finish_stack(buf, x, y, chans, period, offset, shift):
    lanes = lane_tile(y)
    tile = buf[x, period + offset : period + offset + chans, lanes].astype(f32)
    before, after = shifted(tile, shift)
    buf[x, offset : offset + chans, lanes] = before
    buf[x, 2 * period + offset : 2 * period + offset + chans, lanes] = after


def finish_halo(buf, nx, ny, chans, period, offset, shift):
    def step_y(y, carry):
        finish_stack(buf, 0, y, chans, period, offset, shift)
        finish_stack(buf, nx + 1, y, chans, period, offset, shift)
        return carry

    lax.fori_loop(0, ny + 2, step_y, 0)

    def step_x(x, carry):
        finish_stack(buf, x, 0, chans, period, offset, shift)
        finish_stack(buf, x, ny + 1, chans, period, offset, shift)
        return carry

    lax.fori_loop(1, nx + 1, step_x, 0)


def clear_halo(buf, nx, ny, low, high):
    width = (ny + 2) * LANES
    buf[0, low:high, :] = jnp.zeros((high - low, width), bf16)
    buf[nx + 1, low:high, :] = jnp.zeros((high - low, width), bf16)
    for x in range(1, nx + 1):
        buf[x, low:high, lane_tile(0)] = jnp.zeros((high - low, LANES), bf16)
        buf[x, low:high, lane_tile(ny + 1)] = jnp.zeros((high - low, LANES), bf16)


def taps(buf, x, y, count, low, high):
    depth = buf.shape[1]
    parts = []
    for window in range(9):
        first, last = max(low, window * depth), min(high, (window + 1) * depth)
        if first < last:
            a, b = divmod(window, 3)
            parts.append(
                buf[x + a, first - window * depth : last - window * depth, lane_tile(y + b, count)]
            )
    return parts[0] if len(parts) == 1 else jnp.concatenate(parts, axis=0)


def conv(weight, buf, x, y, count):
    window = taps(buf, x, y, count, 0, 9 * buf.shape[1])
    return jnp.dot(weight[...], window, preferred_element_type=f32)


def weight_grad(total, grads, buf, x, count, first):
    width = 9 * buf.shape[1]
    for low in range(0, width, 256):
        high = min(low + 256, width)
        term = lax.dot_general(
            grads,
            taps(buf, x, 0, count, low, high),
            (((1,), (1,)), ((), ())),
            preferred_element_type=f32,
        )
        if first:
            total[:, low:high] = term
        else:
            total[:, low:high] += term


def kernel(
    sizes,
    feat,
    labels,
    w_enc_f,
    w_enc_b,
    w_mid_f,
    w_mid_b,
    w_dec_f,
    w_dec_b,
    w_out,
    feature_grad,
    grad_enc,
    grad_mid,
    grad_dec,
    grad_out,
    F,
    PO,
    U,
    J,
    D,
    MG,
    EG,
    enc_slope,
    mid_slope,
    skip,
    out_total,
    total_dec,
    total_mid,
    total_enc,
    part_dec,
    part_mid,
    part_enc,
    rs_dec,
    rs_mid,
    rs_enc,
    ar_dec,
    ar_mid,
    ar_enc,
    ag_dec,
    ag_mid,
    ag_enc,
    halo_send,
    halo_recv,
    rs_send,
    rs_recv,
    ar_send,
    ar_recv,
    ag_send,
    ag_recv,
):
    nb, nsx, nsy, nx, ny, scale = sizes
    cx, cy = nx // 2, ny // 2
    group = nb * nsy
    bt, sx, sy = lax.axis_index("batch"), lax.axis_index("sx"), lax.axis_index("sy")
    here = bt * nsy + sy

    clear_halo(F, nx, ny, 32, 64)
    clear_halo(PO, cx, cy, 32, 64)
    clear_halo(J, nx, ny, 160, 192)
    clear_halo(U, cx, cy, 0, 64)
    clear_halo(D, nx, ny, 32, 64)
    clear_halo(MG, cx, cy, 64, 128)
    clear_halo(EG, nx, ny, 32, 64)

    def sx_peer(k):
        return lax.rem(sx + k, nsx)

    def group_peer(k):
        return lax.rem(here + k, group)

    def group_id(q):
        return (q // nsy, sx, lax.rem(q, nsy))

    barrier = pltpu.get_barrier_semaphore()
    for k in range(1, nsx):
        pl.semaphore_signal(barrier, inc=1, device_id=(bt, sx_peer(k), sy), device_id_type=MESH)
    for k in range(1, group):
        pl.semaphore_signal(barrier, inc=1, device_id=group_id(group_peer(k)), device_id_type=MESH)
    for dx in (1, nsx - 1):
        for dy in (1, nsy - 1):
            pl.semaphore_signal(
                barrier,
                inc=1,
                device_id=(bt, lax.rem(sx + dx, nsx), lax.rem(sy + dy, nsy)),
                device_id_type=MESH,
            )

    def load_features(x, carry):
        for y in range(ny):
            put_stack(F, x + 1, y + 1, feat[x, :, lane_tile(y)].astype(f32), 32, 0, 1)
        return carry

    lax.fori_loop(0, nx, load_features, 0)
    total_dec[...] = jnp.zeros(total_dec.shape, f32)
    total_mid[...] = jnp.zeros(total_mid.shape, f32)
    total_enc[...] = jnp.zeros(total_enc.shape, f32)
    out_total[...] = jnp.zeros(out_total.shape, f32)

    pl.semaphore_wait(barrier, nsx - 1 + group - 1 + 4)

    fields = {
        FEAT: (F, nx, ny, 32, 64),
        POOL: (PO, cx, cy, 32, 64),
        SKIP: (J, nx, ny, 160, 192),
        MID: (U, cx, cy, 0, 64),
        DECG: (D, nx, ny, 32, 64),
        MIDG: (MG, cx, cy, 64, 128),
        ENCG: (EG, nx, ny, 32, 64),
    }

    def halo_copy(field, index):
        buf, sizex, sizey, low, high = fields[field]
        dx, dy = DIRS[index]

        def source(step, size):
            return {-1: (1, 1), 0: (1, size), 1: (size, 1)}[step]

        def target(step, size):
            return {-1: (size + 1, 1), 0: (1, size), 1: (0, 1)}[step]

        (x0, xn), (y0, yn) = source(dx, sizex), source(dy, sizey)
        (tx0, _), (ty0, _) = target(dx, sizex), target(dy, sizey)
        return pltpu.make_async_remote_copy(
            src_ref=buf.at[pl.ds(x0, xn), low:high, lane_tile(y0, yn)],
            dst_ref=buf.at[pl.ds(tx0, xn), low:high, lane_tile(ty0, yn)],
            send_sem=halo_send.at[field, index],
            recv_sem=halo_recv.at[field, index],
            device_id=(bt, lax.rem(sx + dx + nsx, nsx), lax.rem(sy + dy + nsy, nsy)),
            device_id_type=MESH,
        )

    def inside(dx, dy):
        ok = None
        for step, at, size in ((dx, sx, nsx), (dy, sy, nsy)):
            if step:
                this = at > 0 if step < 0 else at < size - 1
                ok = this if ok is None else jnp.logical_and(ok, this)
        return ok

    def start_halo(field):
        for index, (dx, dy) in enumerate(DIRS):

            @pl.when(inside(dx, dy))
            def _():
                halo_copy(field, index).start()

    def wait_halo(field):
        for index, (dx, dy) in enumerate(DIRS):

            @pl.when(inside(-dx, -dy))
            def _():
                halo_copy(field, index).wait_recv()

    def wait_halo_sent(field):
        for index, (dx, dy) in enumerate(DIRS):

            @pl.when(inside(dx, dy))
            def _():
                halo_copy(field, index).wait_send()

    sums = {
        DEC: (total_dec, part_dec, rs_dec, ar_dec, ag_dec, 32, 384),
        MIDW: (total_mid, part_mid, rs_mid, ar_mid, ag_mid, 64, 128),
        ENC: (total_enc, part_enc, rs_enc, ar_enc, ag_enc, 32, 128),
    }

    def rs_copy(g, k):
        _, part, landing, _, _, _, _ = sums[g]
        return pltpu.make_async_remote_copy(
            src_ref=part.at[sx_peer(k)],
            dst_ref=landing.at[sx],
            send_sem=rs_send.at[g, k - 1],
            recv_sem=rs_recv.at[g, k - 1],
            device_id=(bt, sx_peer(k), sy),
            device_id_type=MESH,
        )

    def rs_arrival(g, k):
        _, part, landing, _, _, _, _ = sums[g]
        origin = sx_peer(nsx - k)
        return pltpu.make_async_remote_copy(
            src_ref=part.at[origin],
            dst_ref=landing.at[origin],
            send_sem=rs_send.at[g, k - 1],
            recv_sem=rs_recv.at[g, k - 1],
            device_id=(bt, origin, sy),
            device_id_type=MESH,
        )

    def ar_copy(g, k):
        landing = sums[g][3]
        return pltpu.make_async_remote_copy(
            src_ref=landing.at[here],
            dst_ref=landing.at[here],
            send_sem=ar_send.at[g, k - 1],
            recv_sem=ar_recv.at[g, k - 1],
            device_id=group_id(group_peer(k)),
            device_id_type=MESH,
        )

    def ar_arrival(g, k):
        landing = sums[g][3]
        origin = group_peer(group - k)
        return pltpu.make_async_remote_copy(
            src_ref=landing.at[origin],
            dst_ref=landing.at[origin],
            send_sem=ar_send.at[g, k - 1],
            recv_sem=ar_recv.at[g, k - 1],
            device_id=group_id(origin),
            device_id_type=MESH,
        )

    def ag_copy(g, k):
        landing = sums[g][4]
        return pltpu.make_async_remote_copy(
            src_ref=landing.at[sx],
            dst_ref=landing.at[sx],
            send_sem=ag_send.at[g, k - 1],
            recv_sem=ag_recv.at[g, k - 1],
            device_id=(bt, sx_peer(k), sy),
            device_id_type=MESH,
        )

    def ag_arrival(g, k):
        landing = sums[g][4]
        origin = sx_peer(nsx - k)
        return pltpu.make_async_remote_copy(
            src_ref=landing.at[origin],
            dst_ref=landing.at[origin],
            send_sem=ag_send.at[g, k - 1],
            recv_sem=ag_recv.at[g, k - 1],
            device_id=(bt, origin, sy),
            device_id_type=MESH,
        )

    def start_scatter(g):
        total, part, _, _, _, _, length = sums[g]
        for j in range(nsx):
            part[j] = total[:, j * length : (j + 1) * length].astype(bf16)
        for k in range(1, nsx):
            rs_copy(g, k).start()

    def start_exchange(g):
        total, _, landing, mine, _, _, length = sums[g]
        for k in range(1, nsx):
            rs_arrival(g, k).wait_recv()
        acc = total[:, pl.ds(pl.multiple_of(sx * length, LANES), length)]
        for k in range(1, nsx):
            acc = acc + landing[sx_peer(k)].astype(f32)
        mine[here] = acc.astype(bf16)
        for k in range(1, group):
            ar_copy(g, k).start()

    def start_gather(g):
        _, _, _, landing, result, _, _ = sums[g]
        for k in range(1, group):
            ar_arrival(g, k).wait_recv()
        acc = landing[0].astype(f32)
        for q in range(1, group):
            acc = acc + landing[q].astype(f32)
        result[sx] = acc.astype(bf16)
        for k in range(1, nsx):
            ag_copy(g, k).start()

    def finish_sum(g, out, chans, factor):
        result = sums[g][4]
        for k in range(1, nsx):
            ag_arrival(g, k).wait_recv()
        for t in range(27):
            j, at = divmod(t, 4)
            out[t] = result[j, :, at * chans : (at + 1) * chans].astype(f32) * factor

    def wait_sum_sent(g):
        for k in range(1, nsx):
            rs_copy(g, k).wait_send()
        for k in range(1, group):
            ar_copy(g, k).wait_send()
        for k in range(1, nsx):
            ag_copy(g, k).wait_send()

    start_halo(FEAT)
    wait_halo(FEAT)
    finish_halo(F, nx, ny, 32, 32, 0, 1)

    def enc_block(bx, carry):
        for by in range(cy):
            block = jnp.zeros((32, LANES), f32)
            for dx in range(2):
                x = 2 * bx + dx
                pre = conv(w_enc_f, F, x, 2 * by, 2)
                s = sigmoid(pre)
                enc_slope[x, :, lane_tile(2 * by, 2)] = s * (1.0 + pre * (1.0 - s))
                act = (pre * s).astype(bf16).astype(f32)
                for dy in range(2):
                    tile = act[:, dy * LANES : (dy + 1) * LANES]
                    put_stack(J, x + 1, 2 * by + dy + 1, tile, 96, 64, 1)
                    block = block + tile
            put_stack(PO, bx + 1, by + 1, pair_sum(block) * 0.125, 32, 0, 2)
        return carry

    lax.fori_loop(0, cx, enc_block, 0)
    start_halo(POOL)
    start_halo(SKIP)
    wait_halo(POOL)
    finish_halo(PO, cx, cy, 32, 32, 0, 2)

    def mid_block(bx, carry):
        for by in range(0, cy, 2):
            pre = conv(w_mid_f, PO, bx, by, 2)
            s = sigmoid(pre)
            mid_slope[bx, :, lane_tile(by, 2)] = s * (1.0 + pre * (1.0 - s))
            U[bx + 1, :, lane_tile(by + 1, 2)] = (pre * s).astype(bf16)
        return carry

    lax.fori_loop(0, cx, mid_block, 0)
    start_halo(MID)
    wait_halo(SKIP)
    finish_halo(J, nx, ny, 32, 96, 64, 1)
    wait_halo(MID)

    for bx in range(cx + 2):
        for by in range(cy + 2):
            tile = U[bx, :, lane_tile(by)]
            before, after = shifted(tile.astype(f32), 1)
            for x in (2 * bx - 1, 2 * bx):
                for y in (2 * by - 1, 2 * by):
                    if 0 <= x <= nx + 1 and 0 <= y <= ny + 1:
                        lanes = lane_tile(y)
                        J[x, 0:64, lanes] = before
                        J[x, 96:160, lanes] = tile
                        J[x, 192:256, lanes] = after

    def dec_row(x, carry):
        for y in range(0, ny, 2):
            pre = conv(w_dec_f, J, x, y, 2)
            s = sigmoid(pre)
            slope = s * (1.0 + pre * (1.0 - s))
            act = (pre * s).astype(bf16)
            logits = jnp.dot(w_out[...], act, preferred_element_type=f32)
            expo = jnp.exp(logits)
            prob = expo / jnp.sum(expo, axis=0, keepdims=True)
            ids = lax.broadcasted_iota(jnp.int32, prob.shape, 0)
            these = jnp.concatenate([labels[x, y : y + 1, :], labels[x, y + 1 : y + 2, :]], axis=1)
            onehot = (these == ids).astype(f32)
            logit_grad = (loss_scale * (prob - onehot)).astype(bf16)
            out_total[...] += lax.dot_general(
                logit_grad, act, (((1,), (1,)), ((), ())), preferred_element_type=f32
            )
            act_grad = lax.dot_general(
                w_out[...], logit_grad, (((0,), (0,)), ((), ())), preferred_element_type=f32
            )
            grads = act_grad * slope
            grads = grads.astype(bf16).astype(f32)
            for dy in range(2):
                tile = grads[:, dy * LANES : (dy + 1) * LANES]
                put_stack(D, x + 1, y + dy + 1, tile, 32, 0, 1)
        return carry

    lax.fori_loop(0, nx, dec_row, 0)
    start_halo(DECG)

    def dec_weights(x, carry):
        grads = D[x + 1, 32:64, lane_tile(1, ny)]
        weight_grad(total_dec, grads, J, x, ny, False)
        return carry

    lax.fori_loop(0, nx, dec_weights, 0)
    total_dec[0:4, 2592:2624] = out_total[...]
    start_scatter(DEC)

    wait_halo(DECG)
    finish_halo(D, nx, ny, 32, 32, 0, 1)

    def dec_back(bx, carry):
        for by in range(cy):
            block = jnp.zeros((64, LANES), f32)
            for dx in range(2):
                x = 2 * bx + dx
                joined = conv(w_dec_b, D, x, 2 * by, 2)
                skip[x, :, lane_tile(2 * by, 2)] = joined[64:96]
                block = block + joined[0:64, 0:LANES] + joined[0:64, LANES : 2 * LANES]
            grads = pair_sum(block) * mid_slope[bx, :, lane_tile(by)]
            put_stack(MG, bx + 1, by + 1, grads, 64, 0, 2)
        return carry

    lax.fori_loop(0, cx, dec_back, 0)
    start_halo(MIDG)

    for bx in range(cx):
        weight_grad(total_mid, MG[bx + 1, 64:128, lane_tile(1, cy)], PO, bx, cy, bx == 0)
    start_scatter(MIDW)
    start_exchange(DEC)

    wait_halo(MIDG)
    finish_halo(MG, cx, cy, 64, 64, 0, 2)

    def mid_back(bx, carry):
        for by in range(0, cy, 2):
            pooled = conv(w_mid_b, MG, bx, by, 2) * 0.125
            for dx in range(2):
                x = 2 * bx + dx
                for dy in range(4):
                    y = 2 * by + dy
                    up = pooled[:, (dy // 2) * LANES : (dy // 2 + 1) * LANES]
                    tile = (skip[x, :, lane_tile(y)] + up) * enc_slope[x, :, lane_tile(y)]
                    put_stack(EG, x + 1, y + 1, tile, 32, 0, 1)
        return carry

    lax.fori_loop(0, cx, mid_back, 0)
    start_halo(ENCG)

    def enc_weights(x, carry):
        grads = EG[x + 1, 32:64, lane_tile(1, ny)]
        weight_grad(total_enc, grads, F, x, ny, False)
        return carry

    lax.fori_loop(0, nx, enc_weights, 0)
    start_scatter(ENC)
    start_exchange(MIDW)
    start_gather(DEC)

    wait_halo(ENCG)
    finish_halo(EG, nx, ny, 32, 32, 0, 1)
    start_exchange(ENC)

    def enc_back(x, carry):
        for y in range(0, ny, 2):
            feature_grad[x, :, lane_tile(y, 2)] = conv(w_enc_b, EG, x, y, 2).astype(bf16)
        return carry

    lax.fori_loop(0, nx, enc_back, 0)

    start_gather(MIDW)
    finish_sum(DEC, grad_dec, 96, scale)
    grad_out[...] = ag_dec[6, 0:16, 288:320].astype(f32)[0:4] * scale
    start_gather(ENC)
    finish_sum(MIDW, grad_mid, 32, 0.5 * scale)
    finish_sum(ENC, grad_enc, 32, scale)

    for g in (DEC, MIDW, ENC):
        wait_sum_sent(g)
    for field in range(7):
        wait_halo_sent(field)


def forward_weights(w):
    taps_count, outs, ins = 27, w.shape[3], w.shape[4]
    return w.reshape(taps_count, outs, ins).transpose(1, 0, 2).reshape(outs, taps_count * ins)


def backward_weights(w):
    taps_count, outs, ins = 27, w.shape[3], w.shape[4]
    flipped = w.reshape(taps_count, outs, ins)[::-1]
    return flipped.transpose(2, 0, 1).reshape(ins, taps_count * outs)


def shards(features, labels, w_enc, w_mid, w_dec, w_out):
    nb, nsx, nsy = lax.axis_size("batch"), lax.axis_size("sx"), lax.axis_size("sy")
    _, chans, nx, ny, nz = features.shape
    cx, cy = nx // 2, ny // 2
    scale = 1.0 / float(nb * nsx * nsy * nx * ny * nz)
    source = features[0].transpose(1, 0, 2, 3).reshape(nx, chans, ny * nz)
    group = nb * nsy

    def fine(depth):
        return pltpu.VMEM((nx + 2, depth, (ny + 2) * LANES), bf16)

    def coarse(depth):
        return pltpu.VMEM((cx + 2, depth, (cy + 2) * LANES), bf16)

    pieces = ((32, 384), (64, 128), (32, 128))
    scratch = [
        fine(96),
        coarse(96),
        coarse(64),
        fine(288),
        fine(96),
        coarse(192),
        fine(96),
        pltpu.VMEM((nx, 32, ny * LANES), f32),
        pltpu.VMEM((cx, 64, cy * LANES), f32),
        pltpu.VMEM((nx, 32, ny * LANES), f32),
        pltpu.VMEM((4, 32), f32),
    ]
    scratch += [pltpu.VMEM((rows, nsx * length), f32) for rows, length in pieces]
    scratch += [pltpu.VMEM((nsx, rows, length), bf16) for rows, length in pieces]
    scratch += [pltpu.VMEM((nsx, rows, length), bf16) for rows, length in pieces]
    scratch += [pltpu.VMEM((group, rows, length), bf16) for rows, length in pieces]
    scratch += [pltpu.VMEM((nsx, rows, length), bf16) for rows, length in pieces]
    scratch += [pltpu.SemaphoreType.DMA((7, 8))] * 2
    scratch += [pltpu.SemaphoreType.DMA((3, nsx - 1))] * 2
    scratch += [pltpu.SemaphoreType.DMA((3, group - 1))] * 2
    scratch += [pltpu.SemaphoreType.DMA((3, nsx - 1))] * 2

    vmem = pl.BlockSpec(memory_space=pltpu.VMEM)
    feature_grad, grad_enc, grad_mid, grad_dec, grad_out = pl.pallas_call(
        functools.partial(kernel, (nb, nsx, nsy, nx, ny, scale)),
        out_shape=(
            jax.ShapeDtypeStruct((nx, chans, ny * nz), bf16),
            jax.ShapeDtypeStruct((27, 32, 32), f32),
            jax.ShapeDtypeStruct((27, 64, 32), f32),
            jax.ShapeDtypeStruct((27, 32, 96), f32),
            jax.ShapeDtypeStruct((4, 32), f32),
        ),
        in_specs=[vmem] * 9,
        out_specs=[vmem] * 5,
        scratch_shapes=scratch,
        compiler_params=pltpu.CompilerParams(
            collective_id=0, has_side_effects=True, vmem_limit_bytes=48 * 1024 * 1024
        ),
        name="unet_step",
    )(
        source,
        labels[0],
        forward_weights(w_enc),
        backward_weights(w_enc),
        forward_weights(w_mid),
        backward_weights(w_mid),
        forward_weights(w_dec),
        backward_weights(w_dec),
        w_out,
    )
    feature_grad = feature_grad.reshape(nx, chans, ny, nz).transpose(1, 0, 2, 3)[None]
    return (
        feature_grad,
        grad_enc.reshape(w_enc.shape),
        grad_mid.reshape(w_mid.shape),
        grad_dec.reshape(w_dec.shape),
        grad_out,
    )


def solution(mesh):
    placed = (P("batch", None, "sx", "sy", None), P("batch", "sx", "sy", None), P(), P(), P(), P())
    return jax.shard_map(
        shards,
        mesh=mesh,
        in_specs=placed,
        out_specs=(P("batch", None, "sx", "sy", None), P(), P(), P(), P()),
        check_vma=False,
    )
```

```python
import functools

import jax
import jax.numpy as jnp
from jax import lax
from jax.experimental import pallas as pl
from jax.experimental.pallas import tpu as pltpu
from jax.sharding import PartitionSpec as P

loss_scale = 32.0
LANES = 128
MESH = pl.DeviceIdType.MESH
f32 = jnp.float32
bf16 = jnp.bfloat16

DIRS = [(dx, dy) for dx in (-1, 0, 1) for dy in (-1, 0, 1) if (dx, dy) != (0, 0)]
FEAT, POOL, SKIP, MID, DECG, MIDG, ENCG = range(7)
DEC, MIDW, ENC = range(3)


def lane_tile(y, count=1):
    if isinstance(y, int):
        return pl.ds(y * LANES, count * LANES)
    return pl.ds(pl.multiple_of(y * LANES, LANES), count * LANES)


def sigmoid(u):
    return 1.0 / (1.0 + jnp.exp(-u))


def shifted(tile, shift):
    lane = lax.broadcasted_iota(jnp.int32, tile.shape, 1)
    before = jnp.where(lane >= shift, pltpu.roll(tile, shift, axis=1), 0.0)
    after = jnp.where(lane < LANES - shift, pltpu.roll(tile, LANES - shift, axis=1), 0.0)
    return before.astype(bf16), after.astype(bf16)


def pair_sum(tile):
    lane = lax.broadcasted_iota(jnp.int32, tile.shape, 1)
    other = jnp.where(
        lane % 2 == 0, pltpu.roll(tile, LANES - 1, axis=1), pltpu.roll(tile, 1, axis=1)
    )
    return tile + other


def packed(tile):
    half = tile.shape[0] // 2
    lane = lax.broadcasted_iota(jnp.int32, (half, LANES), 1)
    return jnp.where(lane % 2 == 0, tile[:half], tile[half:]).astype(bf16)


def unpacked(tile):
    tile = tile.astype(f32)
    lane = lax.broadcasted_iota(jnp.int32, tile.shape, 1)
    first = jnp.where(lane % 2 == 0, tile, pltpu.roll(tile, 1, axis=1))
    second = jnp.where(lane % 2 == 1, tile, pltpu.roll(tile, LANES - 1, axis=1))
    return jnp.concatenate([first, second], axis=0)


def put_sides(buf, x, y, tile, period, offset, shift, back):
    chans = tile.shape[0]
    before, after = shifted(tile, shift)
    lanes = lane_tile(y)
    buf[x, offset : offset + chans, lanes] = after if back else before
    buf[x, 2 * period + offset : 2 * period + offset + chans, lanes] = before if back else after


def put_stack(buf, x, y, tile, period, offset, shift, back=False):
    chans = tile.shape[0]
    buf[x, period + offset : period + offset + chans, lane_tile(y)] = tile.astype(bf16)
    put_sides(buf, x, y, tile, period, offset, shift, back)


def over_halo(nx, ny, step):
    def step_y(y, carry):
        step(0, y)
        step(nx + 1, y)
        return carry

    lax.fori_loop(0, ny + 2, step_y, 0)

    def step_x(x, carry):
        step(x, 0)
        step(x, ny + 1)
        return carry

    lax.fori_loop(1, nx + 1, step_x, 0)


def finish_halo(buf, nx, ny, chans, period, offset, shift, back=False):
    def step(x, y):
        tile = buf[x, period + offset : period + offset + chans, lane_tile(y)].astype(f32)
        put_sides(buf, x, y, tile, period, offset, shift, back)

    over_halo(nx, ny, step)


def unpack_halo(buf, landed, nx, ny, chans, back=False):
    def step(x, y):
        put_stack(buf, x, y, unpacked(landed[x, :, lane_tile(y)]), chans, 0, 2, back)

    over_halo(nx, ny, step)


def clear_halo(buf, nx, ny, low, high):
    width = (ny + 2) * LANES
    buf[0, low:high, :] = jnp.zeros((high - low, width), bf16)
    buf[nx + 1, low:high, :] = jnp.zeros((high - low, width), bf16)
    for x in range(1, nx + 1):
        buf[x, low:high, lane_tile(0)] = jnp.zeros((high - low, LANES), bf16)
        buf[x, low:high, lane_tile(ny + 1)] = jnp.zeros((high - low, LANES), bf16)


def taps(buf, x, y, count, rows, low, high, back=False):
    base, depth = rows[0], rows[1] - rows[0]
    parts = []
    for window in range(9):
        first, last = max(low, window * depth), min(high, (window + 1) * depth)
        if first < last:
            a, b = divmod(8 - window if back else window, 3)
            start = base - window * depth
            parts.append(buf[x + a, start + first : start + last, lane_tile(y + b, count)])
    return parts[0] if len(parts) == 1 else jnp.concatenate(parts, axis=0)


def conv(weight, buf, x, y, count, back=False):
    depth = buf.shape[1]
    window = taps(buf, x, y, count, (0, depth), 0, 9 * depth, back)
    return jnp.dot(weight[...], window, preferred_element_type=f32)


def weight_grad(total, grads, buf, size_x, count, rows):
    width = 9 * (rows[1] - rows[0])
    for low in range(0, width, 256):
        high = min(low + 256, width)
        acc = None
        for x in range(size_x):
            term = lax.dot_general(
                grads(x),
                taps(buf, x, 0, count, rows, low, high),
                (((1,), (1,)), ((), ())),
                preferred_element_type=f32,
            )
            acc = term if acc is None else acc + term
        total[:, low:high] = acc
    rest = total.shape[1] - width
    total[:, width:] = jnp.zeros((total.shape[0], rest), f32)


def forward_weights(dest, w):
    for low in range(0, 27, 4):
        high = min(low + 4, 27)
        dest[:, low * 32 : high * 32] = jnp.concatenate([w[t] for t in range(low, high)], axis=1)


def window_weights(dest, w):
    for b in range(3):
        parts = [w[(a * 3 + b) * 3 + c] for a in range(3) for c in range(3)]
        dest[b * 32 : (b + 1) * 32, :] = jnp.concatenate(parts, axis=1)


def backward_weights(dest, w):
    count, outs, ins = w.shape
    flat = w[...].astype(f32).reshape(count * outs, ins)
    dest[...] = flat.T.astype(bf16)


def kernel(
    sizes,
    feat,
    labels,
    w_enc,
    w_mid,
    w_dec,
    w_out,
    feature_grad,
    grad_enc,
    grad_mid,
    grad_dec,
    grad_out,
    w_enc_f,
    w_enc_b,
    w_mid_f,
    w_mid_b,
    w_dec_f,
    w_dec_b,
    rows32,
    window_sums,
    F,
    PO,
    PP,
    UP,
    J,
    D,
    MG,
    MGP,
    EG,
    enc_slope,
    mid_slope,
    skip,
    out_total,
    total_dec,
    total_mid,
    total_enc,
    part_dec,
    part_mid,
    part_enc,
    rs_dec,
    rs_mid,
    rs_enc,
    ar_dec,
    ar_mid,
    ar_enc,
    ag_dec,
    ag_mid,
    ag_enc,
    halo_send,
    halo_recv,
    rs_send,
    rs_recv,
    ar_send,
    ar_recv,
    ag_send,
    ag_recv,
):
    nb, nsx, nsy, nx, ny, scale = sizes
    cx, cy = nx // 2, ny // 2
    group = nb * nsy
    bt, sx, sy = lax.axis_index("batch"), lax.axis_index("sx"), lax.axis_index("sy")
    here = bt * nsy + sy

    clear_halo(F, nx, ny, 32, 64)
    clear_halo(PP, cx, cy, 0, 16)
    clear_halo(J, nx, ny, 160, 192)
    clear_halo(UP, cx, cy, 0, 32)
    clear_halo(D, nx, ny, 32, 64)
    clear_halo(MGP, cx, cy, 0, 32)
    clear_halo(EG, nx, ny, 32, 64)

    def sx_peer(k):
        return lax.rem(sx + k, nsx)

    def group_peer(k):
        return lax.rem(here + k, group)

    def group_id(q):
        return (q // nsy, sx, lax.rem(q, nsy))

    barrier = pltpu.get_barrier_semaphore()
    for k in range(1, nsx):
        pl.semaphore_signal(barrier, inc=1, device_id=(bt, sx_peer(k), sy), device_id_type=MESH)
    for k in range(1, group):
        pl.semaphore_signal(barrier, inc=1, device_id=group_id(group_peer(k)), device_id_type=MESH)
    for dx in (1, nsx - 1):
        for dy in (1, nsy - 1):
            pl.semaphore_signal(
                barrier,
                inc=1,
                device_id=(bt, lax.rem(sx + dx, nsx), lax.rem(sy + dy, nsy)),
                device_id_type=MESH,
            )

    def load_features(x, carry):
        rows32[x] = feat[:, x].astype(f32).reshape(32 * ny, LANES)
        for y in range(ny):
            put_stack(F, x + 1, y + 1, rows32[x, pl.ds(y, 32, stride=ny), :], 32, 0, 1)
        return carry

    lax.fori_loop(0, nx, load_features, 0)

    pl.semaphore_wait(barrier, nsx - 1 + group - 1 + 4)

    fields = {
        FEAT: (F, nx, ny, 32, 64),
        POOL: (PP, cx, cy, 0, 16),
        SKIP: (J, nx, ny, 160, 192),
        MID: (UP, cx, cy, 0, 32),
        DECG: (D, nx, ny, 32, 64),
        MIDG: (MGP, cx, cy, 0, 32),
        ENCG: (EG, nx, ny, 32, 64),
    }

    def halo_copy(field, index):
        buf, sizex, sizey, low, high = fields[field]
        dx, dy = DIRS[index]

        def source(step, size):
            return {-1: (1, 1), 0: (1, size), 1: (size, 1)}[step]

        def target(step, size):
            return {-1: (size + 1, 1), 0: (1, size), 1: (0, 1)}[step]

        (x0, xn), (y0, yn) = source(dx, sizex), source(dy, sizey)
        (tx0, _), (ty0, _) = target(dx, sizex), target(dy, sizey)
        return pltpu.make_async_remote_copy(
            src_ref=buf.at[pl.ds(x0, xn), low:high, lane_tile(y0, yn)],
            dst_ref=buf.at[pl.ds(tx0, xn), low:high, lane_tile(ty0, yn)],
            send_sem=halo_send.at[field, index],
            recv_sem=halo_recv.at[field, index],
            device_id=(bt, lax.rem(sx + dx + nsx, nsx), lax.rem(sy + dy + nsy, nsy)),
            device_id_type=MESH,
        )

    def inside(dx, dy):
        ok = None
        for step, at, size in ((dx, sx, nsx), (dy, sy, nsy)):
            if step:
                this = at > 0 if step < 0 else at < size - 1
                ok = this if ok is None else jnp.logical_and(ok, this)
        return ok

    def start_halo(field):
        for index, (dx, dy) in enumerate(DIRS):

            @pl.when(inside(dx, dy))
            def _():
                halo_copy(field, index).start()

    def wait_halo(field):
        for index, (dx, dy) in enumerate(DIRS):

            @pl.when(inside(-dx, -dy))
            def _():
                halo_copy(field, index).wait_recv()

    def wait_halo_sent(field):
        for index, (dx, dy) in enumerate(DIRS):

            @pl.when(inside(dx, dy))
            def _():
                halo_copy(field, index).wait_send()

    cut_dec = [(0, 96, 128 * j, 128) for j in range(8)]
    cut_mid = [(0, 64, 128 * j, 128) for j in range(8)]
    cut_enc = [(48 * (j % 2), 48, 128 * (j // 2), 128) for j in range(6)] + [None] * 2
    sums = {
        DEC: (total_dec, part_dec, rs_dec, ar_dec, ag_dec, cut_dec),
        MIDW: (total_mid, part_mid, rs_mid, ar_mid, ag_mid, cut_mid),
        ENC: (total_enc, part_enc, rs_enc, ar_enc, ag_enc, cut_enc),
    }

    def rs_copy(g, k):
        _, part, landing, _, _, _ = sums[g]
        return pltpu.make_async_remote_copy(
            src_ref=part.at[sx_peer(k)],
            dst_ref=landing.at[sx],
            send_sem=rs_send.at[g, k - 1],
            recv_sem=rs_recv.at[g, k - 1],
            device_id=(bt, sx_peer(k), sy),
            device_id_type=MESH,
        )

    def rs_arrival(g, k):
        _, part, landing, _, _, _ = sums[g]
        origin = sx_peer(nsx - k)
        return pltpu.make_async_remote_copy(
            src_ref=part.at[origin],
            dst_ref=landing.at[origin],
            send_sem=rs_send.at[g, k - 1],
            recv_sem=rs_recv.at[g, k - 1],
            device_id=(bt, origin, sy),
            device_id_type=MESH,
        )

    def ar_copy(g, k):
        landing = sums[g][3]
        return pltpu.make_async_remote_copy(
            src_ref=landing.at[here],
            dst_ref=landing.at[here],
            send_sem=ar_send.at[g, k - 1],
            recv_sem=ar_recv.at[g, k - 1],
            device_id=group_id(group_peer(k)),
            device_id_type=MESH,
        )

    def ar_arrival(g, k):
        landing = sums[g][3]
        origin = group_peer(group - k)
        return pltpu.make_async_remote_copy(
            src_ref=landing.at[origin],
            dst_ref=landing.at[origin],
            send_sem=ar_send.at[g, k - 1],
            recv_sem=ar_recv.at[g, k - 1],
            device_id=group_id(origin),
            device_id_type=MESH,
        )

    def ag_copy(g, k):
        landing = sums[g][4]
        return pltpu.make_async_remote_copy(
            src_ref=landing.at[sx],
            dst_ref=landing.at[sx],
            send_sem=ag_send.at[g, k - 1],
            recv_sem=ag_recv.at[g, k - 1],
            device_id=(bt, sx_peer(k), sy),
            device_id_type=MESH,
        )

    def ag_arrival(g, k):
        landing = sums[g][4]
        origin = sx_peer(nsx - k)
        return pltpu.make_async_remote_copy(
            src_ref=landing.at[origin],
            dst_ref=landing.at[origin],
            send_sem=ag_send.at[g, k - 1],
            recv_sem=ag_recv.at[g, k - 1],
            device_id=(bt, origin, sy),
            device_id_type=MESH,
        )

    def start_scatter(g):
        total, part, _, _, _, cut = sums[g]
        for j in range(nsx):
            if cut[j] is None:
                part[j] = jnp.zeros(part.shape[1:], bf16)
            else:
                row, rows, lane, lanes = cut[j]
                part[j] = total[row : row + rows, lane : lane + lanes].astype(bf16)
        for k in range(1, nsx):
            rs_copy(g, k).start()

    def start_exchange(g):
        _, part, landing, mine, _, _ = sums[g]
        for k in range(1, nsx):
            rs_arrival(g, k).wait_recv()
        acc = part[sx].astype(f32)
        for k in range(1, nsx):
            acc = acc + landing[sx_peer(k)].astype(f32)
        mine[here] = acc.astype(bf16)
        for k in range(1, group):
            ar_copy(g, k).start()

    def start_gather(g):
        _, _, _, landing, result, _ = sums[g]
        for k in range(1, group):
            ar_arrival(g, k).wait_recv()
        acc = landing[0].astype(f32)
        for q in range(1, group):
            acc = acc + landing[q].astype(f32)
        result[sx] = acc.astype(bf16)
        for k in range(1, nsx):
            ag_copy(g, k).start()

    def wait_gather(g):
        for k in range(1, nsx):
            ag_arrival(g, k).wait_recv()

    def finish_dec():
        wait_gather(DEC)
        whole = jnp.concatenate([ag_dec[j].astype(f32) for j in range(8)], axis=1) * scale
        for t in range(27):
            window, c = divmod(t, 3)
            grad_dec[t] = whole[c * 32 : (c + 1) * 32, window * 96 : (window + 1) * 96]
        grad_out[...] = whole[0:4, 864:896]

    def finish_mid():
        wait_gather(MIDW)
        for t in range(27):
            j, at = divmod(t, 4)
            grad_mid[t] = ag_mid[j, :, at * 32 : (at + 1) * 32].astype(f32) * (0.5 * scale)

    def finish_enc():
        wait_gather(ENC)
        for window in range(9):
            j, at = divmod(window, 4)
            both = jnp.concatenate([ag_enc[2 * j], ag_enc[2 * j + 1]], axis=0)
            part = both[:, at * 32 : (at + 1) * 32].astype(f32) * scale
            for c in range(3):
                grad_enc[window * 3 + c] = part[c * 32 : (c + 1) * 32]

    def wait_sum_sent(g):
        for k in range(1, nsx):
            rs_copy(g, k).wait_send()
        for k in range(1, group):
            ar_copy(g, k).wait_send()
        for k in range(1, nsx):
            ag_copy(g, k).wait_send()

    start_halo(FEAT)
    forward_weights(w_enc_f, w_enc)
    forward_weights(w_mid_f, w_mid)
    window_weights(w_dec_f, w_dec)
    backward_weights(w_enc_b, w_enc)
    backward_weights(w_mid_b, w_mid)
    backward_weights(w_dec_b, w_dec)
    out_total[...] = jnp.zeros(out_total.shape, f32)
    wait_halo(FEAT)
    finish_halo(F, nx, ny, 32, 32, 0, 1)

    def enc_block(bx, carry):
        for by in range(cy):
            block = jnp.zeros((32, LANES), f32)
            for dx in range(2):
                x = 2 * bx + dx
                pre = conv(w_enc_f, F, x, 2 * by, 2)
                s = sigmoid(pre)
                enc_slope[x, :, lane_tile(2 * by, 2)] = s * (1.0 + pre * (1.0 - s))
                act = (pre * s).astype(bf16).astype(f32)
                for dy in range(2):
                    tile = act[:, dy * LANES : (dy + 1) * LANES]
                    put_stack(J, x + 1, 2 * by + dy + 1, tile, 96, 64, 1)
                    block = block + tile
            pooled = (pair_sum(block) * 0.125).astype(bf16).astype(f32)
            PP[bx + 1, :, lane_tile(by + 1)] = packed(pooled)
            put_stack(PO, bx + 1, by + 1, pooled, 32, 0, 2)
        return carry

    lax.fori_loop(0, cx, enc_block, 0)
    start_halo(POOL)
    wait_halo(POOL)
    start_halo(SKIP)
    unpack_halo(PO, PP, cx, cy, 32)

    def mid_block(bx, carry):
        for by in range(0, cy, 2):
            pre = conv(w_mid_f, PO, bx, by, 2)
            s = sigmoid(pre)
            mid_slope[bx, :, lane_tile(by, 2)] = s * (1.0 + pre * (1.0 - s))
            act = (pre * s).astype(bf16)
            for dy in range(2):
                tile = act[:, dy * LANES : (dy + 1) * LANES]
                UP[bx + 1, :, lane_tile(by + dy + 1)] = packed(tile.astype(f32))
                J[2 * bx + 1, 96:160, lane_tile(2 * (by + dy) + 1)] = tile
        return carry

    lax.fori_loop(0, cx, mid_block, 0)
    start_halo(MID)

    def spread(bx, by, tile):
        before, after = shifted(tile, 1)
        tile = tile.astype(bf16)
        for x in (2 * bx - 1, 2 * bx):
            for y in (2 * by - 1, 2 * by):
                if 0 <= x <= nx + 1 and 0 <= y <= ny + 1:
                    lanes = lane_tile(y)
                    J[x, 0:64, lanes] = before
                    J[x, 96:160, lanes] = tile
                    J[x, 192:256, lanes] = after

    for bx in range(1, cx + 1):
        for by in range(1, cy + 1):
            spread(bx, by, J[2 * bx - 1, 96:160, lane_tile(2 * by - 1)].astype(f32))
    wait_halo(SKIP)
    finish_halo(J, nx, ny, 32, 96, 64, 1)
    wait_halo(MID)
    for bx in range(cx + 2):
        for by in range(cy + 2):
            if bx in (0, cx + 1) or by in (0, cy + 1):
                spread(bx, by, unpacked(UP[bx, :, lane_tile(by)]))

    def dec_row(x, carry):
        for y in range(0, ny + 2, 2):
            lanes = lane_tile(y, 2)
            window = jnp.concatenate([J[x + a, :, lanes] for a in range(3)], axis=0)
            window_sums[:, lanes] = jnp.dot(w_dec_f[...], window, preferred_element_type=f32)
        pre = (
            window_sums[0:32, lane_tile(0, ny)]
            + window_sums[32:64, lane_tile(1, ny)]
            + window_sums[64:96, lane_tile(2, ny)]
        )
        s = sigmoid(pre)
        slope = s * (1.0 + pre * (1.0 - s))
        act = (pre * s).astype(bf16)
        logits = jnp.dot(w_out[...], act, preferred_element_type=f32)
        expo = jnp.exp(logits)
        prob = expo / jnp.sum(expo, axis=0, keepdims=True)
        ids = lax.broadcasted_iota(jnp.int32, prob.shape, 0)
        these = jnp.concatenate([labels[x, y : y + 1, :] for y in range(ny)], axis=1)
        onehot = (these == ids).astype(f32)
        logit_grad = (loss_scale * (prob - onehot)).astype(bf16)
        out_total[...] += lax.dot_general(
            logit_grad, act, (((1,), (1,)), ((), ())), preferred_element_type=f32
        )
        act_grad = lax.dot_general(
            w_out[...], logit_grad, (((0,), (0,)), ((), ())), preferred_element_type=f32
        )
        grads = (act_grad * slope).astype(bf16).astype(f32)
        for y in range(ny):
            put_stack(
                D, x + 1, y + 1, grads[:, y * LANES : (y + 1) * LANES], 32, 0, 1, back=True
            )
        return carry

    lax.fori_loop(0, nx, dec_row, 0)
    start_halo(DECG)

    weight_grad(total_dec, lambda x: D[x + 1, :, lane_tile(1, ny)], J, nx, ny, (96, 192))
    total_dec[0:4, 864:896] = out_total[...]
    start_scatter(DEC)

    wait_halo(DECG)
    finish_halo(D, nx, ny, 32, 32, 0, 1, back=True)

    def dec_back(bx, carry):
        for by in range(cy):
            block = jnp.zeros((64, LANES), f32)
            for dx in range(2):
                x = 2 * bx + dx
                joined = conv(w_dec_b, D, x, 2 * by, 2, back=True)
                skip[x, :, lane_tile(2 * by, 2)] = joined[64:96]
                block = block + joined[0:64, 0:LANES] + joined[0:64, LANES : 2 * LANES]
            grads = pair_sum(block) * mid_slope[bx, :, lane_tile(by)]
            grads = grads.astype(bf16).astype(f32)
            MGP[bx + 1, :, lane_tile(by + 1)] = packed(grads)
            put_stack(MG, bx + 1, by + 1, grads, 64, 0, 2, back=True)
        return carry

    lax.fori_loop(0, cx, dec_back, 0)
    start_halo(MIDG)

    weight_grad(total_mid, lambda x: MG[x + 1, 64:128, lane_tile(1, cy)], PO, cx, cy, (0, 96))
    start_scatter(MIDW)
    start_exchange(DEC)

    wait_halo(MIDG)
    unpack_halo(MG, MGP, cx, cy, 64, back=True)

    def mid_back(bx, carry):
        for by in range(0, cy, 2):
            pooled = conv(w_mid_b, MG, bx, by, 2, back=True) * 0.125
            for dx in range(2):
                x = 2 * bx + dx
                for dy in range(4):
                    y = 2 * by + dy
                    up = pooled[:, (dy // 2) * LANES : (dy // 2 + 1) * LANES]
                    tile = (skip[x, :, lane_tile(y)] + up) * enc_slope[x, :, lane_tile(y)]
                    put_stack(EG, x + 1, y + 1, tile, 32, 0, 1, back=True)
        return carry

    lax.fori_loop(0, cx, mid_back, 0)
    start_halo(ENCG)

    weight_grad(total_enc, lambda x: EG[x + 1, :, lane_tile(1, ny)], F, nx, ny, (32, 64))
    start_scatter(ENC)
    start_exchange(MIDW)
    start_gather(DEC)

    wait_halo(ENCG)
    finish_halo(EG, nx, ny, 32, 32, 0, 1, back=True)
    start_exchange(ENC)

    def enc_back(x, carry):
        for y in range(0, ny, 2):
            grads = conv(w_enc_b, EG, x, y, 2, back=True)
            for dy in range(2):
                tile = grads[:, dy * LANES : (dy + 1) * LANES]
                rows32[x, pl.ds(y + dy, 32, stride=ny), :] = tile
        feature_grad[:, x] = rows32[x].reshape(32, ny, LANES).astype(bf16)
        return carry

    lax.fori_loop(0, nx, enc_back, 0)

    start_gather(MIDW)
    finish_dec()
    start_gather(ENC)
    finish_mid()
    finish_enc()

    for g in (DEC, MIDW, ENC):
        wait_sum_sent(g)
    for field in range(7):
        wait_halo_sent(field)


def shards(features, labels, w_enc, w_mid, w_dec, w_out):
    nb, nsx, nsy = lax.axis_size("batch"), lax.axis_size("sx"), lax.axis_size("sy")
    _, chans, nx, ny, nz = features.shape
    cx, cy = nx // 2, ny // 2
    scale = 1.0 / float(nb * nsx * nsy * nx * ny * nz)
    group = nb * nsy

    def fine(depth):
        return pltpu.VMEM((nx + 2, depth, (ny + 2) * LANES), bf16)

    def coarse(depth):
        return pltpu.VMEM((cx + 2, depth, (cy + 2) * LANES), bf16)

    pieces = ((96, 128), (64, 128), (48, 128))
    scratch = [
        pltpu.VMEM((32, 864), bf16),
        pltpu.VMEM((32, 864), bf16),
        pltpu.VMEM((64, 864), bf16),
        pltpu.VMEM((32, 1728), bf16),
        pltpu.VMEM((96, 864), bf16),
        pltpu.VMEM((96, 864), bf16),
        pltpu.VMEM((nx, 32 * ny, LANES), f32),
        pltpu.VMEM((96, (ny + 2) * LANES), f32),
        fine(96),
        coarse(96),
        coarse(16),
        coarse(32),
        fine(288),
        fine(96),
        coarse(192),
        coarse(32),
        fine(96),
        pltpu.VMEM((nx, 32, ny * LANES), f32),
        pltpu.VMEM((cx, 64, cy * LANES), f32),
        pltpu.VMEM((nx, 32, ny * LANES), f32),
        pltpu.VMEM((4, 32), f32),
        pltpu.VMEM((96, 1024), f32),
        pltpu.VMEM((64, 1024), f32),
        pltpu.VMEM((96, 384), f32),
    ]
    scratch += [pltpu.VMEM((nsx, rows, length), bf16) for rows, length in pieces]
    scratch += [pltpu.VMEM((nsx, rows, length), bf16) for rows, length in pieces]
    scratch += [pltpu.VMEM((group, rows, length), bf16) for rows, length in pieces]
    scratch += [pltpu.VMEM((nsx, rows, length), bf16) for rows, length in pieces]
    scratch += [pltpu.SemaphoreType.DMA((7, 8))] * 2
    scratch += [pltpu.SemaphoreType.DMA((3, nsx - 1))] * 2
    scratch += [pltpu.SemaphoreType.DMA((3, group - 1))] * 2
    scratch += [pltpu.SemaphoreType.DMA((3, nsx - 1))] * 2

    vmem = pl.BlockSpec(memory_space=pltpu.VMEM)
    feature_grad, grad_enc, grad_mid, grad_dec, grad_out = pl.pallas_call(
        functools.partial(kernel, (nb, nsx, nsy, nx, ny, scale)),
        out_shape=(
            jax.ShapeDtypeStruct((chans, nx, ny, nz), bf16),
            jax.ShapeDtypeStruct((27, 32, 32), f32),
            jax.ShapeDtypeStruct((27, 64, 32), f32),
            jax.ShapeDtypeStruct((27, 32, 96), f32),
            jax.ShapeDtypeStruct((4, 32), f32),
        ),
        in_specs=[vmem] * 6,
        out_specs=[vmem] * 5,
        scratch_shapes=scratch,
        compiler_params=pltpu.CompilerParams(
            collective_id=0, has_side_effects=True, vmem_limit_bytes=48 * 1024 * 1024
        ),
        name="unet_step",
    )(
        features[0],
        labels[0],
        w_enc.reshape(27, 32, 32),
        w_mid.reshape(27, 64, 32),
        w_dec.reshape(27, 32, 96),
        w_out,
    )
    return (
        feature_grad[None],
        grad_enc.reshape(w_enc.shape),
        grad_mid.reshape(w_mid.shape),
        grad_dec.reshape(w_dec.shape),
        grad_out,
    )


def solution(mesh):
    placed = (P("batch", None, "sx", "sy", None), P("batch", "sx", "sy", None), P(), P(), P(), P())
    return jax.shard_map(
        shards,
        mesh=mesh,
        in_specs=placed,
        out_specs=(P("batch", None, "sx", "sy", None), P(), P(), P(), P()),
        check_vma=False,
    )
```

```python
import functools

import jax
import jax.numpy as jnp
from jax import lax
from jax.experimental import pallas as pl
from jax.experimental.pallas import tpu as pltpu
from jax.sharding import PartitionSpec as P

loss_scale = 32.0
LANES = 128
MESH = pl.DeviceIdType.MESH
f32 = jnp.float32
bf16 = jnp.bfloat16

DIRS = [(dx, dy) for dx in (-1, 0, 1) for dy in (-1, 0, 1) if (dx, dy) != (0, 0)]
FEAT, POOL, SKIP, MID, DECG, MIDG, ENCG = range(7)
DEC, MIDW, ENC = range(3)


def lane_tile(y, count=1):
    if isinstance(y, int):
        return pl.ds(y * LANES, count * LANES)
    return pl.ds(pl.multiple_of(y * LANES, LANES), count * LANES)


def sigmoid(u):
    return 1.0 / (1.0 + jnp.exp(-u))


def shifted(tile, shift):
    lane = lax.broadcasted_iota(jnp.int32, tile.shape, 1)
    before = jnp.where(lane >= shift, pltpu.roll(tile, shift, axis=1), 0.0)
    after = jnp.where(lane < LANES - shift, pltpu.roll(tile, LANES - shift, axis=1), 0.0)
    return before.astype(bf16), after.astype(bf16)


def pair_sum(tile):
    lane = lax.broadcasted_iota(jnp.int32, tile.shape, 1)
    other = jnp.where(
        lane % 2 == 0, pltpu.roll(tile, LANES - 1, axis=1), pltpu.roll(tile, 1, axis=1)
    )
    return tile + other


def packed(tile):
    half = tile.shape[0] // 2
    lane = lax.broadcasted_iota(jnp.int32, (half, LANES), 1)
    return jnp.where(lane % 2 == 0, tile[:half], tile[half:]).astype(bf16)


def unpacked(tile):
    tile = tile.astype(f32)
    lane = lax.broadcasted_iota(jnp.int32, tile.shape, 1)
    first = jnp.where(lane % 2 == 0, tile, pltpu.roll(tile, 1, axis=1))
    second = jnp.where(lane % 2 == 1, tile, pltpu.roll(tile, LANES - 1, axis=1))
    return jnp.concatenate([first, second], axis=0)


def put_sides(buf, x, y, tile, period, offset, shift, back):
    chans = tile.shape[0]
    before, after = shifted(tile, shift)
    lanes = lane_tile(y)
    buf[x, offset : offset + chans, lanes] = after if back else before
    buf[x, 2 * period + offset : 2 * period + offset + chans, lanes] = before if back else after


def put_stack(buf, x, y, tile, period, offset, shift, back=False):
    chans = tile.shape[0]
    buf[x, period + offset : period + offset + chans, lane_tile(y)] = tile.astype(bf16)
    put_sides(buf, x, y, tile, period, offset, shift, back)


def over_halo(nx, ny, step):
    def step_y(y, carry):
        step(0, y)
        step(nx + 1, y)
        return carry

    lax.fori_loop(0, ny + 2, step_y, 0)

    def step_x(x, carry):
        step(x, 0)
        step(x, ny + 1)
        return carry

    lax.fori_loop(1, nx + 1, step_x, 0)


def finish_halo(buf, nx, ny, chans, period, offset, shift, back=False):
    def step(x, y):
        tile = buf[x, period + offset : period + offset + chans, lane_tile(y)].astype(f32)
        put_sides(buf, x, y, tile, period, offset, shift, back)

    over_halo(nx, ny, step)


def unpack_halo(buf, landed, nx, ny, chans, back=False):
    def step(x, y):
        put_stack(buf, x, y, unpacked(landed[x, :, lane_tile(y)]), chans, 0, 2, back)

    over_halo(nx, ny, step)


def clear_halo(buf, nx, ny, low, high):
    width = (ny + 2) * LANES
    buf[0, low:high, :] = jnp.zeros((high - low, width), bf16)
    buf[nx + 1, low:high, :] = jnp.zeros((high - low, width), bf16)
    for x in range(1, nx + 1):
        buf[x, low:high, lane_tile(0)] = jnp.zeros((high - low, LANES), bf16)
        buf[x, low:high, lane_tile(ny + 1)] = jnp.zeros((high - low, LANES), bf16)


def taps(fields, x, y, count, low, high, back=False):
    depth = sum(rows for _, _, rows in fields)
    parts = []
    for window in range(9):
        a, b = divmod(8 - window if back else window, 3)
        start = window * depth
        for buf, base, rows in fields:
            first, last = max(low, start), min(high, start + rows)
            if first < last:
                where = slice(base + first - start, base + last - start)
                parts.append(buf[x + a, where, lane_tile(y + b, count)])
            start += rows
    return parts[0] if len(parts) == 1 else jnp.concatenate(parts, axis=0)


def conv(weight, buf, x, tiles, back=False):
    depth = buf.shape[1]
    fields = [(buf, 0, depth)]
    y, other = tiles
    if other == y + 1:
        window = taps(fields, x, y, 2, 0, 9 * depth, back)
    else:
        window = jnp.concatenate(
            [taps(fields, x, at, 1, 0, 9 * depth, back) for at in tiles], axis=1
        )
    return jnp.dot(weight[...], window, preferred_element_type=f32)


def inner_pairs(ny):
    return [(y, y + 1) for y in range(1, ny - 1, 2)]


def all_pairs(ny):
    return [(y, y + 1) for y in range(0, ny, 2)]


def ranges_of(nx):
    return [(1, 3) if x == 0 else (0, 2) if x == nx - 1 else (0, 3) for x in range(nx)]


def local_part(sums, weights, buf, nx, ny, first):
    for x, (low, high) in enumerate(ranges_of(nx)):
        for y in range(1, ny + 1, 2):
            lanes = lane_tile(y, 2)
            window = jnp.concatenate([buf[x + a, :, lanes] for a in range(low, high)], axis=0)
            term = jnp.dot(weights[low, high][...], window, preferred_element_type=f32)
            if first:
                sums[x, :, lanes] = term
            else:
                sums[x, :, lanes] += term


def border_part(sums, weights, buf, nx, ny, first):
    sides = (lane_tile(0), lane_tile(ny + 1))
    for x in range(nx):
        window = jnp.concatenate(
            [jnp.concatenate([buf[x + a, :, s] for s in sides], axis=1) for a in range(3)], axis=0
        )
        term = jnp.dot(weights[0, 3][...], window, preferred_element_type=f32)
        for at, lanes in enumerate(sides):
            part = term[:, at * LANES : (at + 1) * LANES]
            if first:
                sums[x, :, lanes] = part
            else:
                sums[x, :, lanes] += part
    for x, a in ((0, 0), (nx - 1, 2)):
        for y in range(1, ny + 1, 2):
            lanes = lane_tile(y, 2)
            sums[x, :, lanes] += jnp.dot(
                weights[a, a + 1][...], buf[x + a, :, lanes], preferred_element_type=f32
            )


def weight_grad(total, grads, fields, size_x, count):
    width = 9 * sum(rows for _, _, rows in fields)
    for low in range(0, width, 256):
        high = min(low + 256, width)
        acc = None
        for x in range(size_x):
            term = lax.dot_general(
                grads(x),
                taps(fields, x, 0, count, low, high),
                (((1,), (1,)), ((), ())),
                preferred_element_type=f32,
            )
            acc = term if acc is None else acc + term
        total[:, low:high] = acc
    rest = total.shape[1] - width
    total[:, width:] = jnp.zeros((total.shape[0], rest), f32)


def laid_lanes(w, order):
    return jnp.concatenate([w[t] for t in order], axis=1)


def forward_weights(dest, w):
    for low in range(0, 27, 4):
        high = min(low + 4, 27)
        dest[:, low * 32 : high * 32] = laid_lanes(w, range(low, high))


def window_weights(dests, w, first, last):
    for (low, high), dest in dests.items():
        for b in range(3):
            parts = [
                w[(a * 3 + b) * 3 + c, :, first:last] for a in range(low, high) for c in range(3)
            ]
            dest[b * 32 : (b + 1) * 32, :] = jnp.concatenate(parts, axis=1)


def turned_weights(dest, w):
    count, outs, ins = w.shape
    flat = w[...].astype(f32).reshape(count * outs, ins)
    dest[...] = flat.T.astype(bf16)


def kernel(
    sizes,
    feat,
    labels,
    w_enc,
    w_mid,
    w_dec,
    w_out,
    feature_grad,
    sum_dec,
    sum_mid,
    sum_enc,
    w_enc_f,
    w_enc_b,
    w_mid_f,
    w_mid_b,
    w_skip_03,
    w_skip_13,
    w_skip_02,
    w_skip_01,
    w_skip_23,
    w_up_03,
    w_up_13,
    w_up_02,
    w_up_01,
    w_up_23,
    w_dec_b,
    rows32,
    window_sums,
    F,
    PO,
    PP,
    UP,
    JU,
    JE,
    D,
    MG,
    MGP,
    EG,
    enc_slope,
    mid_slope,
    joined_grad,
    out_total,
    total_dec,
    total_mid,
    total_enc,
    part_dec,
    part_mid,
    part_enc,
    rs_dec,
    rs_mid,
    rs_enc,
    ar_dec,
    ar_mid,
    ar_enc,
    ag_dec,
    ag_mid,
    ag_enc,
    halo_send,
    halo_recv,
    rs_send,
    rs_recv,
    ar_send,
    ar_recv,
    ag_send,
    ag_recv,
):
    nb, nsx, nsy, nx, ny = sizes
    cx, cy = nx // 2, ny // 2
    half = nsy // 2
    near, far = nb * half, nsx * 2
    bt, sx, sy = lax.axis_index("batch"), lax.axis_index("sx"), lax.axis_index("sy")
    here, there = bt * half + lax.rem(sy, half), sx * 2 + sy // half
    skip_weights = {
        (0, 3): w_skip_03,
        (1, 3): w_skip_13,
        (0, 2): w_skip_02,
        (0, 1): w_skip_01,
        (2, 3): w_skip_23,
    }
    up_weights = {
        (0, 3): w_up_03,
        (1, 3): w_up_13,
        (0, 2): w_up_02,
        (0, 1): w_up_01,
        (2, 3): w_up_23,
    }

    clear_halo(F, nx, ny, 32, 64)
    clear_halo(PP, cx, cy, 0, 16)
    clear_halo(JE, nx, ny, 32, 64)
    clear_halo(UP, cx, cy, 0, 32)
    clear_halo(D, nx, ny, 32, 64)
    clear_halo(MGP, cx, cy, 0, 32)
    clear_halo(EG, nx, ny, 32, 64)

    def near_peer(k):
        return lax.rem(here + k, near)

    def near_id(p):
        return (p // half, sx, (sy // half) * half + lax.rem(p, half))

    def far_peer(k):
        return lax.rem(there + k, far)

    def far_id(q):
        return (bt, q // 2, lax.rem(q, 2) * half + lax.rem(sy, half))

    barrier = pltpu.get_barrier_semaphore()
    for k in range(1, near):
        pl.semaphore_signal(barrier, inc=1, device_id=near_id(near_peer(k)), device_id_type=MESH)
    for k in range(1, far):
        pl.semaphore_signal(barrier, inc=1, device_id=far_id(far_peer(k)), device_id_type=MESH)
    for dx, dy in DIRS:
        pl.semaphore_signal(
            barrier,
            inc=1,
            device_id=(bt, lax.rem(sx + dx + nsx, nsx), lax.rem(sy + dy + nsy, nsy)),
            device_id_type=MESH,
        )

    def load_features(x, carry):
        rows32[x] = feat[:, x].astype(f32).reshape(32 * ny, LANES)
        for y in range(ny):
            put_stack(F, x + 1, y + 1, rows32[x, pl.ds(y, 32, stride=ny), :], 32, 0, 1)
        return carry

    lax.fori_loop(0, nx, load_features, 0)

    pl.semaphore_wait(barrier, near - 1 + far - 1 + 8)

    fields = {
        FEAT: (F, nx, ny, 32, 64),
        POOL: (PP, cx, cy, 0, 16),
        SKIP: (JE, nx, ny, 32, 64),
        MID: (UP, cx, cy, 0, 32),
        DECG: (D, nx, ny, 32, 64),
        MIDG: (MGP, cx, cy, 0, 32),
        ENCG: (EG, nx, ny, 32, 64),
    }

    def halo_copy(field, index):
        buf, sizex, sizey, low, high = fields[field]
        dx, dy = DIRS[index]

        def source(step, size):
            return {-1: (1, 1), 0: (1, size), 1: (size, 1)}[step]

        def target(step, size):
            return {-1: (size + 1, 1), 0: (1, size), 1: (0, 1)}[step]

        (x0, xn), (y0, yn) = source(dx, sizex), source(dy, sizey)
        (tx0, _), (ty0, _) = target(dx, sizex), target(dy, sizey)
        return pltpu.make_async_remote_copy(
            src_ref=buf.at[pl.ds(x0, xn), low:high, lane_tile(y0, yn)],
            dst_ref=buf.at[pl.ds(tx0, xn), low:high, lane_tile(ty0, yn)],
            send_sem=halo_send.at[field, index],
            recv_sem=halo_recv.at[field, index],
            device_id=(bt, lax.rem(sx + dx + nsx, nsx), lax.rem(sy + dy + nsy, nsy)),
            device_id_type=MESH,
        )

    def inside(dx, dy):
        ok = None
        for step, at, size in ((dx, sx, nsx), (dy, sy, nsy)):
            if step:
                this = at > 0 if step < 0 else at < size - 1
                ok = this if ok is None else jnp.logical_and(ok, this)
        return ok

    def start_halo(field):
        for index, (dx, dy) in enumerate(DIRS):

            @pl.when(inside(dx, dy))
            def _():
                halo_copy(field, index).start()

    def wait_halo(field):
        for index, (dx, dy) in enumerate(DIRS):

            @pl.when(inside(-dx, -dy))
            def _():
                halo_copy(field, index).wait_recv()

    def wait_halo_sent(field):
        for index, (dx, dy) in enumerate(DIRS):

            @pl.when(inside(dx, dy))
            def _():
                halo_copy(field, index).wait_send()

    cut_dec = [(0, 96, 128 * j, 128) for j in range(8)]
    cut_mid = [(0, 64, 128 * j, 128) for j in range(8)]
    cut_enc = [(48 * (j % 2), 48, 128 * (j // 2), 128) for j in range(6)] + [None] * 2
    sums = {
        DEC: (total_dec, part_dec, rs_dec, ar_dec, ag_dec, cut_dec),
        MIDW: (total_mid, part_mid, rs_mid, ar_mid, ag_mid, cut_mid),
        ENC: (total_enc, part_enc, rs_enc, ar_enc, ag_enc, cut_enc),
    }

    def rs_copy(g, k):
        _, part, landing, _, _, _ = sums[g]
        return pltpu.make_async_remote_copy(
            src_ref=part.at[near_peer(k)],
            dst_ref=landing.at[here],
            send_sem=rs_send.at[g, k - 1],
            recv_sem=rs_recv.at[g, k - 1],
            device_id=near_id(near_peer(k)),
            device_id_type=MESH,
        )

    def rs_arrival(g, k):
        _, part, landing, _, _, _ = sums[g]
        origin = near_peer(near - k)
        return pltpu.make_async_remote_copy(
            src_ref=part.at[origin],
            dst_ref=landing.at[origin],
            send_sem=rs_send.at[g, k - 1],
            recv_sem=rs_recv.at[g, k - 1],
            device_id=near_id(origin),
            device_id_type=MESH,
        )

    def ar_copy(g, k):
        landing = sums[g][3]
        return pltpu.make_async_remote_copy(
            src_ref=landing.at[there],
            dst_ref=landing.at[there],
            send_sem=ar_send.at[g, k - 1],
            recv_sem=ar_recv.at[g, k - 1],
            device_id=far_id(far_peer(k)),
            device_id_type=MESH,
        )

    def ar_arrival(g, k):
        landing = sums[g][3]
        origin = far_peer(far - k)
        return pltpu.make_async_remote_copy(
            src_ref=landing.at[origin],
            dst_ref=landing.at[origin],
            send_sem=ar_send.at[g, k - 1],
            recv_sem=ar_recv.at[g, k - 1],
            device_id=far_id(origin),
            device_id_type=MESH,
        )

    def ag_copy(g, k):
        landing = sums[g][4]
        return pltpu.make_async_remote_copy(
            src_ref=landing.at[here],
            dst_ref=landing.at[here],
            send_sem=ag_send.at[g, k - 1],
            recv_sem=ag_recv.at[g, k - 1],
            device_id=near_id(near_peer(k)),
            device_id_type=MESH,
        )

    def ag_arrival(g, k):
        landing = sums[g][4]
        origin = near_peer(near - k)
        return pltpu.make_async_remote_copy(
            src_ref=landing.at[origin],
            dst_ref=landing.at[origin],
            send_sem=ag_send.at[g, k - 1],
            recv_sem=ag_recv.at[g, k - 1],
            device_id=near_id(origin),
            device_id_type=MESH,
        )

    def start_scatter(g):
        total, part, _, _, _, cut = sums[g]
        for j in range(near):
            if cut[j] is None:
                part[j] = jnp.zeros(part.shape[1:], bf16)
            else:
                row, rows, lane, lanes = cut[j]
                part[j] = total[row : row + rows, lane : lane + lanes].astype(bf16)
        for k in range(1, near):
            rs_copy(g, k).start()

    def start_exchange(g):
        _, part, landing, mine, _, _ = sums[g]
        for k in range(1, near):
            rs_arrival(g, k).wait_recv()
        acc = part[here].astype(f32)
        for k in range(1, near):
            acc = acc + landing[near_peer(k)].astype(f32)
        mine[there] = acc.astype(bf16)
        for k in range(1, far):
            ar_copy(g, k).start()

    def start_gather(g):
        _, _, _, landing, result, _ = sums[g]
        for k in range(1, far):
            ar_arrival(g, k).wait_recv()
        acc = landing[0].astype(f32)
        for q in range(1, far):
            acc = acc + landing[q].astype(f32)
        result[here] = acc.astype(bf16)
        for k in range(1, near):
            ag_copy(g, k).start()

    def wait_gather(g):
        for k in range(1, near):
            ag_arrival(g, k).wait_recv()

    def wait_sum_sent(g):
        for k in range(1, near):
            rs_copy(g, k).wait_send()
        for k in range(1, far):
            ar_copy(g, k).wait_send()
        for k in range(1, near):
            ag_copy(g, k).wait_send()

    start_halo(FEAT)
    forward_weights(w_enc_f, w_enc)

    def enc_tiles(x, tiles):
        pre = conv(w_enc_f, F, x, tiles)
        s = sigmoid(pre)
        slope = s * (1.0 + pre * (1.0 - s))
        act = (pre * s).astype(bf16).astype(f32)
        for at, y in enumerate(tiles):
            lanes = slice(at * LANES, (at + 1) * LANES)
            enc_slope[x, :, lane_tile(y)] = slope[:, lanes]
            put_stack(JE, x + 1, y + 1, act[:, lanes], 32, 0, 1)

    def enc_inner(x, carry):
        for tiles in inner_pairs(ny):
            enc_tiles(x, tiles)
        return carry

    lax.fori_loop(1, nx - 1, enc_inner, 0)
    turned_weights(w_mid_f, w_mid)
    window_weights(skip_weights, w_dec, 64, 96)
    window_weights(up_weights, w_dec, 0, 64)
    out_total[...] = jnp.zeros(out_total.shape, f32)
    wait_halo(FEAT)
    finish_halo(F, nx, ny, 32, 32, 0, 1)

    def enc_sides(x, carry):
        enc_tiles(x, (0, ny - 1))
        return carry

    lax.fori_loop(1, nx - 1, enc_sides, 0)

    def enc_ends(i, carry):
        for tiles in all_pairs(ny):
            enc_tiles(i * (nx - 1), tiles)
        return carry

    lax.fori_loop(0, 2, enc_ends, 0)

    def pool_block(bx, carry):
        for by in range(cy):
            block = jnp.zeros((32, LANES), f32)
            for dx in range(2):
                for dy in range(2):
                    block += JE[2 * bx + dx + 1, 32:64, lane_tile(2 * by + dy + 1)].astype(f32)
            pooled = (pair_sum(block) * 0.125).astype(bf16).astype(f32)
            PP[bx + 1, :, lane_tile(by + 1)] = packed(pooled)
            put_stack(PO, bx + 1, by + 1, pooled, 32, 0, 2)
        return carry

    lax.fori_loop(0, cx, pool_block, 0)
    start_halo(POOL)
    start_halo(SKIP)
    local_part(window_sums, skip_weights, JE, nx, ny, True)
    turned_weights(w_enc_b, w_enc)
    turned_weights(w_dec_b, w_dec)
    for low in range(0, 27, 2):
        high = min(low + 2, 27)
        w_mid_b[:, low * 64 : high * 64] = laid_lanes(w_mid, range(low, high))
    wait_halo(POOL)
    unpack_halo(PO, PP, cx, cy, 32)

    def mid_block(bx, carry):
        for by in range(0, cy, 2):
            pre = conv(w_mid_f, PO, bx, (by, by + 1))
            s = sigmoid(pre)
            mid_slope[bx, :, lane_tile(by, 2)] = s * (1.0 + pre * (1.0 - s))
            act = (pre * s).astype(bf16)
            for dy in range(2):
                tile = act[:, dy * LANES : (dy + 1) * LANES]
                UP[bx + 1, :, lane_tile(by + dy + 1)] = packed(tile.astype(f32))
                JU[2 * bx + 1, 64:128, lane_tile(2 * (by + dy) + 1)] = tile
        return carry

    lax.fori_loop(0, cx, mid_block, 0)
    start_halo(MID)

    def spread(bx, by, tile):
        before, after = shifted(tile, 1)
        tile = tile.astype(bf16)
        for x in (2 * bx - 1, 2 * bx):
            for y in (2 * by - 1, 2 * by):
                if 0 <= x <= nx + 1 and 0 <= y <= ny + 1:
                    lanes = lane_tile(y)
                    JU[x, 0:64, lanes] = before
                    JU[x, 64:128, lanes] = tile
                    JU[x, 128:192, lanes] = after

    for bx in range(1, cx + 1):
        for by in range(1, cy + 1):
            spread(bx, by, JU[2 * bx - 1, 64:128, lane_tile(2 * by - 1)].astype(f32))
    local_part(window_sums, up_weights, JU, nx, ny, False)
    wait_halo(SKIP)
    finish_halo(JE, nx, ny, 32, 32, 0, 1)
    border_part(window_sums, skip_weights, JE, nx, ny, True)
    wait_halo(MID)
    for bx in range(cx + 2):
        for by in range(cy + 2):
            if bx in (0, cx + 1) or by in (0, cy + 1):
                spread(bx, by, unpacked(UP[bx, :, lane_tile(by)]))

    border_part(window_sums, up_weights, JU, nx, ny, False)

    def dec_row(x, carry):
        pre = (
            window_sums[x, 0:32, lane_tile(0, ny)]
            + window_sums[x, 32:64, lane_tile(1, ny)]
            + window_sums[x, 64:96, lane_tile(2, ny)]
        )
        s = sigmoid(pre)
        slope = s * (1.0 + pre * (1.0 - s))
        act = (pre * s).astype(bf16)
        logits = jnp.dot(w_out[...], act, preferred_element_type=f32)
        expo = jnp.exp(logits)
        prob = expo / jnp.sum(expo, axis=0, keepdims=True)
        ids = lax.broadcasted_iota(jnp.int32, prob.shape, 0)
        these = jnp.concatenate([labels[x, y : y + 1, :] for y in range(ny)], axis=1)
        onehot = (these == ids).astype(f32)
        logit_grad = (loss_scale * (prob - onehot)).astype(bf16)
        out_total[...] += lax.dot_general(
            logit_grad, act, (((1,), (1,)), ((), ())), preferred_element_type=f32
        )
        act_grad = lax.dot_general(
            w_out[...], logit_grad, (((0,), (0,)), ((), ())), preferred_element_type=f32
        )
        grads = (act_grad * slope).astype(bf16).astype(f32)
        for y in range(ny):
            put_stack(
                D, x + 1, y + 1, grads[:, y * LANES : (y + 1) * LANES], 32, 0, 1, back=True
            )
        return carry

    lax.fori_loop(0, nx, dec_row, 0)
    start_halo(DECG)

    def dec_back(x, tiles):
        grads = conv(w_dec_b, D, x, tiles, back=True)
        for at, y in enumerate(tiles):
            joined_grad[x, :, lane_tile(y)] = grads[:, at * LANES : (at + 1) * LANES]

    def dec_back_inner(x, carry):
        for tiles in inner_pairs(ny):
            dec_back(x, tiles)
        return carry

    lax.fori_loop(1, nx - 1, dec_back_inner, 0)
    joined = [(JU, 64, 64), (JE, 32, 32)]
    weight_grad(total_dec, lambda x: D[x + 1, :, lane_tile(1, ny)], joined, nx, ny)
    total_dec[0:4, 864:896] = out_total[...]
    start_scatter(DEC)

    wait_halo(DECG)
    finish_halo(D, nx, ny, 32, 32, 0, 1, back=True)

    def dec_back_sides(x, carry):
        dec_back(x, (0, ny - 1))
        return carry

    lax.fori_loop(1, nx - 1, dec_back_sides, 0)

    def dec_back_ends(i, carry):
        for tiles in all_pairs(ny):
            dec_back(i * (nx - 1), tiles)
        return carry

    lax.fori_loop(0, 2, dec_back_ends, 0)

    def mid_grads(bx, carry):
        for by in range(cy):
            block = jnp.zeros((64, LANES), f32)
            for dx in range(2):
                for dy in range(2):
                    block += joined_grad[2 * bx + dx, 0:64, lane_tile(2 * by + dy)]
            grads = pair_sum(block) * mid_slope[bx, :, lane_tile(by)]
            grads = grads.astype(bf16).astype(f32)
            MGP[bx + 1, :, lane_tile(by + 1)] = packed(grads)
            put_stack(MG, bx + 1, by + 1, grads, 64, 0, 2, back=True)
        return carry

    lax.fori_loop(0, cx, mid_grads, 0)
    start_halo(MIDG)

    weight_grad(total_mid, lambda x: MG[x + 1, 64:128, lane_tile(1, cy)], [(PO, 0, 96)], cx, cy)
    start_scatter(MIDW)
    start_exchange(DEC)

    wait_halo(MIDG)
    unpack_halo(MG, MGP, cx, cy, 64, back=True)

    def mid_back(bx, carry):
        for by in range(0, cy, 2):
            pooled = conv(w_mid_b, MG, bx, (by, by + 1), back=True) * 0.125
            for dx in range(2):
                x = 2 * bx + dx
                for dy in range(4):
                    y = 2 * by + dy
                    up = pooled[:, (dy // 2) * LANES : (dy // 2 + 1) * LANES]
                    tile = (joined_grad[x, 64:96, lane_tile(y)] + up) * enc_slope[x, :, lane_tile(y)]
                    put_stack(EG, x + 1, y + 1, tile, 32, 0, 1, back=True)
        return carry

    lax.fori_loop(0, cx, mid_back, 0)
    start_halo(ENCG)

    weight_grad(total_enc, lambda x: EG[x + 1, :, lane_tile(1, ny)], [(F, 32, 32)], nx, ny)
    start_scatter(ENC)
    start_exchange(MIDW)
    start_gather(DEC)

    wait_halo(ENCG)
    finish_halo(EG, nx, ny, 32, 32, 0, 1, back=True)
    start_exchange(ENC)

    def enc_back(x, carry):
        for y in range(0, ny, 2):
            grads = conv(w_enc_b, EG, x, (y, y + 1), back=True)
            for dy in range(2):
                tile = grads[:, dy * LANES : (dy + 1) * LANES]
                rows32[x, pl.ds(y + dy, 32, stride=ny), :] = tile
        feature_grad[:, x] = rows32[x].reshape(32, ny, LANES).astype(bf16)
        return carry

    lax.fori_loop(0, nx, enc_back, 0)

    start_gather(MIDW)
    wait_gather(DEC)
    sum_dec[...] = ag_dec[...]
    start_gather(ENC)
    wait_gather(MIDW)
    sum_mid[...] = ag_mid[...]
    wait_gather(ENC)
    sum_enc[...] = ag_enc[...]

    for g in (DEC, MIDW, ENC):
        wait_sum_sent(g)
    for field in range(7):
        wait_halo_sent(field)


def outputs(
    scale, features_in, sum_dec, sum_mid, sum_enc, features_out, grad_enc, grad_mid, grad_dec, grad_out
):
    features_out[...] = features_in[...]
    whole = jnp.concatenate([sum_dec[j].astype(f32) for j in range(8)], axis=1) * scale
    for t in range(27):
        window, c = divmod(t, 3)
        grad_dec[t] = whole[c * 32 : (c + 1) * 32, window * 96 : (window + 1) * 96]
    grad_out[...] = whole[0:4, 864:896]
    for j in range(7):
        turned = (sum_mid[j].astype(f32) * (0.5 * scale)).T
        for t in range(4 * j, min(4 * j + 4, 27)):
            grad_mid[t] = turned[(t % 4) * 32 : (t % 4 + 1) * 32]
    for window in range(9):
        j, at = divmod(window, 4)
        both = jnp.concatenate([sum_enc[2 * j], sum_enc[2 * j + 1]], axis=0)
        part = both[:, at * 32 : (at + 1) * 32].astype(f32) * scale
        for c in range(3):
            grad_enc[window * 3 + c] = part[c * 32 : (c + 1) * 32]


def shards(features, labels, w_enc, w_mid, w_dec, w_out):
    nb, nsx, nsy = lax.axis_size("batch"), lax.axis_size("sx"), lax.axis_size("sy")
    _, chans, nx, ny, nz = features.shape
    cx, cy = nx // 2, ny // 2
    scale = 1.0 / float(nb * nsx * nsy * nx * ny * nz)
    near, far = nb * (nsy // 2), nsx * 2

    def fine(depth):
        return pltpu.VMEM((nx + 2, depth, (ny + 2) * LANES), bf16)

    def coarse(depth):
        return pltpu.VMEM((cx + 2, depth, (cy + 2) * LANES), bf16)

    pieces = ((96, 128), (64, 128), (48, 128))
    scratch = [
        pltpu.VMEM((32, 864), bf16),
        pltpu.VMEM((32, 864), bf16),
        pltpu.VMEM((64, 864), bf16),
        pltpu.VMEM((32, 1728), bf16),
        *[pltpu.VMEM((96, 96 * count), bf16) for count in (3, 2, 2, 1, 1)],
        *[pltpu.VMEM((96, 192 * count), bf16) for count in (3, 2, 2, 1, 1)],
        pltpu.VMEM((96, 864), bf16),
        pltpu.VMEM((nx, 32 * ny, LANES), f32),
        pltpu.VMEM((nx, 96, (ny + 2) * LANES), f32),
        fine(96),
        coarse(96),
        coarse(16),
        coarse(32),
        fine(192),
        fine(96),
        fine(96),
        coarse(192),
        coarse(32),
        fine(96),
        pltpu.VMEM((nx, 32, ny * LANES), f32),
        pltpu.VMEM((cx, 64, cy * LANES), f32),
        pltpu.VMEM((nx, 96, ny * LANES), f32),
        pltpu.VMEM((4, 32), f32),
        pltpu.VMEM((96, 1024), f32),
        pltpu.VMEM((64, 1024), f32),
        pltpu.VMEM((96, 384), f32),
    ]
    scratch += [pltpu.VMEM((near, rows, length), bf16) for rows, length in pieces]
    scratch += [pltpu.VMEM((near, rows, length), bf16) for rows, length in pieces]
    scratch += [pltpu.VMEM((far, rows, length), bf16) for rows, length in pieces]
    scratch += [pltpu.VMEM((near, rows, length), bf16) for rows, length in pieces]
    scratch += [pltpu.SemaphoreType.DMA((7, 8))] * 2
    scratch += [pltpu.SemaphoreType.DMA((3, near - 1))] * 2
    scratch += [pltpu.SemaphoreType.DMA((3, far - 1))] * 2
    scratch += [pltpu.SemaphoreType.DMA((3, near - 1))] * 2

    vmem = pl.BlockSpec(memory_space=pltpu.VMEM)
    partial_outputs = pl.pallas_call(
        functools.partial(kernel, (nb, nsx, nsy, nx, ny)),
        out_shape=(
            jax.ShapeDtypeStruct((chans, nx, ny, nz), bf16),
            *[jax.ShapeDtypeStruct((near, rows, length), bf16) for rows, length in pieces],
        ),
        in_specs=[vmem] * 6,
        out_specs=[vmem] * 4,
        scratch_shapes=scratch,
        compiler_params=pltpu.CompilerParams(
            collective_id=0, has_side_effects=True, vmem_limit_bytes=48 * 1024 * 1024
        ),
        name="unet_step",
    )(
        features[0],
        labels[0],
        w_enc.reshape(27, 32, 32),
        w_mid.swapaxes(3, 4).reshape(27, 32, 64),
        w_dec.reshape(27, 32, 96),
        w_out,
    )
    feature_grad, grad_enc, grad_mid, grad_dec, grad_out = pl.pallas_call(
        functools.partial(outputs, scale),
        out_shape=(
            jax.ShapeDtypeStruct((chans, nx, ny, nz), bf16),
            jax.ShapeDtypeStruct((27, 32, 32), f32),
            jax.ShapeDtypeStruct((27, 32, 64), f32),
            jax.ShapeDtypeStruct((27, 32, 96), f32),
            jax.ShapeDtypeStruct((4, 32), f32),
        ),
        in_specs=[vmem] * 4,
        out_specs=[vmem] * 5,
        compiler_params=pltpu.CompilerParams(vmem_limit_bytes=16 * 1024 * 1024),
        name="unet_outputs",
    )(*partial_outputs)
    return (
        feature_grad[None],
        grad_enc.reshape(w_enc.shape),
        grad_mid.reshape(3, 3, 3, 32, 64).swapaxes(3, 4),
        grad_dec.reshape(w_dec.shape),
        grad_out,
    )


def solution(mesh):
    placed = (P("batch", None, "sx", "sy", None), P("batch", "sx", "sy", None), P(), P(), P(), P())
    return jax.shard_map(
        shards,
        mesh=mesh,
        in_specs=placed,
        out_specs=(P("batch", None, "sx", "sy", None), P(), P(), P(), P()),
        check_vma=False,
    )
```

```python
import functools

import jax
import jax.numpy as jnp
from jax import lax
from jax.experimental import pallas as pl
from jax.experimental.pallas import tpu as pltpu
from jax.sharding import PartitionSpec as P

loss_scale = 32.0
LANES = 128
MESH = pl.DeviceIdType.MESH
f32 = jnp.float32
bf16 = jnp.bfloat16

DIRS = [(dx, dy) for dx in (-1, 0, 1) for dy in (-1, 0, 1) if (dx, dy) != (0, 0)]
FEAT, POOL, SKIP, MID, DECG, MIDG, ENCG = range(7)
DEC, MIDW, ENC = range(3)


def lane_tile(y, count=1):
    if isinstance(y, int):
        return pl.ds(y * LANES, count * LANES)
    return pl.ds(pl.multiple_of(y * LANES, LANES), count * LANES)


def sigmoid(u):
    return 1.0 / (1.0 + jnp.exp(-u))


def shifted(tile, shift):
    lane = lax.broadcasted_iota(jnp.int32, tile.shape, 1)
    before = jnp.where(lane >= shift, pltpu.roll(tile, shift, axis=1), 0.0)
    after = jnp.where(lane < LANES - shift, pltpu.roll(tile, LANES - shift, axis=1), 0.0)
    return before.astype(bf16), after.astype(bf16)


def pair_sum(tile):
    lane = lax.broadcasted_iota(jnp.int32, tile.shape, 1)
    other = jnp.where(
        lane % 2 == 0, pltpu.roll(tile, LANES - 1, axis=1), pltpu.roll(tile, 1, axis=1)
    )
    return tile + other


def packed(tile):
    half = tile.shape[0] // 2
    lane = lax.broadcasted_iota(jnp.int32, (half, LANES), 1)
    return jnp.where(lane % 2 == 0, tile[:half], tile[half:]).astype(bf16)


def unpacked(tile):
    tile = tile.astype(f32)
    lane = lax.broadcasted_iota(jnp.int32, tile.shape, 1)
    first = jnp.where(lane % 2 == 0, tile, pltpu.roll(tile, 1, axis=1))
    second = jnp.where(lane % 2 == 1, tile, pltpu.roll(tile, LANES - 1, axis=1))
    return jnp.concatenate([first, second], axis=0)


def put_sides(buf, x, y, tile, period, offset, shift, back):
    chans = tile.shape[0]
    before, after = shifted(tile, shift)
    lanes = lane_tile(y)
    buf[x, offset : offset + chans, lanes] = after if back else before
    buf[x, 2 * period + offset : 2 * period + offset + chans, lanes] = before if back else after


def put_stack(buf, x, y, tile, period, offset, shift, back=False):
    chans = tile.shape[0]
    buf[x, period + offset : period + offset + chans, lane_tile(y)] = tile.astype(bf16)
    put_sides(buf, x, y, tile, period, offset, shift, back)


def over_halo(nx, ny, step):
    def step_y(y, carry):
        step(0, y)
        step(nx + 1, y)
        return carry

    lax.fori_loop(0, ny + 2, step_y, 0)

    def step_x(x, carry):
        step(x, 0)
        step(x, ny + 1)
        return carry

    lax.fori_loop(1, nx + 1, step_x, 0)


def finish_halo(buf, nx, ny, chans, period, offset, shift, back=False):
    def step(x, y):
        tile = buf[x, period + offset : period + offset + chans, lane_tile(y)].astype(f32)
        put_sides(buf, x, y, tile, period, offset, shift, back)

    over_halo(nx, ny, step)


def unpack_halo(buf, landed, nx, ny, chans, back=False):
    def step(x, y):
        put_stack(buf, x, y, unpacked(landed[x, :, lane_tile(y)]), chans, 0, 2, back)

    over_halo(nx, ny, step)


def clear_halo(buf, nx, ny, low, high):
    width = (ny + 2) * LANES
    buf[0, low:high, :] = jnp.zeros((high - low, width), bf16)
    buf[nx + 1, low:high, :] = jnp.zeros((high - low, width), bf16)
    for x in range(1, nx + 1):
        buf[x, low:high, lane_tile(0)] = jnp.zeros((high - low, LANES), bf16)
        buf[x, low:high, lane_tile(ny + 1)] = jnp.zeros((high - low, LANES), bf16)


def taps(fields, x, y, count, low, high, back=False):
    depth = sum(rows for _, _, rows in fields)
    parts = []
    for window in range(9):
        a, b = divmod(8 - window if back else window, 3)
        start = window * depth
        for buf, base, rows in fields:
            first, last = max(low, start), min(high, start + rows)
            if first < last:
                where = slice(base + first - start, base + last - start)
                parts.append(buf[x + a, where, lane_tile(y + b, count)])
            start += rows
    return parts[0] if len(parts) == 1 else jnp.concatenate(parts, axis=0)


def conv(weight, buf, x, tiles, back=False):
    depth = buf.shape[1]
    fields = [(buf, 0, depth)]
    y, other = tiles
    if other == y + 1:
        window = taps(fields, x, y, 2, 0, 9 * depth, back)
    else:
        window = jnp.concatenate(
            [taps(fields, x, at, 1, 0, 9 * depth, back) for at in tiles], axis=1
        )
    return jnp.dot(weight[...], window, preferred_element_type=f32)


def inner_pairs(ny):
    return [(y, y + 1) for y in range(1, ny - 1, 2)]


def all_pairs(ny):
    return [(y, y + 1) for y in range(0, ny, 2)]


def ranges_of(nx):
    return [(1, 3) if x == 0 else (0, 2) if x == nx - 1 else (0, 3) for x in range(nx)]


def local_part(sums, weights, buf, nx, ny, first):
    for x, (low, high) in enumerate(ranges_of(nx)):
        for y in range(1, ny + 1, 2):
            lanes = lane_tile(y, 2)
            window = jnp.concatenate([buf[x + a, :, lanes] for a in range(low, high)], axis=0)
            term = jnp.dot(weights[low, high][...], window, preferred_element_type=f32)
            if first:
                sums[x, :, lanes] = term
            else:
                sums[x, :, lanes] += term


def border_part(sums, weights, buf, nx, ny, first):
    sides = (lane_tile(0), lane_tile(ny + 1))
    for x in range(nx):
        window = jnp.concatenate(
            [jnp.concatenate([buf[x + a, :, s] for s in sides], axis=1) for a in range(3)], axis=0
        )
        term = jnp.dot(weights[0, 3][...], window, preferred_element_type=f32)
        for at, lanes in enumerate(sides):
            part = term[:, at * LANES : (at + 1) * LANES]
            if first:
                sums[x, :, lanes] = part
            else:
                sums[x, :, lanes] += part
    for x, a in ((0, 0), (nx - 1, 2)):
        for y in range(1, ny + 1, 2):
            lanes = lane_tile(y, 2)
            sums[x, :, lanes] += jnp.dot(
                weights[a, a + 1][...], buf[x + a, :, lanes], preferred_element_type=f32
            )


def weight_grad(total, grads, fields, size_x, count):
    width = 9 * sum(rows for _, _, rows in fields)
    for low in range(0, width, 256):
        high = min(low + 256, width)
        acc = None
        for x in range(size_x):
            term = lax.dot_general(
                grads(x),
                taps(fields, x, 0, count, low, high),
                (((1,), (1,)), ((), ())),
                preferred_element_type=f32,
            )
            acc = term if acc is None else acc + term
        total[:, low:high] = acc
    rest = total.shape[1] - width
    total[:, width:] = jnp.zeros((total.shape[0], rest), f32)


def laid_lanes(w, order):
    return jnp.concatenate([w[t] for t in order], axis=1)


def forward_weights(dest, w):
    for low in range(0, 27, 4):
        high = min(low + 4, 27)
        dest[:, low * 32 : high * 32] = laid_lanes(w, range(low, high))


def window_weights(dests, w, first, last):
    for (low, high), dest in dests.items():
        for b in range(3):
            parts = [
                w[(a * 3 + b) * 3 + c, :, first:last] for a in range(low, high) for c in range(3)
            ]
            dest[b * 32 : (b + 1) * 32, :] = jnp.concatenate(parts, axis=1)


def turned_weights(dest, w):
    count, outs, ins = w.shape
    flat = w[...].astype(f32).reshape(count * outs, ins)
    dest[...] = flat.T.astype(bf16)


def kernel(
    sizes,
    feat_hbm,
    labels_hbm,
    w_enc_hbm,
    w_mid_hbm,
    w_dec_hbm,
    w_out_hbm,
    feature_grad,
    sum_dec,
    sum_mid,
    sum_enc,
    feat,
    labels,
    w_enc,
    w_mid,
    w_dec,
    w_out,
    load_sem,
    w_enc_f,
    w_enc_b,
    w_mid_f,
    w_mid_b,
    w_skip_03,
    w_skip_13,
    w_skip_02,
    w_skip_01,
    w_skip_23,
    w_up_03,
    w_up_13,
    w_up_02,
    w_up_01,
    w_up_23,
    w_dec_b,
    rows32,
    window_sums,
    F,
    PO,
    PP,
    UP,
    JU,
    JE,
    D,
    MG,
    MGP,
    EG,
    enc_slope,
    mid_slope,
    joined_grad,
    out_total,
    total_dec,
    total_mid,
    total_enc,
    part_dec,
    part_mid,
    part_enc,
    rs_dec,
    rs_mid,
    rs_enc,
    ar_dec,
    ar_mid,
    ar_enc,
    ag_dec,
    ag_mid,
    ag_enc,
    halo_send,
    halo_recv,
    rs_send,
    rs_recv,
    ar_send,
    ar_recv,
    ag_send,
    ag_recv,
):
    nb, nsx, nsy, nx, ny = sizes
    cx, cy = nx // 2, ny // 2
    half = nsy // 2
    near, far = nb * half, nsx * 2
    bt, sx, sy = lax.axis_index("batch"), lax.axis_index("sx"), lax.axis_index("sy")
    here, there = bt * half + lax.rem(sy, half), sx * 2 + sy // half
    skip_weights = {
        (0, 3): w_skip_03,
        (1, 3): w_skip_13,
        (0, 2): w_skip_02,
        (0, 1): w_skip_01,
        (2, 3): w_skip_23,
    }
    up_weights = {
        (0, 3): w_up_03,
        (1, 3): w_up_13,
        (0, 2): w_up_02,
        (0, 1): w_up_01,
        (2, 3): w_up_23,
    }

    loads = {
        name: pltpu.make_async_copy(source, dest, load_sem.at[at])
        for at, (name, source, dest) in enumerate(
            (
                ("feat", feat_hbm, feat),
                ("w_enc", w_enc_hbm, w_enc),
                ("w_mid", w_mid_hbm, w_mid),
                ("w_dec", w_dec_hbm, w_dec),
                ("w_out", w_out_hbm, w_out),
                ("labels", labels_hbm, labels),
            )
        )
    }
    for load in loads.values():
        load.start()

    clear_halo(F, nx, ny, 32, 64)
    clear_halo(PP, cx, cy, 0, 16)
    clear_halo(JE, nx, ny, 32, 64)
    clear_halo(UP, cx, cy, 0, 32)
    clear_halo(D, nx, ny, 32, 64)
    clear_halo(MGP, cx, cy, 0, 32)
    clear_halo(EG, nx, ny, 32, 64)

    def near_peer(k):
        return lax.rem(here + k, near)

    def near_id(p):
        return (p // half, sx, (sy // half) * half + lax.rem(p, half))

    def far_peer(k):
        return lax.rem(there + k, far)

    def far_id(q):
        return (bt, q // 2, lax.rem(q, 2) * half + lax.rem(sy, half))

    barrier = pltpu.get_barrier_semaphore()
    for k in range(1, near):
        pl.semaphore_signal(barrier, inc=1, device_id=near_id(near_peer(k)), device_id_type=MESH)
    for k in range(1, far):
        pl.semaphore_signal(barrier, inc=1, device_id=far_id(far_peer(k)), device_id_type=MESH)
    for dx, dy in DIRS:
        pl.semaphore_signal(
            barrier,
            inc=1,
            device_id=(bt, lax.rem(sx + dx + nsx, nsx), lax.rem(sy + dy + nsy, nsy)),
            device_id_type=MESH,
        )

    loads["feat"].wait()

    def load_features(x, carry):
        rows32[x] = feat[:, x].astype(f32).reshape(32 * ny, LANES)
        for y in range(ny):
            put_stack(F, x + 1, y + 1, rows32[x, pl.ds(y, 32, stride=ny), :], 32, 0, 1)
        return carry

    lax.fori_loop(0, nx, load_features, 0)

    pl.semaphore_wait(barrier, near - 1 + far - 1 + 8)

    fields = {
        FEAT: (F, nx, ny, 32, 64),
        POOL: (PP, cx, cy, 0, 16),
        SKIP: (JE, nx, ny, 32, 64),
        MID: (UP, cx, cy, 0, 32),
        DECG: (D, nx, ny, 32, 64),
        MIDG: (MGP, cx, cy, 0, 32),
        ENCG: (EG, nx, ny, 32, 64),
    }

    def halo_copy(field, index):
        buf, sizex, sizey, low, high = fields[field]
        dx, dy = DIRS[index]

        def source(step, size):
            return {-1: (1, 1), 0: (1, size), 1: (size, 1)}[step]

        def target(step, size):
            return {-1: (size + 1, 1), 0: (1, size), 1: (0, 1)}[step]

        (x0, xn), (y0, yn) = source(dx, sizex), source(dy, sizey)
        (tx0, _), (ty0, _) = target(dx, sizex), target(dy, sizey)
        return pltpu.make_async_remote_copy(
            src_ref=buf.at[pl.ds(x0, xn), low:high, lane_tile(y0, yn)],
            dst_ref=buf.at[pl.ds(tx0, xn), low:high, lane_tile(ty0, yn)],
            send_sem=halo_send.at[field, index],
            recv_sem=halo_recv.at[field, index],
            device_id=(bt, lax.rem(sx + dx + nsx, nsx), lax.rem(sy + dy + nsy, nsy)),
            device_id_type=MESH,
        )

    def inside(dx, dy):
        ok = None
        for step, at, size in ((dx, sx, nsx), (dy, sy, nsy)):
            if step:
                this = at > 0 if step < 0 else at < size - 1
                ok = this if ok is None else jnp.logical_and(ok, this)
        return ok

    def start_halo(field):
        for index, (dx, dy) in enumerate(DIRS):

            @pl.when(inside(dx, dy))
            def _():
                halo_copy(field, index).start()

    def wait_halo(field):
        for index, (dx, dy) in enumerate(DIRS):

            @pl.when(inside(-dx, -dy))
            def _():
                halo_copy(field, index).wait_recv()

    def wait_halo_sent(field):
        for index, (dx, dy) in enumerate(DIRS):

            @pl.when(inside(dx, dy))
            def _():
                halo_copy(field, index).wait_send()

    cut_dec = [(0, 96, 128 * j, 128) for j in range(8)]
    cut_mid = [(0, 64, 128 * j, 128) for j in range(8)]
    cut_enc = [(48 * (j % 2), 48, 128 * (j // 2), 128) for j in range(6)] + [None] * 2
    sums = {
        DEC: (total_dec, part_dec, rs_dec, ar_dec, ag_dec, cut_dec),
        MIDW: (total_mid, part_mid, rs_mid, ar_mid, ag_mid, cut_mid),
        ENC: (total_enc, part_enc, rs_enc, ar_enc, ag_enc, cut_enc),
    }

    def rs_copy(g, k):
        _, part, landing, _, _, _ = sums[g]
        return pltpu.make_async_remote_copy(
            src_ref=part.at[near_peer(k)],
            dst_ref=landing.at[here],
            send_sem=rs_send.at[g, k - 1],
            recv_sem=rs_recv.at[g, k - 1],
            device_id=near_id(near_peer(k)),
            device_id_type=MESH,
        )

    def rs_arrival(g, k):
        _, part, landing, _, _, _ = sums[g]
        origin = near_peer(near - k)
        return pltpu.make_async_remote_copy(
            src_ref=part.at[origin],
            dst_ref=landing.at[origin],
            send_sem=rs_send.at[g, k - 1],
            recv_sem=rs_recv.at[g, k - 1],
            device_id=near_id(origin),
            device_id_type=MESH,
        )

    def ar_copy(g, k):
        landing = sums[g][3]
        return pltpu.make_async_remote_copy(
            src_ref=landing.at[there],
            dst_ref=landing.at[there],
            send_sem=ar_send.at[g, k - 1],
            recv_sem=ar_recv.at[g, k - 1],
            device_id=far_id(far_peer(k)),
            device_id_type=MESH,
        )

    def ar_arrival(g, k):
        landing = sums[g][3]
        origin = far_peer(far - k)
        return pltpu.make_async_remote_copy(
            src_ref=landing.at[origin],
            dst_ref=landing.at[origin],
            send_sem=ar_send.at[g, k - 1],
            recv_sem=ar_recv.at[g, k - 1],
            device_id=far_id(origin),
            device_id_type=MESH,
        )

    def ag_copy(g, k):
        landing = sums[g][4]
        return pltpu.make_async_remote_copy(
            src_ref=landing.at[here],
            dst_ref=landing.at[here],
            send_sem=ag_send.at[g, k - 1],
            recv_sem=ag_recv.at[g, k - 1],
            device_id=near_id(near_peer(k)),
            device_id_type=MESH,
        )

    def ag_arrival(g, k):
        landing = sums[g][4]
        origin = near_peer(near - k)
        return pltpu.make_async_remote_copy(
            src_ref=landing.at[origin],
            dst_ref=landing.at[origin],
            send_sem=ag_send.at[g, k - 1],
            recv_sem=ag_recv.at[g, k - 1],
            device_id=near_id(origin),
            device_id_type=MESH,
        )

    def start_scatter(g):
        total, part, _, _, _, cut = sums[g]
        for j in range(near):
            if cut[j] is None:
                part[j] = jnp.zeros(part.shape[1:], bf16)
            else:
                row, rows, lane, lanes = cut[j]
                part[j] = total[row : row + rows, lane : lane + lanes].astype(bf16)
        for k in range(1, near):
            rs_copy(g, k).start()

    def start_exchange(g):
        _, part, landing, mine, _, _ = sums[g]
        for k in range(1, near):
            rs_arrival(g, k).wait_recv()
        acc = part[here].astype(f32)
        for k in range(1, near):
            acc = acc + landing[near_peer(k)].astype(f32)
        mine[there] = acc.astype(bf16)
        for k in range(1, far):
            ar_copy(g, k).start()

    def start_gather(g):
        _, _, _, landing, result, _ = sums[g]
        for k in range(1, far):
            ar_arrival(g, k).wait_recv()
        acc = landing[0].astype(f32)
        for q in range(1, far):
            acc = acc + landing[q].astype(f32)
        result[here] = acc.astype(bf16)
        for k in range(1, near):
            ag_copy(g, k).start()

    def wait_gather(g):
        for k in range(1, near):
            ag_arrival(g, k).wait_recv()

    def wait_sum_sent(g):
        for k in range(1, near):
            rs_copy(g, k).wait_send()
        for k in range(1, far):
            ar_copy(g, k).wait_send()
        for k in range(1, near):
            ag_copy(g, k).wait_send()

    start_halo(FEAT)
    for name in ("w_enc", "w_mid", "w_dec", "w_out", "labels"):
        loads[name].wait()
    forward_weights(w_enc_f, w_enc)

    def enc_tiles(x, tiles):
        pre = conv(w_enc_f, F, x, tiles)
        s = sigmoid(pre)
        slope = s * (1.0 + pre * (1.0 - s))
        act = (pre * s).astype(bf16).astype(f32)
        for at, y in enumerate(tiles):
            lanes = slice(at * LANES, (at + 1) * LANES)
            enc_slope[x, :, lane_tile(y)] = slope[:, lanes]
            put_stack(JE, x + 1, y + 1, act[:, lanes], 32, 0, 1)

    def enc_inner(x, carry):
        for tiles in inner_pairs(ny):
            enc_tiles(x, tiles)
        return carry

    lax.fori_loop(1, nx - 1, enc_inner, 0)
    turned_weights(w_mid_f, w_mid)
    window_weights(skip_weights, w_dec, 64, 96)
    window_weights(up_weights, w_dec, 0, 64)
    out_total[...] = jnp.zeros(out_total.shape, f32)
    wait_halo(FEAT)
    finish_halo(F, nx, ny, 32, 32, 0, 1)

    def enc_sides(x, carry):
        enc_tiles(x, (0, ny - 1))
        return carry

    lax.fori_loop(1, nx - 1, enc_sides, 0)

    def enc_ends(i, carry):
        for tiles in all_pairs(ny):
            enc_tiles(i * (nx - 1), tiles)
        return carry

    lax.fori_loop(0, 2, enc_ends, 0)

    def pool_block(bx, carry):
        for by in range(cy):
            block = jnp.zeros((32, LANES), f32)
            for dx in range(2):
                for dy in range(2):
                    block += JE[2 * bx + dx + 1, 32:64, lane_tile(2 * by + dy + 1)].astype(f32)
            pooled = (pair_sum(block) * 0.125).astype(bf16).astype(f32)
            PP[bx + 1, :, lane_tile(by + 1)] = packed(pooled)
            put_stack(PO, bx + 1, by + 1, pooled, 32, 0, 2)
        return carry

    lax.fori_loop(0, cx, pool_block, 0)
    start_halo(POOL)
    start_halo(SKIP)
    local_part(window_sums, skip_weights, JE, nx, ny, True)
    turned_weights(w_enc_b, w_enc)
    turned_weights(w_dec_b, w_dec)
    for low in range(0, 27, 2):
        high = min(low + 2, 27)
        w_mid_b[:, low * 64 : high * 64] = laid_lanes(w_mid, range(low, high))
    wait_halo(POOL)
    unpack_halo(PO, PP, cx, cy, 32)

    def mid_block(bx, carry):
        for by in range(0, cy, 2):
            pre = conv(w_mid_f, PO, bx, (by, by + 1))
            s = sigmoid(pre)
            mid_slope[bx, :, lane_tile(by, 2)] = s * (1.0 + pre * (1.0 - s))
            act = (pre * s).astype(bf16)
            for dy in range(2):
                tile = act[:, dy * LANES : (dy + 1) * LANES]
                UP[bx + 1, :, lane_tile(by + dy + 1)] = packed(tile.astype(f32))
                JU[2 * bx + 1, 64:128, lane_tile(2 * (by + dy) + 1)] = tile
        return carry

    lax.fori_loop(0, cx, mid_block, 0)
    start_halo(MID)

    def spread(bx, by, tile):
        before, after = shifted(tile, 1)
        tile = tile.astype(bf16)
        for x in (2 * bx - 1, 2 * bx):
            for y in (2 * by - 1, 2 * by):
                if 0 <= x <= nx + 1 and 0 <= y <= ny + 1:
                    lanes = lane_tile(y)
                    JU[x, 0:64, lanes] = before
                    JU[x, 64:128, lanes] = tile
                    JU[x, 128:192, lanes] = after

    for bx in range(1, cx + 1):
        for by in range(1, cy + 1):
            spread(bx, by, JU[2 * bx - 1, 64:128, lane_tile(2 * by - 1)].astype(f32))
    local_part(window_sums, up_weights, JU, nx, ny, False)
    wait_halo(SKIP)
    finish_halo(JE, nx, ny, 32, 32, 0, 1)
    border_part(window_sums, skip_weights, JE, nx, ny, True)
    wait_halo(MID)
    for bx in range(cx + 2):
        for by in range(cy + 2):
            if bx in (0, cx + 1) or by in (0, cy + 1):
                spread(bx, by, unpacked(UP[bx, :, lane_tile(by)]))

    border_part(window_sums, up_weights, JU, nx, ny, False)

    def dec_row(x, carry):
        pre = (
            window_sums[x, 0:32, lane_tile(0, ny)]
            + window_sums[x, 32:64, lane_tile(1, ny)]
            + window_sums[x, 64:96, lane_tile(2, ny)]
        )
        s = sigmoid(pre)
        slope = s * (1.0 + pre * (1.0 - s))
        act = (pre * s).astype(bf16)
        logits = jnp.dot(w_out[...], act, preferred_element_type=f32)
        expo = jnp.exp(logits)
        prob = expo / jnp.sum(expo, axis=0, keepdims=True)
        ids = lax.broadcasted_iota(jnp.int32, prob.shape, 0)
        these = jnp.concatenate([labels[x, y : y + 1, :] for y in range(ny)], axis=1)
        onehot = (these == ids).astype(f32)
        logit_grad = (loss_scale * (prob - onehot)).astype(bf16)
        out_total[...] += lax.dot_general(
            logit_grad, act, (((1,), (1,)), ((), ())), preferred_element_type=f32
        )
        act_grad = lax.dot_general(
            w_out[...], logit_grad, (((0,), (0,)), ((), ())), preferred_element_type=f32
        )
        grads = (act_grad * slope).astype(bf16).astype(f32)
        for y in range(ny):
            put_stack(
                D, x + 1, y + 1, grads[:, y * LANES : (y + 1) * LANES], 32, 0, 1, back=True
            )
        return carry

    lax.fori_loop(0, nx, dec_row, 0)
    start_halo(DECG)

    def dec_back(x, tiles):
        grads = conv(w_dec_b, D, x, tiles, back=True)
        for at, y in enumerate(tiles):
            joined_grad[x, :, lane_tile(y)] = grads[:, at * LANES : (at + 1) * LANES]

    def dec_back_inner(x, carry):
        for tiles in inner_pairs(ny):
            dec_back(x, tiles)
        return carry

    lax.fori_loop(1, nx - 1, dec_back_inner, 0)
    joined = [(JU, 64, 64), (JE, 32, 32)]
    weight_grad(total_dec, lambda x: D[x + 1, :, lane_tile(1, ny)], joined, nx, ny)
    total_dec[0:4, 864:896] = out_total[...]
    start_scatter(DEC)

    wait_halo(DECG)
    finish_halo(D, nx, ny, 32, 32, 0, 1, back=True)

    def dec_back_sides(x, carry):
        dec_back(x, (0, ny - 1))
        return carry

    lax.fori_loop(1, nx - 1, dec_back_sides, 0)

    def dec_back_ends(i, carry):
        for tiles in all_pairs(ny):
            dec_back(i * (nx - 1), tiles)
        return carry

    lax.fori_loop(0, 2, dec_back_ends, 0)

    def mid_grads(bx, carry):
        for by in range(cy):
            block = jnp.zeros((64, LANES), f32)
            for dx in range(2):
                for dy in range(2):
                    block += joined_grad[2 * bx + dx, 0:64, lane_tile(2 * by + dy)]
            grads = pair_sum(block) * mid_slope[bx, :, lane_tile(by)]
            grads = grads.astype(bf16).astype(f32)
            MGP[bx + 1, :, lane_tile(by + 1)] = packed(grads)
            put_stack(MG, bx + 1, by + 1, grads, 64, 0, 2, back=True)
        return carry

    lax.fori_loop(0, cx, mid_grads, 0)
    start_halo(MIDG)

    weight_grad(total_mid, lambda x: MG[x + 1, 64:128, lane_tile(1, cy)], [(PO, 0, 96)], cx, cy)
    start_scatter(MIDW)
    start_exchange(DEC)

    wait_halo(MIDG)
    unpack_halo(MG, MGP, cx, cy, 64, back=True)

    def mid_back(bx, carry):
        for by in range(0, cy, 2):
            pooled = conv(w_mid_b, MG, bx, (by, by + 1), back=True) * 0.125
            for dx in range(2):
                x = 2 * bx + dx
                for dy in range(4):
                    y = 2 * by + dy
                    up = pooled[:, (dy // 2) * LANES : (dy // 2 + 1) * LANES]
                    tile = (joined_grad[x, 64:96, lane_tile(y)] + up) * enc_slope[x, :, lane_tile(y)]
                    put_stack(EG, x + 1, y + 1, tile, 32, 0, 1, back=True)
        return carry

    lax.fori_loop(0, cx, mid_back, 0)
    start_halo(ENCG)

    weight_grad(total_enc, lambda x: EG[x + 1, :, lane_tile(1, ny)], [(F, 32, 32)], nx, ny)
    start_scatter(ENC)
    start_exchange(MIDW)

    def enc_back(x, tiles):
        grads = conv(w_enc_b, EG, x, tiles, back=True)
        for at, y in enumerate(tiles):
            rows32[x, pl.ds(y, 32, stride=ny), :] = grads[:, at * LANES : (at + 1) * LANES]

    def enc_back_inner(x, carry):
        for tiles in inner_pairs(ny):
            enc_back(x, tiles)
        return carry

    lax.fori_loop(1, nx - 1, enc_back_inner, 0)
    start_exchange(ENC)
    wait_halo(ENCG)
    finish_halo(EG, nx, ny, 32, 32, 0, 1, back=True)

    def enc_back_sides(x, carry):
        enc_back(x, (0, ny - 1))
        return carry

    lax.fori_loop(1, nx - 1, enc_back_sides, 0)

    def enc_back_ends(i, carry):
        for tiles in all_pairs(ny):
            enc_back(i * (nx - 1), tiles)
        return carry

    lax.fori_loop(0, 2, enc_back_ends, 0)

    def lay_out(x, carry):
        feature_grad[:, x] = rows32[x].reshape(32, ny, LANES).astype(bf16)
        return carry

    lax.fori_loop(0, nx, lay_out, 0)
    start_gather(DEC)
    start_gather(MIDW)
    start_gather(ENC)
    wait_gather(DEC)
    sum_dec[...] = ag_dec[...]
    wait_gather(MIDW)
    sum_mid[...] = ag_mid[...]
    wait_gather(ENC)
    sum_enc[...] = ag_enc[...]

    for g in (DEC, MIDW, ENC):
        wait_sum_sent(g)
    for field in range(7):
        wait_halo_sent(field)


def outputs(
    scale, features_in, sum_dec, sum_mid, sum_enc, features_out, grad_enc, grad_mid, grad_dec, grad_out
):
    features_out[...] = features_in[...]
    whole = jnp.concatenate([sum_dec[j].astype(f32) for j in range(8)], axis=1) * scale
    for t in range(27):
        window, c = divmod(t, 3)
        grad_dec[t] = whole[c * 32 : (c + 1) * 32, window * 96 : (window + 1) * 96]
    grad_out[...] = whole[0:4, 864:896]
    for j in range(7):
        turned = (sum_mid[j].astype(f32) * (0.5 * scale)).T
        for t in range(4 * j, min(4 * j + 4, 27)):
            grad_mid[t] = turned[(t % 4) * 32 : (t % 4 + 1) * 32]
    for window in range(9):
        j, at = divmod(window, 4)
        both = jnp.concatenate([sum_enc[2 * j], sum_enc[2 * j + 1]], axis=0)
        part = both[:, at * 32 : (at + 1) * 32].astype(f32) * scale
        for c in range(3):
            grad_enc[window * 3 + c] = part[c * 32 : (c + 1) * 32]


def shards(features, labels, w_enc, w_mid, w_dec, w_out):
    nb, nsx, nsy = lax.axis_size("batch"), lax.axis_size("sx"), lax.axis_size("sy")
    _, chans, nx, ny, nz = features.shape
    cx, cy = nx // 2, ny // 2
    scale = 1.0 / float(nb * nsx * nsy * nx * ny * nz)
    near, far = nb * (nsy // 2), nsx * 2

    def fine(depth):
        return pltpu.VMEM((nx + 2, depth, (ny + 2) * LANES), bf16)

    def coarse(depth):
        return pltpu.VMEM((cx + 2, depth, (cy + 2) * LANES), bf16)

    pieces = ((96, 128), (64, 128), (48, 128))
    scratch = [
        pltpu.VMEM((chans, nx, ny, nz), bf16),
        pltpu.VMEM((nx, ny, nz), jnp.int32),
        pltpu.VMEM((27, 32, 32), bf16),
        pltpu.VMEM((27, 32, 64), bf16),
        pltpu.VMEM((27, 32, 96), bf16),
        pltpu.VMEM((4, 32), bf16),
        pltpu.SemaphoreType.DMA((6,)),
        pltpu.VMEM((32, 864), bf16),
        pltpu.VMEM((32, 864), bf16),
        pltpu.VMEM((64, 864), bf16),
        pltpu.VMEM((32, 1728), bf16),
        *[pltpu.VMEM((96, 96 * count), bf16) for count in (3, 2, 2, 1, 1)],
        *[pltpu.VMEM((96, 192 * count), bf16) for count in (3, 2, 2, 1, 1)],
        pltpu.VMEM((96, 864), bf16),
        pltpu.VMEM((nx, 32 * ny, LANES), f32),
        pltpu.VMEM((nx, 96, (ny + 2) * LANES), f32),
        fine(96),
        coarse(96),
        coarse(16),
        coarse(32),
        fine(192),
        fine(96),
        fine(96),
        coarse(192),
        coarse(32),
        fine(96),
        pltpu.VMEM((nx, 32, ny * LANES), f32),
        pltpu.VMEM((cx, 64, cy * LANES), f32),
        pltpu.VMEM((nx, 96, ny * LANES), f32),
        pltpu.VMEM((4, 32), f32),
        pltpu.VMEM((96, 1024), f32),
        pltpu.VMEM((64, 1024), f32),
        pltpu.VMEM((96, 384), f32),
    ]
    scratch += [pltpu.VMEM((near, rows, length), bf16) for rows, length in pieces]
    scratch += [pltpu.VMEM((near, rows, length), bf16) for rows, length in pieces]
    scratch += [pltpu.VMEM((far, rows, length), bf16) for rows, length in pieces]
    scratch += [pltpu.VMEM((near, rows, length), bf16) for rows, length in pieces]
    scratch += [pltpu.SemaphoreType.DMA((7, 8))] * 2
    scratch += [pltpu.SemaphoreType.DMA((3, near - 1))] * 2
    scratch += [pltpu.SemaphoreType.DMA((3, far - 1))] * 2
    scratch += [pltpu.SemaphoreType.DMA((3, near - 1))] * 2

    vmem = pl.BlockSpec(memory_space=pltpu.VMEM)
    partial_outputs = pl.pallas_call(
        functools.partial(kernel, (nb, nsx, nsy, nx, ny)),
        out_shape=(
            jax.ShapeDtypeStruct((chans, nx, ny, nz), bf16),
            *[jax.ShapeDtypeStruct((near, rows, length), bf16) for rows, length in pieces],
        ),
        in_specs=[pl.BlockSpec(memory_space=pl.ANY)] * 6,
        out_specs=[vmem] * 4,
        scratch_shapes=scratch,
        compiler_params=pltpu.CompilerParams(
            collective_id=0, has_side_effects=True, vmem_limit_bytes=62 * 1024 * 1024
        ),
        name="unet_step",
    )(
        features[0],
        labels[0],
        w_enc.reshape(27, 32, 32),
        w_mid.swapaxes(3, 4).reshape(27, 32, 64),
        w_dec.reshape(27, 32, 96),
        w_out,
    )
    feature_grad, grad_enc, grad_mid, grad_dec, grad_out = pl.pallas_call(
        functools.partial(outputs, scale),
        out_shape=(
            jax.ShapeDtypeStruct((chans, nx, ny, nz), bf16),
            jax.ShapeDtypeStruct((27, 32, 32), f32),
            jax.ShapeDtypeStruct((27, 32, 64), f32),
            jax.ShapeDtypeStruct((27, 32, 96), f32),
            jax.ShapeDtypeStruct((4, 32), f32),
        ),
        in_specs=[vmem] * 4,
        out_specs=[vmem] * 5,
        compiler_params=pltpu.CompilerParams(vmem_limit_bytes=62 * 1024 * 1024),
        name="unet_outputs",
    )(*partial_outputs)
    return (
        feature_grad[None],
        grad_enc.reshape(w_enc.shape),
        grad_mid.reshape(3, 3, 3, 32, 64).swapaxes(3, 4),
        grad_dec.reshape(w_dec.shape),
        grad_out,
    )


def solution(mesh):
    placed = (P("batch", None, "sx", "sy", None), P("batch", "sx", "sy", None), P(), P(), P(), P())
    return jax.shard_map(
        shards,
        mesh=mesh,
        in_specs=placed,
        out_specs=(P("batch", None, "sx", "sy", None), P(), P(), P(), P()),
        check_vma=False,
    )
```

```python
import functools

import jax
import jax.numpy as jnp
from jax import lax
from jax.experimental import pallas as pl
from jax.experimental.pallas import tpu as pltpu
from jax.sharding import PartitionSpec as P

loss_scale = 32.0
LANES = 128
MESH = pl.DeviceIdType.MESH
f32 = jnp.float32
bf16 = jnp.bfloat16

DIRS = [(dx, dy) for dx in (-1, 0, 1) for dy in (-1, 0, 1) if (dx, dy) != (0, 0)]
FEAT, POOL, SKIP, MID, DECG, MIDG, ENCG = range(7)
DEC, MIDW, ENC = range(3)


def lane_tile(y, count=1):
    if isinstance(y, int):
        return pl.ds(y * LANES, count * LANES)
    return pl.ds(pl.multiple_of(y * LANES, LANES), count * LANES)


def sigmoid(u):
    return 1.0 / (1.0 + jnp.exp(-u))


def shifted(tile, shift):
    lane = lax.broadcasted_iota(jnp.int32, tile.shape, 1)
    before = jnp.where(lane >= shift, pltpu.roll(tile, shift, axis=1), 0.0)
    after = jnp.where(lane < LANES - shift, pltpu.roll(tile, LANES - shift, axis=1), 0.0)
    return before.astype(bf16), after.astype(bf16)


def pair_sum(tile):
    lane = lax.broadcasted_iota(jnp.int32, tile.shape, 1)
    other = jnp.where(
        lane % 2 == 0, pltpu.roll(tile, LANES - 1, axis=1), pltpu.roll(tile, 1, axis=1)
    )
    return tile + other


def packed(tile):
    half = tile.shape[0] // 2
    lane = lax.broadcasted_iota(jnp.int32, (half, LANES), 1)
    return jnp.where(lane % 2 == 0, tile[:half], tile[half:]).astype(bf16)


def unpacked(tile):
    tile = tile.astype(f32)
    lane = lax.broadcasted_iota(jnp.int32, tile.shape, 1)
    first = jnp.where(lane % 2 == 0, tile, pltpu.roll(tile, 1, axis=1))
    second = jnp.where(lane % 2 == 1, tile, pltpu.roll(tile, LANES - 1, axis=1))
    return jnp.concatenate([first, second], axis=0)


def put_sides(buf, x, y, tile, period, offset, shift, back):
    chans = tile.shape[0]
    before, after = shifted(tile, shift)
    lanes = lane_tile(y)
    buf[x, offset : offset + chans, lanes] = after if back else before
    buf[x, 2 * period + offset : 2 * period + offset + chans, lanes] = before if back else after


def put_stack(buf, x, y, tile, period, offset, shift, back=False):
    chans = tile.shape[0]
    buf[x, period + offset : period + offset + chans, lane_tile(y)] = tile.astype(bf16)
    put_sides(buf, x, y, tile, period, offset, shift, back)


def each(first, last, step, carry):
    for at in range(first, last):
        step(at, carry)


def over_halo(nx, ny, step):
    for x in range(nx + 2):
        for y in range(ny + 2):
            if x in (0, nx + 1) or y in (0, ny + 1):
                step(x, y)


def finish_halo(buf, nx, ny, chans, period, offset, shift, back=False):
    def step(x, y):
        tile = buf[x, period + offset : period + offset + chans, lane_tile(y)].astype(f32)
        put_sides(buf, x, y, tile, period, offset, shift, back)

    over_halo(nx, ny, step)


def unpack_halo(buf, landed, nx, ny, chans, back=False):
    def step(x, y):
        put_stack(buf, x, y, unpacked(landed[x, :, lane_tile(y)]), chans, 0, 2, back)

    over_halo(nx, ny, step)


def clear_halo(buf, nx, ny, low, high):
    width = (ny + 2) * LANES
    buf[0, low:high, :] = jnp.zeros((high - low, width), bf16)
    buf[nx + 1, low:high, :] = jnp.zeros((high - low, width), bf16)
    for x in range(1, nx + 1):
        buf[x, low:high, lane_tile(0)] = jnp.zeros((high - low, LANES), bf16)
        buf[x, low:high, lane_tile(ny + 1)] = jnp.zeros((high - low, LANES), bf16)


def taps(fields, x, y, count, low, high, back=False):
    depth = sum(rows for _, _, rows in fields)
    parts = []
    for window in range(9):
        a, b = divmod(8 - window if back else window, 3)
        start = window * depth
        for buf, base, rows in fields:
            first, last = max(low, start), min(high, start + rows)
            if first < last:
                where = slice(base + first - start, base + last - start)
                parts.append(buf[x + a, where, lane_tile(y + b, count)])
            start += rows
    return parts[0] if len(parts) == 1 else jnp.concatenate(parts, axis=0)


def conv(weight, buf, x, tiles, back=False):
    depth = buf.shape[1]
    fields = [(buf, 0, depth)]
    y, other = tiles
    if other == y + 1:
        window = taps(fields, x, y, 2, 0, 9 * depth, back)
    else:
        window = jnp.concatenate(
            [taps(fields, x, at, 1, 0, 9 * depth, back) for at in tiles], axis=1
        )
    return jnp.dot(weight[...], window, preferred_element_type=f32)


def inner_pairs(ny):
    return [(y, y + 1) for y in range(1, ny - 1, 2)]


def all_pairs(ny):
    return [(y, y + 1) for y in range(0, ny, 2)]


def ranges_of(nx):
    return [(1, 3) if x == 0 else (0, 2) if x == nx - 1 else (0, 3) for x in range(nx)]


def local_part(sums, weights, buf, nx, ny, first):
    for x, (low, high) in enumerate(ranges_of(nx)):
        for y in range(1, ny + 1, 2):
            lanes = lane_tile(y, 2)
            window = jnp.concatenate([buf[x + a, :, lanes] for a in range(low, high)], axis=0)
            term = jnp.dot(weights[low, high][...], window, preferred_element_type=f32)
            if first:
                sums[x, :, lanes] = term
            else:
                sums[x, :, lanes] += term


def border_part(sums, weights, buf, nx, ny, first):
    sides = (lane_tile(0), lane_tile(ny + 1))
    for x in range(nx):
        window = jnp.concatenate(
            [jnp.concatenate([buf[x + a, :, s] for s in sides], axis=1) for a in range(3)], axis=0
        )
        term = jnp.dot(weights[0, 3][...], window, preferred_element_type=f32)
        for at, lanes in enumerate(sides):
            part = term[:, at * LANES : (at + 1) * LANES]
            if first:
                sums[x, :, lanes] = part
            else:
                sums[x, :, lanes] += part
    for x, a in ((0, 0), (nx - 1, 2)):
        for y in range(1, ny + 1, 2):
            lanes = lane_tile(y, 2)
            sums[x, :, lanes] += jnp.dot(
                weights[a, a + 1][...], buf[x + a, :, lanes], preferred_element_type=f32
            )


def weight_grad(total, grads, fields, size_x, count):
    width = 9 * sum(rows for _, _, rows in fields)
    for low in range(0, width, 256):
        high = min(low + 256, width)
        acc = None
        for x in range(size_x):
            term = lax.dot_general(
                grads(x),
                taps(fields, x, 0, count, low, high),
                (((1,), (1,)), ((), ())),
                preferred_element_type=f32,
            )
            acc = term if acc is None else acc + term
        total[:, low:high] = acc
    rest = total.shape[1] - width
    total[:, width:] = jnp.zeros((total.shape[0], rest), f32)


def laid_lanes(w, order):
    return jnp.concatenate([w[t] for t in order], axis=1)


def forward_weights(dest, w):
    for low in range(0, 27, 4):
        high = min(low + 4, 27)
        dest[:, low * 32 : high * 32] = laid_lanes(w, range(low, high))


def window_weights(dests, w, first, last):
    for (low, high), dest in dests.items():
        for b in range(3):
            parts = [
                w[(a * 3 + b) * 3 + c, :, first:last] for a in range(low, high) for c in range(3)
            ]
            dest[b * 32 : (b + 1) * 32, :] = jnp.concatenate(parts, axis=1)


def turned_weights(dest, w):
    count, outs, ins = w.shape
    flat = w[...].astype(f32).reshape(count * outs, ins)
    dest[...] = flat.T.astype(bf16)


def kernel(
    sizes,
    feat_hbm,
    labels_hbm,
    w_enc_hbm,
    w_mid_hbm,
    w_dec_hbm,
    w_out_hbm,
    feature_grad,
    sum_dec,
    sum_mid,
    sum_enc,
    feat,
    labels,
    w_enc,
    w_mid,
    w_dec,
    w_out,
    load_sem,
    w_enc_f,
    w_enc_b,
    w_mid_f,
    w_mid_b,
    w_skip_03,
    w_skip_13,
    w_skip_02,
    w_skip_01,
    w_skip_23,
    w_up_03,
    w_up_13,
    w_up_02,
    w_up_01,
    w_up_23,
    w_dec_b,
    rows32,
    window_sums,
    F,
    PO,
    PP,
    UP,
    JU,
    JE,
    D,
    MG,
    MGP,
    EG,
    enc_slope,
    mid_slope,
    joined_grad,
    out_total,
    total_dec,
    total_mid,
    total_enc,
    part_dec,
    part_mid,
    part_enc,
    rs_dec,
    rs_mid,
    rs_enc,
    ar_dec,
    ar_mid,
    ar_enc,
    ag_dec,
    ag_mid,
    ag_enc,
    halo_send,
    halo_recv,
    rs_send,
    rs_recv,
    ar_send,
    ar_recv,
    ag_send,
    ag_recv,
):
    nb, nsx, nsy, nx, ny = sizes
    cx, cy = nx // 2, ny // 2
    half = nsy // 2
    near, far = nb * half, nsx * 2
    bt, sx, sy = lax.axis_index("batch"), lax.axis_index("sx"), lax.axis_index("sy")
    here, there = bt * half + lax.rem(sy, half), sx * 2 + sy // half
    skip_weights = {
        (0, 3): w_skip_03,
        (1, 3): w_skip_13,
        (0, 2): w_skip_02,
        (0, 1): w_skip_01,
        (2, 3): w_skip_23,
    }
    up_weights = {
        (0, 3): w_up_03,
        (1, 3): w_up_13,
        (0, 2): w_up_02,
        (0, 1): w_up_01,
        (2, 3): w_up_23,
    }

    loads = {
        name: pltpu.make_async_copy(source, dest, load_sem.at[at])
        for at, (name, source, dest) in enumerate(
            (
                ("feat", feat_hbm, feat),
                ("w_enc", w_enc_hbm, w_enc),
                ("w_mid", w_mid_hbm, w_mid),
                ("w_dec", w_dec_hbm, w_dec),
                ("w_out", w_out_hbm, w_out),
                ("labels", labels_hbm, labels),
            )
        )
    }
    for load in loads.values():
        load.start()

    clear_halo(F, nx, ny, 32, 64)
    clear_halo(PP, cx, cy, 0, 16)
    clear_halo(JE, nx, ny, 32, 64)
    clear_halo(UP, cx, cy, 0, 32)
    clear_halo(D, nx, ny, 32, 64)
    clear_halo(MGP, cx, cy, 0, 32)
    clear_halo(EG, nx, ny, 32, 64)

    def near_peer(k):
        return lax.rem(here + k, near)

    def near_id(p):
        return (p // half, sx, (sy // half) * half + lax.rem(p, half))

    def far_peer(k):
        return lax.rem(there + k, far)

    def far_id(q):
        return (bt, q // 2, lax.rem(q, 2) * half + lax.rem(sy, half))

    barrier = pltpu.get_barrier_semaphore()
    for k in range(1, near):
        pl.semaphore_signal(barrier, inc=1, device_id=near_id(near_peer(k)), device_id_type=MESH)
    for k in range(1, far):
        pl.semaphore_signal(barrier, inc=1, device_id=far_id(far_peer(k)), device_id_type=MESH)
    for dx, dy in DIRS:
        pl.semaphore_signal(
            barrier,
            inc=1,
            device_id=(bt, lax.rem(sx + dx + nsx, nsx), lax.rem(sy + dy + nsy, nsy)),
            device_id_type=MESH,
        )

    loads["feat"].wait()

    def load_features(x, carry):
        rows32[x] = feat[:, x].astype(f32).reshape(32 * ny, LANES)
        for y in range(ny):
            put_stack(F, x + 1, y + 1, rows32[x, pl.ds(y, 32, stride=ny), :], 32, 0, 1)
        return carry

    each(0, nx, load_features, 0)

    pl.semaphore_wait(barrier, near - 1 + far - 1 + 8)

    fields = {
        FEAT: (F, nx, ny, 32, 64),
        POOL: (PP, cx, cy, 0, 16),
        SKIP: (JE, nx, ny, 32, 64),
        MID: (UP, cx, cy, 0, 32),
        DECG: (D, nx, ny, 32, 64),
        MIDG: (MGP, cx, cy, 0, 32),
        ENCG: (EG, nx, ny, 32, 64),
    }

    def halo_copy(field, index):
        buf, sizex, sizey, low, high = fields[field]
        dx, dy = DIRS[index]

        def source(step, size):
            return {-1: (1, 1), 0: (1, size), 1: (size, 1)}[step]

        def target(step, size):
            return {-1: (size + 1, 1), 0: (1, size), 1: (0, 1)}[step]

        (x0, xn), (y0, yn) = source(dx, sizex), source(dy, sizey)
        (tx0, _), (ty0, _) = target(dx, sizex), target(dy, sizey)
        return pltpu.make_async_remote_copy(
            src_ref=buf.at[pl.ds(x0, xn), low:high, lane_tile(y0, yn)],
            dst_ref=buf.at[pl.ds(tx0, xn), low:high, lane_tile(ty0, yn)],
            send_sem=halo_send.at[field, index],
            recv_sem=halo_recv.at[field, index],
            device_id=(bt, lax.rem(sx + dx + nsx, nsx), lax.rem(sy + dy + nsy, nsy)),
            device_id_type=MESH,
        )

    def inside(dx, dy):
        ok = None
        for step, at, size in ((dx, sx, nsx), (dy, sy, nsy)):
            if step:
                this = at > 0 if step < 0 else at < size - 1
                ok = this if ok is None else jnp.logical_and(ok, this)
        return ok

    def start_halo(field):
        for index, (dx, dy) in enumerate(DIRS):

            @pl.when(inside(dx, dy))
            def _():
                halo_copy(field, index).start()

    def wait_halo(field):
        for index, (dx, dy) in enumerate(DIRS):

            @pl.when(inside(-dx, -dy))
            def _():
                halo_copy(field, index).wait_recv()

    def wait_halo_sent(field):
        for index, (dx, dy) in enumerate(DIRS):

            @pl.when(inside(dx, dy))
            def _():
                halo_copy(field, index).wait_send()

    cut_dec = [(0, 96, 128 * j, 128) for j in range(8)]
    cut_mid = [(0, 64, 128 * j, 128) for j in range(8)]
    cut_enc = [(48 * (j % 2), 48, 128 * (j // 2), 128) for j in range(6)] + [None] * 2
    sums = {
        DEC: (total_dec, part_dec, rs_dec, ar_dec, ag_dec, cut_dec),
        MIDW: (total_mid, part_mid, rs_mid, ar_mid, ag_mid, cut_mid),
        ENC: (total_enc, part_enc, rs_enc, ar_enc, ag_enc, cut_enc),
    }

    def rs_copy(g, k):
        _, part, landing, _, _, _ = sums[g]
        return pltpu.make_async_remote_copy(
            src_ref=part.at[near_peer(k)],
            dst_ref=landing.at[here],
            send_sem=rs_send.at[g, k - 1],
            recv_sem=rs_recv.at[g, k - 1],
            device_id=near_id(near_peer(k)),
            device_id_type=MESH,
        )

    def rs_arrival(g, k):
        _, part, landing, _, _, _ = sums[g]
        origin = near_peer(near - k)
        return pltpu.make_async_remote_copy(
            src_ref=part.at[origin],
            dst_ref=landing.at[origin],
            send_sem=rs_send.at[g, k - 1],
            recv_sem=rs_recv.at[g, k - 1],
            device_id=near_id(origin),
            device_id_type=MESH,
        )

    def ar_copy(g, k):
        landing = sums[g][3]
        return pltpu.make_async_remote_copy(
            src_ref=landing.at[there],
            dst_ref=landing.at[there],
            send_sem=ar_send.at[g, k - 1],
            recv_sem=ar_recv.at[g, k - 1],
            device_id=far_id(far_peer(k)),
            device_id_type=MESH,
        )

    def ar_arrival(g, k):
        landing = sums[g][3]
        origin = far_peer(far - k)
        return pltpu.make_async_remote_copy(
            src_ref=landing.at[origin],
            dst_ref=landing.at[origin],
            send_sem=ar_send.at[g, k - 1],
            recv_sem=ar_recv.at[g, k - 1],
            device_id=far_id(origin),
            device_id_type=MESH,
        )

    def ag_copy(g, k):
        landing = sums[g][4]
        return pltpu.make_async_remote_copy(
            src_ref=landing.at[here],
            dst_ref=landing.at[here],
            send_sem=ag_send.at[g, k - 1],
            recv_sem=ag_recv.at[g, k - 1],
            device_id=near_id(near_peer(k)),
            device_id_type=MESH,
        )

    def ag_arrival(g, k):
        landing = sums[g][4]
        origin = near_peer(near - k)
        return pltpu.make_async_remote_copy(
            src_ref=landing.at[origin],
            dst_ref=landing.at[origin],
            send_sem=ag_send.at[g, k - 1],
            recv_sem=ag_recv.at[g, k - 1],
            device_id=near_id(origin),
            device_id_type=MESH,
        )

    def start_scatter(g):
        total, part, _, _, _, cut = sums[g]
        for j in range(near):
            if cut[j] is None:
                part[j] = jnp.zeros(part.shape[1:], bf16)
            else:
                row, rows, lane, lanes = cut[j]
                part[j] = total[row : row + rows, lane : lane + lanes].astype(bf16)
        for k in range(1, near):
            rs_copy(g, k).start()

    def start_exchange(g):
        _, part, landing, mine, _, _ = sums[g]
        for k in range(1, near):
            rs_arrival(g, k).wait_recv()
        acc = part[here].astype(f32)
        for k in range(1, near):
            acc = acc + landing[near_peer(k)].astype(f32)
        mine[there] = acc.astype(bf16)
        for k in range(1, far):
            ar_copy(g, k).start()

    def start_gather(g):
        _, _, _, landing, result, _ = sums[g]
        for k in range(1, far):
            ar_arrival(g, k).wait_recv()
        acc = landing[0].astype(f32)
        for q in range(1, far):
            acc = acc + landing[q].astype(f32)
        result[here] = acc.astype(bf16)
        for k in range(1, near):
            ag_copy(g, k).start()

    def wait_gather(g):
        for k in range(1, near):
            ag_arrival(g, k).wait_recv()

    def wait_sum_sent(g):
        for k in range(1, near):
            rs_copy(g, k).wait_send()
        for k in range(1, far):
            ar_copy(g, k).wait_send()
        for k in range(1, near):
            ag_copy(g, k).wait_send()

    start_halo(FEAT)
    for name in ("w_enc", "w_mid", "w_dec", "w_out", "labels"):
        loads[name].wait()
    forward_weights(w_enc_f, w_enc)

    def enc_tiles(x, tiles):
        pre = conv(w_enc_f, F, x, tiles)
        s = sigmoid(pre)
        slope = s * (1.0 + pre * (1.0 - s))
        act = (pre * s).astype(bf16).astype(f32)
        for at, y in enumerate(tiles):
            lanes = slice(at * LANES, (at + 1) * LANES)
            enc_slope[x, :, lane_tile(y)] = slope[:, lanes]
            put_stack(JE, x + 1, y + 1, act[:, lanes], 32, 0, 1)

    def enc_inner(x, carry):
        for tiles in inner_pairs(ny):
            enc_tiles(x, tiles)
        return carry

    each(1, nx - 1, enc_inner, 0)
    turned_weights(w_mid_f, w_mid)
    window_weights(skip_weights, w_dec, 64, 96)
    window_weights(up_weights, w_dec, 0, 64)
    out_total[...] = jnp.zeros(out_total.shape, f32)
    wait_halo(FEAT)
    finish_halo(F, nx, ny, 32, 32, 0, 1)

    def enc_sides(x, carry):
        enc_tiles(x, (0, ny - 1))
        return carry

    each(1, nx - 1, enc_sides, 0)

    def enc_ends(i, carry):
        for tiles in all_pairs(ny):
            enc_tiles(i * (nx - 1), tiles)
        return carry

    each(0, 2, enc_ends, 0)

    def pool_block(bx, carry):
        for by in range(cy):
            block = jnp.zeros((32, LANES), f32)
            for dx in range(2):
                for dy in range(2):
                    block += JE[2 * bx + dx + 1, 32:64, lane_tile(2 * by + dy + 1)].astype(f32)
            pooled = (pair_sum(block) * 0.125).astype(bf16).astype(f32)
            PP[bx + 1, :, lane_tile(by + 1)] = packed(pooled)
            put_stack(PO, bx + 1, by + 1, pooled, 32, 0, 2)
        return carry

    each(0, cx, pool_block, 0)
    start_halo(POOL)
    start_halo(SKIP)
    local_part(window_sums, skip_weights, JE, nx, ny, True)
    turned_weights(w_enc_b, w_enc)
    turned_weights(w_dec_b, w_dec)
    for low in range(0, 27, 2):
        high = min(low + 2, 27)
        w_mid_b[:, low * 64 : high * 64] = laid_lanes(w_mid, range(low, high))
    wait_halo(POOL)
    unpack_halo(PO, PP, cx, cy, 32)

    def mid_block(bx, carry):
        for by in range(0, cy, 2):
            pre = conv(w_mid_f, PO, bx, (by, by + 1))
            s = sigmoid(pre)
            mid_slope[bx, :, lane_tile(by, 2)] = s * (1.0 + pre * (1.0 - s))
            act = (pre * s).astype(bf16)
            for dy in range(2):
                tile = act[:, dy * LANES : (dy + 1) * LANES]
                UP[bx + 1, :, lane_tile(by + dy + 1)] = packed(tile.astype(f32))
                JU[2 * bx + 1, 64:128, lane_tile(2 * (by + dy) + 1)] = tile
        return carry

    each(0, cx, mid_block, 0)
    start_halo(MID)

    def spread(bx, by, tile):
        before, after = shifted(tile, 1)
        tile = tile.astype(bf16)
        for x in (2 * bx - 1, 2 * bx):
            for y in (2 * by - 1, 2 * by):
                if 0 <= x <= nx + 1 and 0 <= y <= ny + 1:
                    lanes = lane_tile(y)
                    JU[x, 0:64, lanes] = before
                    JU[x, 64:128, lanes] = tile
                    JU[x, 128:192, lanes] = after

    for bx in range(1, cx + 1):
        for by in range(1, cy + 1):
            spread(bx, by, JU[2 * bx - 1, 64:128, lane_tile(2 * by - 1)].astype(f32))
    local_part(window_sums, up_weights, JU, nx, ny, False)
    wait_halo(SKIP)
    finish_halo(JE, nx, ny, 32, 32, 0, 1)
    border_part(window_sums, skip_weights, JE, nx, ny, True)
    wait_halo(MID)
    for bx in range(cx + 2):
        for by in range(cy + 2):
            if bx in (0, cx + 1) or by in (0, cy + 1):
                spread(bx, by, unpacked(UP[bx, :, lane_tile(by)]))

    border_part(window_sums, up_weights, JU, nx, ny, False)

    def dec_row(x, carry):
        pre = (
            window_sums[x, 0:32, lane_tile(0, ny)]
            + window_sums[x, 32:64, lane_tile(1, ny)]
            + window_sums[x, 64:96, lane_tile(2, ny)]
        )
        s = sigmoid(pre)
        slope = s * (1.0 + pre * (1.0 - s))
        act = (pre * s).astype(bf16)
        logits = jnp.dot(w_out[...], act, preferred_element_type=f32)
        expo = jnp.exp(logits)
        prob = expo / jnp.sum(expo, axis=0, keepdims=True)
        ids = lax.broadcasted_iota(jnp.int32, prob.shape, 0)
        these = jnp.concatenate([labels[x, y : y + 1, :] for y in range(ny)], axis=1)
        onehot = (these == ids).astype(f32)
        logit_grad = (loss_scale * (prob - onehot)).astype(bf16)
        out_total[...] += lax.dot_general(
            logit_grad, act, (((1,), (1,)), ((), ())), preferred_element_type=f32
        )
        act_grad = lax.dot_general(
            w_out[...], logit_grad, (((0,), (0,)), ((), ())), preferred_element_type=f32
        )
        grads = (act_grad * slope).astype(bf16).astype(f32)
        for y in range(ny):
            put_stack(
                D, x + 1, y + 1, grads[:, y * LANES : (y + 1) * LANES], 32, 0, 1, back=True
            )
        return carry

    each(0, nx, dec_row, 0)
    start_halo(DECG)

    def dec_back(x, tiles):
        grads = conv(w_dec_b, D, x, tiles, back=True)
        for at, y in enumerate(tiles):
            joined_grad[x, :, lane_tile(y)] = grads[:, at * LANES : (at + 1) * LANES]

    def dec_back_inner(x, carry):
        for tiles in inner_pairs(ny):
            dec_back(x, tiles)
        return carry

    each(1, nx - 1, dec_back_inner, 0)
    joined = [(JU, 64, 64), (JE, 32, 32)]
    weight_grad(total_dec, lambda x: D[x + 1, :, lane_tile(1, ny)], joined, nx, ny)
    total_dec[0:4, 864:896] = out_total[...]
    start_scatter(DEC)

    wait_halo(DECG)
    finish_halo(D, nx, ny, 32, 32, 0, 1, back=True)

    def dec_back_sides(x, carry):
        dec_back(x, (0, ny - 1))
        return carry

    each(1, nx - 1, dec_back_sides, 0)

    def dec_back_ends(i, carry):
        for tiles in all_pairs(ny):
            dec_back(i * (nx - 1), tiles)
        return carry

    each(0, 2, dec_back_ends, 0)

    def mid_grads(bx, carry):
        for by in range(cy):
            block = jnp.zeros((64, LANES), f32)
            for dx in range(2):
                for dy in range(2):
                    block += joined_grad[2 * bx + dx, 0:64, lane_tile(2 * by + dy)]
            grads = pair_sum(block) * mid_slope[bx, :, lane_tile(by)]
            grads = grads.astype(bf16).astype(f32)
            MGP[bx + 1, :, lane_tile(by + 1)] = packed(grads)
            put_stack(MG, bx + 1, by + 1, grads, 64, 0, 2, back=True)
        return carry

    each(0, cx, mid_grads, 0)
    start_halo(MIDG)

    weight_grad(total_mid, lambda x: MG[x + 1, 64:128, lane_tile(1, cy)], [(PO, 0, 96)], cx, cy)
    start_scatter(MIDW)
    start_exchange(DEC)

    wait_halo(MIDG)
    unpack_halo(MG, MGP, cx, cy, 64, back=True)

    def mid_back(bx, carry):
        for by in range(0, cy, 2):
            pooled = conv(w_mid_b, MG, bx, (by, by + 1), back=True) * 0.125
            for dx in range(2):
                x = 2 * bx + dx
                for dy in range(4):
                    y = 2 * by + dy
                    up = pooled[:, (dy // 2) * LANES : (dy // 2 + 1) * LANES]
                    tile = (joined_grad[x, 64:96, lane_tile(y)] + up) * enc_slope[x, :, lane_tile(y)]
                    put_stack(EG, x + 1, y + 1, tile, 32, 0, 1, back=True)
        return carry

    each(0, cx, mid_back, 0)
    start_halo(ENCG)

    weight_grad(total_enc, lambda x: EG[x + 1, :, lane_tile(1, ny)], [(F, 32, 32)], nx, ny)
    start_scatter(ENC)
    start_exchange(MIDW)

    def enc_back(x, tiles):
        grads = conv(w_enc_b, EG, x, tiles, back=True)
        for at, y in enumerate(tiles):
            rows32[x, pl.ds(y, 32, stride=ny), :] = grads[:, at * LANES : (at + 1) * LANES]

    def enc_back_inner(x, carry):
        for tiles in inner_pairs(ny):
            enc_back(x, tiles)
        return carry

    each(1, nx - 1, enc_back_inner, 0)
    start_exchange(ENC)
    wait_halo(ENCG)
    finish_halo(EG, nx, ny, 32, 32, 0, 1, back=True)

    def enc_back_sides(x, carry):
        enc_back(x, (0, ny - 1))
        return carry

    each(1, nx - 1, enc_back_sides, 0)

    def enc_back_ends(i, carry):
        for tiles in all_pairs(ny):
            enc_back(i * (nx - 1), tiles)
        return carry

    each(0, 2, enc_back_ends, 0)

    def lay_out(x, carry):
        feature_grad[:, x] = rows32[x].reshape(32, ny, LANES).astype(bf16)
        return carry

    each(0, nx, lay_out, 0)
    start_gather(DEC)
    start_gather(MIDW)
    start_gather(ENC)
    wait_gather(DEC)
    sum_dec[...] = ag_dec[...]
    wait_gather(MIDW)
    sum_mid[...] = ag_mid[...]
    wait_gather(ENC)
    sum_enc[...] = ag_enc[...]

    for g in (DEC, MIDW, ENC):
        wait_sum_sent(g)
    for field in range(7):
        wait_halo_sent(field)


def outputs(
    scale, features_in, sum_dec, sum_mid, sum_enc, features_out, grad_enc, grad_mid, grad_dec, grad_out
):
    features_out[...] = features_in[...]
    whole = jnp.concatenate([sum_dec[j].astype(f32) for j in range(8)], axis=1) * scale
    for t in range(27):
        window, c = divmod(t, 3)
        grad_dec[t] = whole[c * 32 : (c + 1) * 32, window * 96 : (window + 1) * 96]
    grad_out[...] = whole[0:4, 864:896]
    for j in range(7):
        turned = (sum_mid[j].astype(f32) * (0.5 * scale)).T
        for t in range(4 * j, min(4 * j + 4, 27)):
            grad_mid[t] = turned[(t % 4) * 32 : (t % 4 + 1) * 32]
    for window in range(9):
        j, at = divmod(window, 4)
        both = jnp.concatenate([sum_enc[2 * j], sum_enc[2 * j + 1]], axis=0)
        part = both[:, at * 32 : (at + 1) * 32].astype(f32) * scale
        for c in range(3):
            grad_enc[window * 3 + c] = part[c * 32 : (c + 1) * 32]


def shards(features, labels, w_enc, w_mid, w_dec, w_out):
    nb, nsx, nsy = lax.axis_size("batch"), lax.axis_size("sx"), lax.axis_size("sy")
    _, chans, nx, ny, nz = features.shape
    cx, cy = nx // 2, ny // 2
    scale = 1.0 / float(nb * nsx * nsy * nx * ny * nz)
    near, far = nb * (nsy // 2), nsx * 2

    def fine(depth):
        return pltpu.VMEM((nx + 2, depth, (ny + 2) * LANES), bf16)

    def coarse(depth):
        return pltpu.VMEM((cx + 2, depth, (cy + 2) * LANES), bf16)

    pieces = ((96, 128), (64, 128), (48, 128))
    scratch = [
        pltpu.VMEM((chans, nx, ny, nz), bf16),
        pltpu.VMEM((nx, ny, nz), jnp.int32),
        pltpu.VMEM((27, 32, 32), bf16),
        pltpu.VMEM((27, 32, 64), bf16),
        pltpu.VMEM((27, 32, 96), bf16),
        pltpu.VMEM((4, 32), bf16),
        pltpu.SemaphoreType.DMA((6,)),
        pltpu.VMEM((32, 864), bf16),
        pltpu.VMEM((32, 864), bf16),
        pltpu.VMEM((64, 864), bf16),
        pltpu.VMEM((32, 1728), bf16),
        *[pltpu.VMEM((96, 96 * count), bf16) for count in (3, 2, 2, 1, 1)],
        *[pltpu.VMEM((96, 192 * count), bf16) for count in (3, 2, 2, 1, 1)],
        pltpu.VMEM((96, 864), bf16),
        pltpu.VMEM((nx, 32 * ny, LANES), f32),
        pltpu.VMEM((nx, 96, (ny + 2) * LANES), f32),
        fine(96),
        coarse(96),
        coarse(16),
        coarse(32),
        fine(192),
        fine(96),
        fine(96),
        coarse(192),
        coarse(32),
        fine(96),
        pltpu.VMEM((nx, 32, ny * LANES), f32),
        pltpu.VMEM((cx, 64, cy * LANES), f32),
        pltpu.VMEM((nx, 96, ny * LANES), f32),
        pltpu.VMEM((4, 32), f32),
        pltpu.VMEM((96, 1024), f32),
        pltpu.VMEM((64, 1024), f32),
        pltpu.VMEM((96, 384), f32),
    ]
    scratch += [pltpu.VMEM((near, rows, length), bf16) for rows, length in pieces]
    scratch += [pltpu.VMEM((near, rows, length), bf16) for rows, length in pieces]
    scratch += [pltpu.VMEM((far, rows, length), bf16) for rows, length in pieces]
    scratch += [pltpu.VMEM((near, rows, length), bf16) for rows, length in pieces]
    scratch += [pltpu.SemaphoreType.DMA((7, 8))] * 2
    scratch += [pltpu.SemaphoreType.DMA((3, near - 1))] * 2
    scratch += [pltpu.SemaphoreType.DMA((3, far - 1))] * 2
    scratch += [pltpu.SemaphoreType.DMA((3, near - 1))] * 2

    vmem = pl.BlockSpec(memory_space=pltpu.VMEM)
    partial_outputs = pl.pallas_call(
        functools.partial(kernel, (nb, nsx, nsy, nx, ny)),
        out_shape=(
            jax.ShapeDtypeStruct((chans, nx, ny, nz), bf16),
            *[jax.ShapeDtypeStruct((near, rows, length), bf16) for rows, length in pieces],
        ),
        in_specs=[pl.BlockSpec(memory_space=pl.ANY)] * 6,
        out_specs=[vmem] * 4,
        scratch_shapes=scratch,
        compiler_params=pltpu.CompilerParams(
            collective_id=0, has_side_effects=True, vmem_limit_bytes=62 * 1024 * 1024
        ),
        name="unet_step",
    )(
        features[0],
        labels[0],
        w_enc.reshape(27, 32, 32),
        w_mid.swapaxes(3, 4).reshape(27, 32, 64),
        w_dec.reshape(27, 32, 96),
        w_out,
    )
    feature_grad, grad_enc, grad_mid, grad_dec, grad_out = pl.pallas_call(
        functools.partial(outputs, scale),
        out_shape=(
            jax.ShapeDtypeStruct((chans, nx, ny, nz), bf16),
            jax.ShapeDtypeStruct((27, 32, 32), f32),
            jax.ShapeDtypeStruct((27, 32, 64), f32),
            jax.ShapeDtypeStruct((27, 32, 96), f32),
            jax.ShapeDtypeStruct((4, 32), f32),
        ),
        in_specs=[vmem] * 4,
        out_specs=[vmem] * 5,
        compiler_params=pltpu.CompilerParams(vmem_limit_bytes=62 * 1024 * 1024),
        name="unet_outputs",
    )(*partial_outputs)
    return (
        feature_grad[None],
        grad_enc.reshape(w_enc.shape),
        grad_mid.reshape(3, 3, 3, 32, 64).swapaxes(3, 4),
        grad_dec.reshape(w_dec.shape),
        grad_out,
    )


def solution(mesh):
    placed = (P("batch", None, "sx", "sy", None), P("batch", "sx", "sy", None), P(), P(), P(), P())
    return jax.shard_map(
        shards,
        mesh=mesh,
        in_specs=placed,
        out_specs=(P("batch", None, "sx", "sy", None), P(), P(), P(), P()),
        check_vma=False,
    )
```

```python
import functools

import jax
import jax.numpy as jnp
from jax import lax
from jax.experimental import pallas as pl
from jax.experimental.pallas import tpu as pltpu
from jax.sharding import PartitionSpec as P

loss_scale = 32.0
LANES = 128
MESH = pl.DeviceIdType.MESH
f32 = jnp.float32
bf16 = jnp.bfloat16

DIRS = [(0, -1), (0, 1), (-1, -1), (-1, 1), (1, -1), (1, 1), (-1, 0), (1, 0)]
FEAT, POOL, SKIP, MID, DECG, MIDG, ENCG = range(7)
DEC, MIDW, ENC = range(3)


def lane_tile(y, count=1):
    if isinstance(y, int):
        return pl.ds(y * LANES, count * LANES)
    return pl.ds(pl.multiple_of(y * LANES, LANES), count * LANES)


def sigmoid(u):
    return 1.0 / (1.0 + jnp.exp(-u))


def shifted(tile, shift):
    lane = lax.broadcasted_iota(jnp.int32, tile.shape, 1)
    before = jnp.where(lane >= shift, pltpu.roll(tile, shift, axis=1), 0.0)
    after = jnp.where(lane < LANES - shift, pltpu.roll(tile, LANES - shift, axis=1), 0.0)
    return before.astype(bf16), after.astype(bf16)


def pair_sum(tile):
    lane = lax.broadcasted_iota(jnp.int32, tile.shape, 1)
    other = jnp.where(
        lane % 2 == 0, pltpu.roll(tile, LANES - 1, axis=1), pltpu.roll(tile, 1, axis=1)
    )
    return tile + other


def packed(tile):
    half = tile.shape[0] // 2
    lane = lax.broadcasted_iota(jnp.int32, (half, LANES), 1)
    return jnp.where(lane % 2 == 0, tile[:half], tile[half:]).astype(bf16)


def unpacked(tile):
    tile = tile.astype(f32)
    lane = lax.broadcasted_iota(jnp.int32, tile.shape, 1)
    first = jnp.where(lane % 2 == 0, tile, pltpu.roll(tile, 1, axis=1))
    second = jnp.where(lane % 2 == 1, tile, pltpu.roll(tile, LANES - 1, axis=1))
    return jnp.concatenate([first, second], axis=0)


def put_sides(buf, x, y, tile, period, offset, shift, back):
    chans = tile.shape[0]
    before, after = shifted(tile, shift)
    lanes = lane_tile(y)
    buf[x, offset : offset + chans, lanes] = after if back else before
    buf[x, 2 * period + offset : 2 * period + offset + chans, lanes] = before if back else after


def put_stack(buf, x, y, tile, period, offset, shift, back=False):
    chans = tile.shape[0]
    buf[x, period + offset : period + offset + chans, lane_tile(y)] = tile.astype(bf16)
    put_sides(buf, x, y, tile, period, offset, shift, back)


def each(first, last, step, carry):
    for at in range(first, last):
        step(at, carry)


def over_halo(nx, ny, step):
    for x in range(nx + 2):
        for y in range(ny + 2):
            if x in (0, nx + 1) or y in (0, ny + 1):
                step(x, y)


def finish_halo(buf, nx, ny, chans, period, offset, shift, back=False):
    def step(x, y):
        tile = buf[x, period + offset : period + offset + chans, lane_tile(y)].astype(f32)
        put_sides(buf, x, y, tile, period, offset, shift, back)

    over_halo(nx, ny, step)


def unpack_halo(buf, landed, nx, ny, chans, back=False):
    def step(x, y):
        put_stack(buf, x, y, unpacked(landed[x, :, lane_tile(y)]), chans, 0, 2, back)

    over_halo(nx, ny, step)


def clear_halo(buf, nx, ny, low, high):
    width = (ny + 2) * LANES
    buf[0, low:high, :] = jnp.zeros((high - low, width), bf16)
    buf[nx + 1, low:high, :] = jnp.zeros((high - low, width), bf16)
    for x in range(1, nx + 1):
        buf[x, low:high, lane_tile(0)] = jnp.zeros((high - low, LANES), bf16)
        buf[x, low:high, lane_tile(ny + 1)] = jnp.zeros((high - low, LANES), bf16)


def taps(fields, x, y, count, low, high, back=False):
    depth = sum(rows for _, _, rows in fields)
    parts = []
    for window in range(9):
        a, b = divmod(8 - window if back else window, 3)
        start = window * depth
        for buf, base, rows in fields:
            first, last = max(low, start), min(high, start + rows)
            if first < last:
                where = slice(base + first - start, base + last - start)
                parts.append(buf[x + a, where, lane_tile(y + b, count)])
            start += rows
    return parts[0] if len(parts) == 1 else jnp.concatenate(parts, axis=0)


def conv(weight, buf, x, tiles, back=False):
    depth = buf.shape[1]
    fields = [(buf, 0, depth)]
    y, other = tiles
    if other == y + 1:
        window = taps(fields, x, y, 2, 0, 9 * depth, back)
    else:
        window = jnp.concatenate(
            [taps(fields, x, at, 1, 0, 9 * depth, back) for at in tiles], axis=1
        )
    return jnp.dot(weight[...], window, preferred_element_type=f32)


def inner_pairs(ny):
    return [(y, y + 1) for y in range(1, ny - 1, 2)]


def all_pairs(ny):
    return [(y, y + 1) for y in range(0, ny, 2)]


def ranges_of(nx):
    return [(1, 3) if x == 0 else (0, 2) if x == nx - 1 else (0, 3) for x in range(nx)]


def local_part(sums, weights, buf, nx, ny, first):
    for x, (low, high) in enumerate(ranges_of(nx)):
        for y in range(1, ny + 1, 2):
            lanes = lane_tile(y, 2)
            window = jnp.concatenate([buf[x + a, :, lanes] for a in range(low, high)], axis=0)
            term = jnp.dot(weights[low, high][...], window, preferred_element_type=f32)
            if first:
                sums[x, :, lanes] = term
            else:
                sums[x, :, lanes] += term


def border_part(sums, weights, buf, nx, ny, first):
    sides = (lane_tile(0), lane_tile(ny + 1))
    for x in range(nx):
        window = jnp.concatenate(
            [jnp.concatenate([buf[x + a, :, s] for s in sides], axis=1) for a in range(3)], axis=0
        )
        term = jnp.dot(weights[0, 3][...], window, preferred_element_type=f32)
        for at, lanes in enumerate(sides):
            part = term[:, at * LANES : (at + 1) * LANES]
            if first:
                sums[x, :, lanes] = part
            else:
                sums[x, :, lanes] += part
    for x, a in ((0, 0), (nx - 1, 2)):
        for y in range(1, ny + 1, 2):
            lanes = lane_tile(y, 2)
            sums[x, :, lanes] += jnp.dot(
                weights[a, a + 1][...], buf[x + a, :, lanes], preferred_element_type=f32
            )


def weight_grad(total, grads, fields, size_x, count):
    width = 9 * sum(rows for _, _, rows in fields)
    for low in range(0, width, 256):
        high = min(low + 256, width)
        acc = None
        for x in range(size_x):
            term = lax.dot_general(
                grads(x),
                taps(fields, x, 0, count, low, high),
                (((1,), (1,)), ((), ())),
                preferred_element_type=f32,
            )
            acc = term if acc is None else acc + term
        total[:, low:high] = acc
    rest = total.shape[1] - width
    total[:, width:] = jnp.zeros((total.shape[0], rest), f32)


def laid_lanes(w, order):
    return jnp.concatenate([w[t] for t in order], axis=1)


def forward_weights(dest, w):
    for low in range(0, 27, 4):
        high = min(low + 4, 27)
        dest[:, low * 32 : high * 32] = laid_lanes(w, range(low, high))


def window_weights(dests, w, first, last):
    for (low, high), dest in dests.items():
        for b in range(3):
            parts = [
                w[(a * 3 + b) * 3 + c, :, first:last] for a in range(low, high) for c in range(3)
            ]
            dest[b * 32 : (b + 1) * 32, :] = jnp.concatenate(parts, axis=1)


def turned_weights(dest, w):
    count, outs, ins = w.shape
    flat = w[...].astype(f32).reshape(count * outs, ins)
    dest[...] = flat.T.astype(bf16)


def kernel(
    sizes,
    feat_hbm,
    labels_hbm,
    w_enc_hbm,
    w_mid_hbm,
    w_dec_hbm,
    w_out_hbm,
    feature_grad_hbm,
    sum_dec,
    sum_mid,
    sum_enc,
    feat,
    labels,
    w_enc,
    w_mid,
    w_dec,
    w_out,
    load_sem,
    feature_grad,
    store_sem,
    w_enc_f,
    w_enc_b,
    w_mid_f,
    w_mid_b,
    w_skip_03,
    w_skip_13,
    w_skip_02,
    w_skip_01,
    w_skip_23,
    w_up_03,
    w_up_13,
    w_up_02,
    w_up_01,
    w_up_23,
    w_dec_b,
    rows32,
    window_sums,
    F,
    PO,
    PP,
    UP,
    JU,
    JE,
    D,
    MG,
    MGP,
    EG,
    enc_slope,
    mid_slope,
    joined_grad,
    out_total,
    total_dec,
    total_mid,
    total_enc,
    part_dec,
    part_mid,
    part_enc,
    rs_dec,
    rs_mid,
    rs_enc,
    ar_dec,
    ar_mid,
    ar_enc,
    ag_dec,
    ag_mid,
    ag_enc,
    halo_send,
    halo_recv,
    rs_send,
    rs_recv,
    ar_send,
    ar_recv,
    ag_send,
    ag_recv,
):
    nb, nsx, nsy, nx, ny = sizes
    cx, cy = nx // 2, ny // 2
    half = nsy // 2
    near, far = nb * half, nsx * 2
    bt, sx, sy = lax.axis_index("batch"), lax.axis_index("sx"), lax.axis_index("sy")
    here, there = bt * half + lax.rem(sy, half), sx * 2 + sy // half
    skip_weights = {
        (0, 3): w_skip_03,
        (1, 3): w_skip_13,
        (0, 2): w_skip_02,
        (0, 1): w_skip_01,
        (2, 3): w_skip_23,
    }
    up_weights = {
        (0, 3): w_up_03,
        (1, 3): w_up_13,
        (0, 2): w_up_02,
        (0, 1): w_up_01,
        (2, 3): w_up_23,
    }

    loads = {
        name: pltpu.make_async_copy(source, dest, load_sem.at[at])
        for at, (name, source, dest) in enumerate(
            (
                ("feat", feat_hbm, feat),
                ("w_enc", w_enc_hbm, w_enc),
                ("w_mid", w_mid_hbm, w_mid),
                ("w_dec", w_dec_hbm, w_dec),
                ("w_out", w_out_hbm, w_out),
                ("labels", labels_hbm, labels),
            )
        )
    }
    for load in loads.values():
        load.start()

    clear_halo(F, nx, ny, 32, 64)
    clear_halo(PP, cx, cy, 0, 16)
    clear_halo(JE, nx, ny, 32, 64)
    clear_halo(UP, cx, cy, 0, 32)
    clear_halo(D, nx, ny, 32, 64)
    clear_halo(MGP, cx, cy, 0, 32)
    clear_halo(EG, nx, ny, 32, 64)

    def near_peer(k):
        return lax.rem(here + k, near)

    def near_id(p):
        return (p // half, sx, (sy // half) * half + lax.rem(p, half))

    def far_peer(k):
        return lax.rem(there + k, far)

    def far_id(q):
        return (bt, q // 2, lax.rem(q, 2) * half + lax.rem(sy, half))

    barrier = pltpu.get_barrier_semaphore()
    for k in range(1, near):
        pl.semaphore_signal(barrier, inc=1, device_id=near_id(near_peer(k)), device_id_type=MESH)
    for k in range(1, far):
        pl.semaphore_signal(barrier, inc=1, device_id=far_id(far_peer(k)), device_id_type=MESH)
    for dx, dy in DIRS:
        pl.semaphore_signal(
            barrier,
            inc=1,
            device_id=(bt, lax.rem(sx + dx + nsx, nsx), lax.rem(sy + dy + nsy, nsy)),
            device_id_type=MESH,
        )

    loads["feat"].wait()

    def load_features(x, carry):
        rows32[x] = feat[:, x].astype(f32).reshape(32 * ny, LANES)
        for y in range(ny):
            put_stack(F, x + 1, y + 1, rows32[x, pl.ds(y, 32, stride=ny), :], 32, 0, 1)
        return carry

    each(0, nx, load_features, 0)

    pl.semaphore_wait(barrier, near - 1 + far - 1 + 8)

    fields = {
        FEAT: (F, nx, ny, 32, 64),
        POOL: (PP, cx, cy, 0, 16),
        SKIP: (JE, nx, ny, 32, 64),
        MID: (UP, cx, cy, 0, 32),
        DECG: (D, nx, ny, 32, 64),
        MIDG: (MGP, cx, cy, 0, 32),
        ENCG: (EG, nx, ny, 32, 64),
    }

    def halo_copy(field, index):
        buf, sizex, sizey, low, high = fields[field]
        dx, dy = DIRS[index]

        def source(step, size):
            return {-1: (1, 1), 0: (1, size), 1: (size, 1)}[step]

        def target(step, size):
            return {-1: (size + 1, 1), 0: (1, size), 1: (0, 1)}[step]

        (x0, xn), (y0, yn) = source(dx, sizex), source(dy, sizey)
        (tx0, _), (ty0, _) = target(dx, sizex), target(dy, sizey)
        return pltpu.make_async_remote_copy(
            src_ref=buf.at[pl.ds(x0, xn), low:high, lane_tile(y0, yn)],
            dst_ref=buf.at[pl.ds(tx0, xn), low:high, lane_tile(ty0, yn)],
            send_sem=halo_send.at[field, index],
            recv_sem=halo_recv.at[field, index],
            device_id=(bt, lax.rem(sx + dx + nsx, nsx), lax.rem(sy + dy + nsy, nsy)),
            device_id_type=MESH,
        )

    def inside(dx, dy):
        ok = None
        for step, at, size in ((dx, sx, nsx), (dy, sy, nsy)):
            if step:
                this = at > 0 if step < 0 else at < size - 1
                ok = this if ok is None else jnp.logical_and(ok, this)
        return ok

    def start_halo(field):
        for index, (dx, dy) in enumerate(DIRS):

            @pl.when(inside(dx, dy))
            def _():
                halo_copy(field, index).start()

    def wait_halo(field):
        for index, (dx, dy) in enumerate(DIRS):

            @pl.when(inside(-dx, -dy))
            def _():
                halo_copy(field, index).wait_recv()

    def wait_halo_sent(field):
        for index, (dx, dy) in enumerate(DIRS):

            @pl.when(inside(dx, dy))
            def _():
                halo_copy(field, index).wait_send()

    cut_dec = [(0, 96, 128 * j, 128) for j in range(8)]
    cut_mid = [(0, 64, 128 * j, 128) for j in range(8)]
    cut_enc = [(48 * (j % 2), 48, 128 * (j // 2), 128) for j in range(6)] + [None] * 2
    sums = {
        DEC: (total_dec, part_dec, rs_dec, ar_dec, ag_dec, cut_dec),
        MIDW: (total_mid, part_mid, rs_mid, ar_mid, ag_mid, cut_mid),
        ENC: (total_enc, part_enc, rs_enc, ar_enc, ag_enc, cut_enc),
    }

    def rs_copy(g, k):
        _, part, landing, _, _, _ = sums[g]
        return pltpu.make_async_remote_copy(
            src_ref=part.at[near_peer(k)],
            dst_ref=landing.at[here],
            send_sem=rs_send.at[g],
            recv_sem=rs_recv.at[g],
            device_id=near_id(near_peer(k)),
            device_id_type=MESH,
        )

    def ar_copy(g, k):
        landing = sums[g][3]
        return pltpu.make_async_remote_copy(
            src_ref=landing.at[there],
            dst_ref=landing.at[there],
            send_sem=ar_send.at[g],
            recv_sem=ar_recv.at[g],
            device_id=far_id(far_peer(k)),
            device_id_type=MESH,
        )

    def ag_copy(g, k):
        landing = sums[g][4]
        return pltpu.make_async_remote_copy(
            src_ref=landing.at[here],
            dst_ref=landing.at[here],
            send_sem=ag_send.at[g],
            recv_sem=ag_recv.at[g],
            device_id=near_id(near_peer(k)),
            device_id_type=MESH,
        )

    def wait_bytes(sem, pieces):
        pltpu.make_async_copy(pieces, pieces, sem).wait()

    def start_scatter(g):
        total, part, _, _, _, cut = sums[g]
        for j in range(near):
            if cut[j] is None:
                part[j] = jnp.zeros(part.shape[1:], bf16)
            else:
                row, rows, lane, lanes = cut[j]
                part[j] = total[row : row + rows, lane : lane + lanes].astype(bf16)
        for k in range(1, near):
            rs_copy(g, k).start()

    def start_exchange(g):
        _, part, landing, mine, _, _ = sums[g]
        wait_bytes(rs_recv.at[g], landing.at[pl.ds(0, near - 1)])
        acc = part[here].astype(f32)
        for k in range(1, near):
            acc = acc + landing[near_peer(k)].astype(f32)
        mine[there] = acc.astype(bf16)
        for k in range(1, far):
            ar_copy(g, k).start()

    def start_gather(g):
        _, _, _, landing, result, _ = sums[g]
        wait_bytes(ar_recv.at[g], landing.at[pl.ds(0, far - 1)])
        acc = landing[0].astype(f32)
        for q in range(1, far):
            acc = acc + landing[q].astype(f32)
        result[here] = acc.astype(bf16)
        for k in range(1, near):
            ag_copy(g, k).start()

    def wait_gather(g):
        wait_bytes(ag_recv.at[g], sums[g][4].at[pl.ds(0, near - 1)])

    def wait_scatter_sent(g):
        wait_bytes(rs_send.at[g], sums[g][1].at[pl.ds(0, near - 1)])

    def wait_exchange_sent(g):
        wait_bytes(ar_send.at[g], sums[g][3].at[pl.ds(0, far - 1)])

    def wait_gather_sent(g):
        wait_bytes(ag_send.at[g], sums[g][4].at[pl.ds(0, near - 1)])

    start_halo(FEAT)
    for name in ("w_enc", "w_mid", "w_dec", "w_out", "labels"):
        loads[name].wait()
    forward_weights(w_enc_f, w_enc)

    def enc_tiles(x, tiles):
        pre = conv(w_enc_f, F, x, tiles)
        s = sigmoid(pre)
        slope = s * (1.0 + pre * (1.0 - s))
        act = (pre * s).astype(bf16).astype(f32)
        for at, y in enumerate(tiles):
            lanes = slice(at * LANES, (at + 1) * LANES)
            enc_slope[x, :, lane_tile(y)] = slope[:, lanes]
            put_stack(JE, x + 1, y + 1, act[:, lanes], 32, 0, 1)

    def enc_inner(x, carry):
        for tiles in inner_pairs(ny):
            enc_tiles(x, tiles)
        return carry

    each(1, nx - 1, enc_inner, 0)
    turned_weights(w_mid_f, w_mid)
    window_weights(skip_weights, w_dec, 64, 96)
    window_weights(up_weights, w_dec, 0, 64)
    out_total[...] = jnp.zeros(out_total.shape, f32)
    wait_halo(FEAT)
    finish_halo(F, nx, ny, 32, 32, 0, 1)

    def enc_sides(x, carry):
        enc_tiles(x, (0, ny - 1))
        return carry

    each(1, nx - 1, enc_sides, 0)

    def enc_ends(i, carry):
        for tiles in all_pairs(ny):
            enc_tiles(i * (nx - 1), tiles)
        return carry

    each(0, 2, enc_ends, 0)

    def pool_block(bx, carry):
        for by in range(cy):
            block = jnp.zeros((32, LANES), f32)
            for dx in range(2):
                for dy in range(2):
                    block += JE[2 * bx + dx + 1, 32:64, lane_tile(2 * by + dy + 1)].astype(f32)
            pooled = (pair_sum(block) * 0.125).astype(bf16).astype(f32)
            PP[bx + 1, :, lane_tile(by + 1)] = packed(pooled)
            put_stack(PO, bx + 1, by + 1, pooled, 32, 0, 2)
        return carry

    each(0, cx, pool_block, 0)
    start_halo(POOL)
    start_halo(SKIP)
    local_part(window_sums, skip_weights, JE, nx, ny, True)
    turned_weights(w_enc_b, w_enc)
    turned_weights(w_dec_b, w_dec)
    for low in range(0, 27, 2):
        high = min(low + 2, 27)
        w_mid_b[:, low * 64 : high * 64] = laid_lanes(w_mid, range(low, high))
    wait_halo(POOL)
    unpack_halo(PO, PP, cx, cy, 32)

    def mid_block(bx, carry):
        for by in range(0, cy, 2):
            pre = conv(w_mid_f, PO, bx, (by, by + 1))
            s = sigmoid(pre)
            mid_slope[bx, :, lane_tile(by, 2)] = s * (1.0 + pre * (1.0 - s))
            act = (pre * s).astype(bf16)
            for dy in range(2):
                tile = act[:, dy * LANES : (dy + 1) * LANES]
                UP[bx + 1, :, lane_tile(by + dy + 1)] = packed(tile.astype(f32))
                JU[2 * bx + 1, 64:128, lane_tile(2 * (by + dy) + 1)] = tile
        return carry

    each(0, cx, mid_block, 0)
    start_halo(MID)

    def spread(bx, by, tile):
        before, after = shifted(tile, 1)
        tile = tile.astype(bf16)
        for x in (2 * bx - 1, 2 * bx):
            for y in (2 * by - 1, 2 * by):
                if 0 <= x <= nx + 1 and 0 <= y <= ny + 1:
                    lanes = lane_tile(y)
                    JU[x, 0:64, lanes] = before
                    JU[x, 64:128, lanes] = tile
                    JU[x, 128:192, lanes] = after

    for bx in range(1, cx + 1):
        for by in range(1, cy + 1):
            spread(bx, by, JU[2 * bx - 1, 64:128, lane_tile(2 * by - 1)].astype(f32))
    local_part(window_sums, up_weights, JU, nx, ny, False)
    wait_halo(SKIP)
    finish_halo(JE, nx, ny, 32, 32, 0, 1)
    border_part(window_sums, skip_weights, JE, nx, ny, True)
    wait_halo(MID)
    for bx in range(cx + 2):
        for by in range(cy + 2):
            if bx in (0, cx + 1) or by in (0, cy + 1):
                spread(bx, by, unpacked(UP[bx, :, lane_tile(by)]))

    border_part(window_sums, up_weights, JU, nx, ny, False)

    def dec_row(x, carry):
        pre = (
            window_sums[x, 0:32, lane_tile(0, ny)]
            + window_sums[x, 32:64, lane_tile(1, ny)]
            + window_sums[x, 64:96, lane_tile(2, ny)]
        )
        s = sigmoid(pre)
        slope = s * (1.0 + pre * (1.0 - s))
        act = (pre * s).astype(bf16)
        logits = jnp.dot(w_out[...], act, preferred_element_type=f32)
        expo = jnp.exp(logits)
        prob = expo / jnp.sum(expo, axis=0, keepdims=True)
        ids = lax.broadcasted_iota(jnp.int32, prob.shape, 0)
        these = jnp.concatenate([labels[x, y : y + 1, :] for y in range(ny)], axis=1)
        onehot = (these == ids).astype(f32)
        logit_grad = (loss_scale * (prob - onehot)).astype(bf16)
        out_total[...] += lax.dot_general(
            logit_grad, act, (((1,), (1,)), ((), ())), preferred_element_type=f32
        )
        act_grad = lax.dot_general(
            w_out[...], logit_grad, (((0,), (0,)), ((), ())), preferred_element_type=f32
        )
        grads = (act_grad * slope).astype(bf16).astype(f32)
        for y in range(ny):
            put_stack(
                D, x + 1, y + 1, grads[:, y * LANES : (y + 1) * LANES], 32, 0, 1, back=True
            )
        return carry

    each(0, nx, dec_row, 0)
    start_halo(DECG)

    def dec_back(x, tiles):
        grads = conv(w_dec_b, D, x, tiles, back=True)
        for at, y in enumerate(tiles):
            joined_grad[x, :, lane_tile(y)] = grads[:, at * LANES : (at + 1) * LANES]

    def dec_back_inner(x, carry):
        for tiles in inner_pairs(ny):
            dec_back(x, tiles)
        return carry

    each(1, nx - 1, dec_back_inner, 0)
    joined = [(JU, 64, 64), (JE, 32, 32)]
    weight_grad(total_dec, lambda x: D[x + 1, :, lane_tile(1, ny)], joined, nx, ny)
    total_dec[0:4, 864:896] = out_total[...]
    start_scatter(DEC)

    wait_halo(DECG)
    finish_halo(D, nx, ny, 32, 32, 0, 1, back=True)

    def dec_back_sides(x, carry):
        dec_back(x, (0, ny - 1))
        return carry

    each(1, nx - 1, dec_back_sides, 0)

    def dec_back_ends(i, carry):
        for tiles in all_pairs(ny):
            dec_back(i * (nx - 1), tiles)
        return carry

    each(0, 2, dec_back_ends, 0)

    def mid_grads(bx, carry):
        for by in range(cy):
            block = jnp.zeros((64, LANES), f32)
            for dx in range(2):
                for dy in range(2):
                    block += joined_grad[2 * bx + dx, 0:64, lane_tile(2 * by + dy)]
            grads = pair_sum(block) * mid_slope[bx, :, lane_tile(by)]
            grads = grads.astype(bf16).astype(f32)
            MGP[bx + 1, :, lane_tile(by + 1)] = packed(grads)
            put_stack(MG, bx + 1, by + 1, grads, 64, 0, 2, back=True)
        return carry

    each(0, cx, mid_grads, 0)
    start_halo(MIDG)

    weight_grad(total_mid, lambda x: MG[x + 1, 64:128, lane_tile(1, cy)], [(PO, 0, 96)], cx, cy)
    start_scatter(MIDW)
    start_exchange(DEC)

    wait_halo(MIDG)
    unpack_halo(MG, MGP, cx, cy, 64, back=True)

    def mid_back(bx, carry):
        for by in range(0, cy, 2):
            pooled = conv(w_mid_b, MG, bx, (by, by + 1), back=True) * 0.125
            for dx in range(2):
                x = 2 * bx + dx
                for dy in range(4):
                    y = 2 * by + dy
                    up = pooled[:, (dy // 2) * LANES : (dy // 2 + 1) * LANES]
                    tile = (joined_grad[x, 64:96, lane_tile(y)] + up) * enc_slope[x, :, lane_tile(y)]
                    put_stack(EG, x + 1, y + 1, tile, 32, 0, 1, back=True)
        return carry

    each(0, cx, mid_back, 0)
    start_halo(ENCG)

    weight_grad(total_enc, lambda x: EG[x + 1, :, lane_tile(1, ny)], [(F, 32, 32)], nx, ny)
    start_scatter(ENC)
    start_exchange(MIDW)

    def enc_back(x, tiles):
        grads = conv(w_enc_b, EG, x, tiles, back=True)
        for at, y in enumerate(tiles):
            rows32[x, pl.ds(y, 32, stride=ny), :] = grads[:, at * LANES : (at + 1) * LANES]

    def enc_back_inner(x, carry):
        for tiles in inner_pairs(ny):
            enc_back(x, tiles)
        return carry

    each(1, nx - 1, enc_back_inner, 0)
    start_exchange(ENC)
    wait_halo(ENCG)
    finish_halo(EG, nx, ny, 32, 32, 0, 1, back=True)

    def enc_back_sides(x, carry):
        enc_back(x, (0, ny - 1))
        return carry

    each(1, nx - 1, enc_back_sides, 0)

    def enc_back_ends(i, carry):
        for tiles in all_pairs(ny):
            enc_back(i * (nx - 1), tiles)
        return carry

    each(0, 2, enc_back_ends, 0)

    def lay_out(x, carry):
        feature_grad[:, x] = rows32[x].reshape(32, ny, LANES).astype(bf16)
        return carry

    each(0, nx, lay_out, 0)
    stores = [
        pltpu.make_async_copy(source, dest, store_sem.at[at])
        for at, (source, dest) in enumerate(
            (
                (feature_grad, feature_grad_hbm),
                (ag_dec, sum_dec),
                (ag_mid, sum_mid),
                (ag_enc, sum_enc),
            )
        )
    ]
    stores[0].start()
    start_gather(DEC)
    start_gather(MIDW)
    for field in range(7):
        wait_halo_sent(field)
    for g in (DEC, MIDW, ENC):
        wait_scatter_sent(g)
    start_gather(ENC)
    wait_gather(DEC)
    stores[1].start()
    wait_gather(MIDW)
    stores[2].start()
    for g in (DEC, MIDW, ENC):
        wait_exchange_sent(g)
    for g in (DEC, MIDW):
        wait_gather_sent(g)
    wait_gather(ENC)
    stores[3].start()
    wait_gather_sent(ENC)
    for store in stores:
        store.wait()


def outputs(
    scale,
    features_in,
    dec_in,
    mid_in,
    enc_in,
    features_out,
    enc_out,
    mid_out,
    dec_out,
    out_out,
    features,
    sum_dec,
    sum_mid,
    sum_enc,
    grad_enc,
    grad_mid,
    grad_dec,
    grad_out,
    sems,
):
    copies = [
        pltpu.make_async_copy(source, dest, sems.at[at])
        for at, (source, dest) in enumerate(
            (
                (dec_in, sum_dec),
                (mid_in, sum_mid),
                (enc_in, sum_enc),
                (features_in, features),
                (grad_dec, dec_out),
                (grad_out, out_out),
                (grad_mid, mid_out),
                (grad_enc, enc_out),
                (features, features_out),
            )
        )
    ]
    for copy in copies[:4]:
        copy.start()
    copies[0].wait()
    whole = jnp.concatenate([sum_dec[j].astype(f32) for j in range(8)], axis=1) * scale
    for t in range(27):
        window, c = divmod(t, 3)
        grad_dec[t] = whole[c * 32 : (c + 1) * 32, window * 96 : (window + 1) * 96]
    grad_out[...] = whole[0:4, 864:896]
    copies[4].start()
    copies[5].start()
    copies[3].wait()
    copies[8].start()
    copies[1].wait()
    for j in range(7):
        turned = (sum_mid[j].astype(f32) * (0.5 * scale)).T
        for t in range(4 * j, min(4 * j + 4, 27)):
            grad_mid[t] = turned[(t % 4) * 32 : (t % 4 + 1) * 32]
    copies[6].start()
    copies[2].wait()
    for window in range(9):
        j, at = divmod(window, 4)
        both = jnp.concatenate([sum_enc[2 * j], sum_enc[2 * j + 1]], axis=0)
        part = both[:, at * 32 : (at + 1) * 32].astype(f32) * scale
        for c in range(3):
            grad_enc[window * 3 + c] = part[c * 32 : (c + 1) * 32]
    copies[7].start()
    for copy in copies[4:]:
        copy.wait()


def shards(features, labels, w_enc, w_mid, w_dec, w_out):
    nb, nsx, nsy = lax.axis_size("batch"), lax.axis_size("sx"), lax.axis_size("sy")
    _, chans, nx, ny, nz = features.shape
    cx, cy = nx // 2, ny // 2
    scale = 1.0 / float(nb * nsx * nsy * nx * ny * nz)
    near, far = nb * (nsy // 2), nsx * 2

    def fine(depth):
        return pltpu.VMEM((nx + 2, depth, (ny + 2) * LANES), bf16)

    def coarse(depth):
        return pltpu.VMEM((cx + 2, depth, (cy + 2) * LANES), bf16)

    pieces = ((96, 128), (64, 128), (48, 128))
    scratch = [
        pltpu.VMEM((chans, nx, ny, nz), bf16),
        pltpu.VMEM((nx, ny, nz), jnp.int32),
        pltpu.VMEM((27, 32, 32), bf16),
        pltpu.VMEM((27, 32, 64), bf16),
        pltpu.VMEM((27, 32, 96), bf16),
        pltpu.VMEM((4, 32), bf16),
        pltpu.SemaphoreType.DMA((6,)),
        pltpu.VMEM((chans, nx, ny, nz), bf16),
        pltpu.SemaphoreType.DMA((4,)),
        pltpu.VMEM((32, 864), bf16),
        pltpu.VMEM((32, 864), bf16),
        pltpu.VMEM((64, 864), bf16),
        pltpu.VMEM((32, 1728), bf16),
        *[pltpu.VMEM((96, 96 * count), bf16) for count in (3, 2, 2, 1, 1)],
        *[pltpu.VMEM((96, 192 * count), bf16) for count in (3, 2, 2, 1, 1)],
        pltpu.VMEM((96, 864), bf16),
        pltpu.VMEM((nx, 32 * ny, LANES), f32),
        pltpu.VMEM((nx, 96, (ny + 2) * LANES), f32),
        fine(96),
        coarse(96),
        coarse(16),
        coarse(32),
        fine(192),
        fine(96),
        fine(96),
        coarse(192),
        coarse(32),
        fine(96),
        pltpu.VMEM((nx, 32, ny * LANES), f32),
        pltpu.VMEM((cx, 64, cy * LANES), f32),
        pltpu.VMEM((nx, 96, ny * LANES), f32),
        pltpu.VMEM((4, 32), f32),
        pltpu.VMEM((96, 1024), f32),
        pltpu.VMEM((64, 1024), f32),
        pltpu.VMEM((96, 384), f32),
    ]
    scratch += [pltpu.VMEM((near, rows, length), bf16) for rows, length in pieces]
    scratch += [pltpu.VMEM((near, rows, length), bf16) for rows, length in pieces]
    scratch += [pltpu.VMEM((far, rows, length), bf16) for rows, length in pieces]
    scratch += [pltpu.VMEM((near, rows, length), bf16) for rows, length in pieces]
    scratch += [pltpu.SemaphoreType.DMA((7, 8))] * 2
    scratch += [pltpu.SemaphoreType.DMA((3,))] * 2
    scratch += [pltpu.SemaphoreType.DMA((3,))] * 2
    scratch += [pltpu.SemaphoreType.DMA((3,))] * 2

    vmem = pl.BlockSpec(memory_space=pltpu.VMEM)
    partial_outputs = pl.pallas_call(
        functools.partial(kernel, (nb, nsx, nsy, nx, ny)),
        out_shape=(
            jax.ShapeDtypeStruct((chans, nx, ny, nz), bf16),
            *[jax.ShapeDtypeStruct((near, rows, length), bf16) for rows, length in pieces],
        ),
        in_specs=[pl.BlockSpec(memory_space=pl.ANY)] * 6,
        out_specs=[pl.BlockSpec(memory_space=pl.ANY)] * 4,
        scratch_shapes=scratch,
        compiler_params=pltpu.CompilerParams(
            collective_id=0, has_side_effects=True, vmem_limit_bytes=62 * 1024 * 1024
        ),
        name="unet_step",
    )(
        features[0],
        labels[0],
        w_enc.reshape(27, 32, 32),
        w_mid.swapaxes(3, 4).reshape(27, 32, 64),
        w_dec.reshape(27, 32, 96),
        w_out,
    )
    feature_grad, grad_enc, grad_mid, grad_dec, grad_out = pl.pallas_call(
        functools.partial(outputs, scale),
        out_shape=(
            jax.ShapeDtypeStruct((chans, nx, ny, nz), bf16),
            jax.ShapeDtypeStruct((27, 32, 32), f32),
            jax.ShapeDtypeStruct((27, 32, 64), f32),
            jax.ShapeDtypeStruct((27, 32, 96), f32),
            jax.ShapeDtypeStruct((4, 32), f32),
        ),
        in_specs=[pl.BlockSpec(memory_space=pl.ANY)] * 4,
        out_specs=[pl.BlockSpec(memory_space=pl.ANY)] * 5,
        scratch_shapes=[
            pltpu.VMEM((chans, nx, ny, nz), bf16),
            *[pltpu.VMEM((near, rows, length), bf16) for rows, length in pieces],
            pltpu.VMEM((27, 32, 32), f32),
            pltpu.VMEM((27, 32, 64), f32),
            pltpu.VMEM((27, 32, 96), f32),
            pltpu.VMEM((4, 32), f32),
            pltpu.SemaphoreType.DMA((9,)),
        ],
        compiler_params=pltpu.CompilerParams(vmem_limit_bytes=62 * 1024 * 1024),
        name="unet_outputs",
    )(*partial_outputs)
    return (
        feature_grad[None],
        grad_enc.reshape(w_enc.shape),
        grad_mid.reshape(3, 3, 3, 32, 64).swapaxes(3, 4),
        grad_dec.reshape(w_dec.shape),
        grad_out,
    )


def solution(mesh):
    placed = (P("batch", None, "sx", "sy", None), P("batch", "sx", "sy", None), P(), P(), P(), P())
    return jax.shard_map(
        shards,
        mesh=mesh,
        in_specs=placed,
        out_specs=(P("batch", None, "sx", "sy", None), P(), P(), P(), P()),
        check_vma=False,
    )
```

```python
import functools

import jax
import jax.numpy as jnp
from jax import lax
from jax.experimental import pallas as pl
from jax.experimental.pallas import tpu as pltpu
from jax.sharding import PartitionSpec as P

loss_scale = 32.0
LANES = 128
MESH = pl.DeviceIdType.MESH
f32 = jnp.float32
bf16 = jnp.bfloat16

DIRS = [(0, -1), (0, 1), (-1, -1), (-1, 1), (1, -1), (1, 1), (-1, 0), (1, 0)]
FEAT, POOL, SKIP, MID, DECG, MIDG, ENCG = range(7)
DEC, MIDW, ENC = range(3)


def lane_tile(y, count=1):
    if isinstance(y, int):
        return pl.ds(y * LANES, count * LANES)
    return pl.ds(pl.multiple_of(y * LANES, LANES), count * LANES)


def sigmoid(u):
    return 1.0 / (1.0 + jnp.exp(-u))


def shifted(tile, shift):
    lane = lax.broadcasted_iota(jnp.int32, tile.shape, 1)
    before = jnp.where(lane >= shift, pltpu.roll(tile, shift, axis=1), 0.0)
    after = jnp.where(lane < LANES - shift, pltpu.roll(tile, LANES - shift, axis=1), 0.0)
    return before.astype(bf16), after.astype(bf16)


def pair_sum(tile):
    lane = lax.broadcasted_iota(jnp.int32, tile.shape, 1)
    other = jnp.where(
        lane % 2 == 0, pltpu.roll(tile, LANES - 1, axis=1), pltpu.roll(tile, 1, axis=1)
    )
    return tile + other


def packed(tile):
    half = tile.shape[0] // 2
    lane = lax.broadcasted_iota(jnp.int32, (half, LANES), 1)
    return jnp.where(lane % 2 == 0, tile[:half], tile[half:]).astype(bf16)


def unpacked(tile):
    tile = tile.astype(f32)
    lane = lax.broadcasted_iota(jnp.int32, tile.shape, 1)
    first = jnp.where(lane % 2 == 0, tile, pltpu.roll(tile, 1, axis=1))
    second = jnp.where(lane % 2 == 1, tile, pltpu.roll(tile, LANES - 1, axis=1))
    return jnp.concatenate([first, second], axis=0)


def put_sides(buf, x, y, tile, period, offset, shift, back):
    chans = tile.shape[0]
    before, after = shifted(tile, shift)
    lanes = lane_tile(y)
    buf[x, offset : offset + chans, lanes] = after if back else before
    buf[x, 2 * period + offset : 2 * period + offset + chans, lanes] = before if back else after


def put_stack(buf, x, y, tile, period, offset, shift, back=False):
    chans = tile.shape[0]
    buf[x, period + offset : period + offset + chans, lane_tile(y)] = tile.astype(bf16)
    put_sides(buf, x, y, tile, period, offset, shift, back)


def each(first, last, step, carry):
    for at in range(first, last):
        step(at, carry)


def over_halo(nx, ny, step):
    for x in range(nx + 2):
        for y in range(ny + 2):
            if x in (0, nx + 1) or y in (0, ny + 1):
                step(x, y)


def finish_halo(buf, nx, ny, chans, period, offset, shift, back=False):
    def step(x, y):
        tile = buf[x, period + offset : period + offset + chans, lane_tile(y)].astype(f32)
        put_sides(buf, x, y, tile, period, offset, shift, back)

    over_halo(nx, ny, step)


def finish_inner(buf, nx, ny, chans, shift, back=False):
    for x in range(1, nx + 1):
        for y in range(1, ny + 1):
            tile = buf[x, chans : 2 * chans, lane_tile(y)].astype(f32)
            put_sides(buf, x, y, tile, chans, 0, shift, back)


def unpack_halo(buf, landed, nx, ny, chans, back=False):
    def step(x, y):
        put_stack(buf, x, y, unpacked(landed[x, :, lane_tile(y)]), chans, 0, 2, back)

    over_halo(nx, ny, step)


def clear_halo(buf, nx, ny, low, high):
    width = (ny + 2) * LANES
    buf[0, low:high, :] = jnp.zeros((high - low, width), bf16)
    buf[nx + 1, low:high, :] = jnp.zeros((high - low, width), bf16)
    for x in range(1, nx + 1):
        buf[x, low:high, lane_tile(0)] = jnp.zeros((high - low, LANES), bf16)
        buf[x, low:high, lane_tile(ny + 1)] = jnp.zeros((high - low, LANES), bf16)


def taps(fields, x, y, count, low, high, back=False):
    depth = sum(rows for _, _, rows in fields)
    parts = []
    for window in range(9):
        a, b = divmod(8 - window if back else window, 3)
        start = window * depth
        for buf, base, rows in fields:
            first, last = max(low, start), min(high, start + rows)
            if first < last:
                where = slice(base + first - start, base + last - start)
                parts.append(buf[x + a, where, lane_tile(y + b, count)])
            start += rows
    return parts[0] if len(parts) == 1 else jnp.concatenate(parts, axis=0)


def conv(weight, buf, x, tiles, back=False):
    depth = buf.shape[1]
    fields = [(buf, 0, depth)]
    y, other = tiles
    if other == y + 1:
        window = taps(fields, x, y, 2, 0, 9 * depth, back)
    else:
        window = jnp.concatenate(
            [taps(fields, x, at, 1, 0, 9 * depth, back) for at in tiles], axis=1
        )
    return jnp.dot(weight[...], window, preferred_element_type=f32)


def inner_pairs(ny):
    return [(y, y + 1) for y in range(1, ny - 1, 2)]


def all_pairs(ny):
    return [(y, y + 1) for y in range(0, ny, 2)]


def ranges_of(nx):
    return [(1, 3) if x == 0 else (0, 2) if x == nx - 1 else (0, 3) for x in range(nx)]


def local_part(sums, weights, buf, nx, ny, first):
    for x, (low, high) in enumerate(ranges_of(nx)):
        for y in range(1, ny + 1, 2):
            lanes = lane_tile(y, 2)
            window = jnp.concatenate([buf[x + a, :, lanes] for a in range(low, high)], axis=0)
            term = jnp.dot(weights[low, high][...], window, preferred_element_type=f32)
            if first:
                sums[x, :, lanes] = term
            else:
                sums[x, :, lanes] += term


def border_part(sums, weights, buf, nx, ny, first):
    sides = (lane_tile(0), lane_tile(ny + 1))
    for x in range(nx):
        window = jnp.concatenate(
            [jnp.concatenate([buf[x + a, :, s] for s in sides], axis=1) for a in range(3)], axis=0
        )
        term = jnp.dot(weights[0, 3][...], window, preferred_element_type=f32)
        for at, lanes in enumerate(sides):
            part = term[:, at * LANES : (at + 1) * LANES]
            if first:
                sums[x, :, lanes] = part
            else:
                sums[x, :, lanes] += part
    for x, a in ((0, 0), (nx - 1, 2)):
        for y in range(1, ny + 1, 2):
            lanes = lane_tile(y, 2)
            sums[x, :, lanes] += jnp.dot(
                weights[a, a + 1][...], buf[x + a, :, lanes], preferred_element_type=f32
            )


def weight_grad(total, grads, fields, size_x, count):
    width = 9 * sum(rows for _, _, rows in fields)
    for low in range(0, width, 256):
        high = min(low + 256, width)
        acc = None
        for x in range(size_x):
            term = lax.dot_general(
                grads(x),
                taps(fields, x, 0, count, low, high),
                (((1,), (1,)), ((), ())),
                preferred_element_type=f32,
            )
            acc = term if acc is None else acc + term
        total[:, low:high] = acc
    rest = total.shape[1] - width
    total[:, width:] = jnp.zeros((total.shape[0], rest), f32)


def laid_lanes(w, order):
    return jnp.concatenate([w[t] for t in order], axis=1)


def forward_weights(dest, w):
    for low in range(0, 27, 4):
        high = min(low + 4, 27)
        dest[:, low * 32 : high * 32] = laid_lanes(w, range(low, high))


def window_weights(dests, w, first, last):
    for (low, high), dest in dests.items():
        for b in range(3):
            parts = [
                w[(a * 3 + b) * 3 + c, :, first:last] for a in range(low, high) for c in range(3)
            ]
            dest[b * 32 : (b + 1) * 32, :] = jnp.concatenate(parts, axis=1)


def turned_weights(dest, w):
    count, outs, ins = w.shape
    flat = w[...].astype(f32).reshape(count * outs, ins)
    dest[...] = flat.T.astype(bf16)


def kernel(
    sizes,
    feat_hbm,
    labels_hbm,
    w_enc_hbm,
    w_mid_hbm,
    w_dec_hbm,
    w_out_hbm,
    feature_grad_hbm,
    sum_dec,
    sum_mid,
    sum_enc,
    feat,
    labels,
    w_enc,
    w_mid,
    w_dec,
    w_out,
    load_sem,
    feature_grad,
    store_sem,
    w_enc_f,
    w_enc_b,
    w_mid_f,
    w_mid_b,
    w_skip_03,
    w_skip_13,
    w_skip_02,
    w_skip_01,
    w_skip_23,
    w_up_03,
    w_up_13,
    w_up_02,
    w_up_01,
    w_up_23,
    w_dec_b,
    rows32,
    window_sums,
    F,
    PO,
    PP,
    UP,
    JU,
    JE,
    D,
    MG,
    MGP,
    EG,
    enc_slope,
    mid_slope,
    joined_grad,
    out_total,
    total_dec,
    total_mid,
    total_enc,
    part_dec,
    part_mid,
    part_enc,
    rs_dec,
    rs_mid,
    rs_enc,
    ar_dec,
    ar_mid,
    ar_enc,
    ag_dec,
    ag_mid,
    ag_enc,
    halo_send,
    halo_recv,
    rs_send,
    rs_recv,
    ar_send,
    ar_recv,
    ag_send,
    ag_recv,
):
    nb, nsx, nsy, nx, ny = sizes
    cx, cy = nx // 2, ny // 2
    half = nsy // 2
    near, far = nb * half, nsx * 2
    bt, sx, sy = lax.axis_index("batch"), lax.axis_index("sx"), lax.axis_index("sy")
    here, there = bt * half + lax.rem(sy, half), sx * 2 + sy // half
    skip_weights = {
        (0, 3): w_skip_03,
        (1, 3): w_skip_13,
        (0, 2): w_skip_02,
        (0, 1): w_skip_01,
        (2, 3): w_skip_23,
    }
    up_weights = {
        (0, 3): w_up_03,
        (1, 3): w_up_13,
        (0, 2): w_up_02,
        (0, 1): w_up_01,
        (2, 3): w_up_23,
    }

    loads = {
        name: pltpu.make_async_copy(source, dest, load_sem.at[at])
        for at, (name, source, dest) in enumerate(
            (
                ("feat", feat_hbm, feat),
                ("w_enc", w_enc_hbm, w_enc),
                ("w_mid", w_mid_hbm, w_mid),
                ("w_dec", w_dec_hbm, w_dec),
                ("w_out", w_out_hbm, w_out),
                ("labels", labels_hbm, labels),
            )
        )
    }
    for load in loads.values():
        load.start()

    clear_halo(F, nx, ny, 32, 64)
    clear_halo(PP, cx, cy, 0, 16)
    clear_halo(JE, nx, ny, 32, 64)
    clear_halo(UP, cx, cy, 0, 32)
    clear_halo(D, nx, ny, 32, 64)
    clear_halo(MGP, cx, cy, 0, 32)
    clear_halo(EG, nx, ny, 32, 64)

    def near_peer(k):
        return lax.rem(here + k, near)

    def near_id(p):
        return (p // half, sx, (sy // half) * half + lax.rem(p, half))

    def far_peer(k):
        return lax.rem(there + k, far)

    def far_id(q):
        return (bt, q // 2, lax.rem(q, 2) * half + lax.rem(sy, half))

    barrier = pltpu.get_barrier_semaphore()
    for dx, dy in DIRS:
        pl.semaphore_signal(
            barrier,
            inc=1,
            device_id=(bt, lax.rem(sx + dx + nsx, nsx), lax.rem(sy + dy + nsy, nsy)),
            device_id_type=MESH,
        )
    for k in range(1, far):
        pl.semaphore_signal(barrier, inc=1, device_id=far_id(far_peer(k)), device_id_type=MESH)
    for k in range(1, near):
        pl.semaphore_signal(barrier, inc=1, device_id=near_id(near_peer(k)), device_id_type=MESH)

    loads["feat"].wait()

    def load_features(x, carry):
        rows32[x] = feat[:, x].astype(f32).reshape(32 * ny, LANES)
        for y in range(ny):
            put_stack(F, x + 1, y + 1, rows32[x, pl.ds(y, 32, stride=ny), :], 32, 0, 1)
        return carry

    each(0, nx, load_features, 0)

    pl.semaphore_wait(barrier, near - 1 + far - 1 + 8)

    fields = {
        FEAT: (F, nx, ny, 32, 64),
        POOL: (PP, cx, cy, 0, 16),
        SKIP: (JE, nx, ny, 32, 64),
        MID: (UP, cx, cy, 0, 32),
        DECG: (D, nx, ny, 32, 64),
        MIDG: (MGP, cx, cy, 0, 32),
        ENCG: (EG, nx, ny, 32, 64),
    }

    def halo_copy(field, index):
        buf, sizex, sizey, low, high = fields[field]
        dx, dy = DIRS[index]

        def source(step, size):
            return {-1: (1, 1), 0: (1, size), 1: (size, 1)}[step]

        def target(step, size):
            return {-1: (size + 1, 1), 0: (1, size), 1: (0, 1)}[step]

        (x0, xn), (y0, yn) = source(dx, sizex), source(dy, sizey)
        (tx0, _), (ty0, _) = target(dx, sizex), target(dy, sizey)
        return pltpu.make_async_remote_copy(
            src_ref=buf.at[pl.ds(x0, xn), low:high, lane_tile(y0, yn)],
            dst_ref=buf.at[pl.ds(tx0, xn), low:high, lane_tile(ty0, yn)],
            send_sem=halo_send.at[field, index],
            recv_sem=halo_recv.at[field, index],
            device_id=(bt, lax.rem(sx + dx + nsx, nsx), lax.rem(sy + dy + nsy, nsy)),
            device_id_type=MESH,
        )

    def inside(dx, dy):
        ok = None
        for step, at, size in ((dx, sx, nsx), (dy, sy, nsy)):
            if step:
                this = at > 0 if step < 0 else at < size - 1
                ok = this if ok is None else jnp.logical_and(ok, this)
        return ok

    def start_halo(field):
        for index, (dx, dy) in enumerate(DIRS):

            @pl.when(inside(dx, dy))
            def _():
                halo_copy(field, index).start()

    def wait_halo(field):
        for index, (dx, dy) in enumerate(DIRS):

            @pl.when(inside(-dx, -dy))
            def _():
                halo_copy(field, index).wait_recv()

    def wait_halo_sent(field):
        for index, (dx, dy) in enumerate(DIRS):

            @pl.when(inside(dx, dy))
            def _():
                halo_copy(field, index).wait_send()

    cut_dec = [(0, 96, 128 * j, 128) for j in range(8)]
    cut_mid = [(0, 64, 128 * j, 128) for j in range(8)]
    cut_enc = [(48 * (j % 2), 48, 128 * (j // 2), 128) for j in range(6)] + [None] * 2
    sums = {
        DEC: (total_dec, part_dec, rs_dec, ar_dec, ag_dec, cut_dec),
        MIDW: (total_mid, part_mid, rs_mid, ar_mid, ag_mid, cut_mid),
        ENC: (total_enc, part_enc, rs_enc, ar_enc, ag_enc, cut_enc),
    }

    def rs_copy(g, k):
        _, part, landing, _, _, _ = sums[g]
        return pltpu.make_async_remote_copy(
            src_ref=part.at[near_peer(k)],
            dst_ref=landing.at[here],
            send_sem=rs_send.at[g],
            recv_sem=rs_recv.at[g],
            device_id=near_id(near_peer(k)),
            device_id_type=MESH,
        )

    def ar_copy(g, k):
        landing = sums[g][3]
        return pltpu.make_async_remote_copy(
            src_ref=landing.at[there],
            dst_ref=landing.at[there],
            send_sem=ar_send.at[g],
            recv_sem=ar_recv.at[g],
            device_id=far_id(far_peer(k)),
            device_id_type=MESH,
        )

    def ag_copy(g, k):
        landing = sums[g][4]
        return pltpu.make_async_remote_copy(
            src_ref=landing.at[here],
            dst_ref=landing.at[here],
            send_sem=ag_send.at[g],
            recv_sem=ag_recv.at[g],
            device_id=near_id(near_peer(k)),
            device_id_type=MESH,
        )

    def wait_bytes(sem, pieces):
        pltpu.make_async_copy(pieces, pieces, sem).wait()

    def start_scatter(g):
        total, part, _, _, _, cut = sums[g]
        for j in range(near):
            if cut[j] is None:
                part[j] = jnp.zeros(part.shape[1:], bf16)
            else:
                row, rows, lane, lanes = cut[j]
                part[j] = total[row : row + rows, lane : lane + lanes].astype(bf16)
        for k in range(1, near):
            rs_copy(g, k).start()

    def start_exchange(g):
        _, part, landing, mine, _, _ = sums[g]
        wait_bytes(rs_recv.at[g], landing.at[pl.ds(0, near - 1)])
        acc = part[here].astype(f32)
        for k in range(1, near):
            acc = acc + landing[near_peer(k)].astype(f32)
        mine[there] = acc.astype(bf16)
        for k in range(1, far):
            ar_copy(g, k).start()

    def start_gather(g):
        _, _, _, landing, result, _ = sums[g]
        wait_bytes(ar_recv.at[g], landing.at[pl.ds(0, far - 1)])
        acc = landing[0].astype(f32)
        for q in range(1, far):
            acc = acc + landing[q].astype(f32)
        result[here] = acc.astype(bf16)
        for k in range(1, near):
            ag_copy(g, k).start()

    def wait_gather(g):
        wait_bytes(ag_recv.at[g], sums[g][4].at[pl.ds(0, near - 1)])

    def wait_scatter_sent(g):
        wait_bytes(rs_send.at[g], sums[g][1].at[pl.ds(0, near - 1)])

    def wait_exchange_sent(g):
        wait_bytes(ar_send.at[g], sums[g][3].at[pl.ds(0, far - 1)])

    def wait_gather_sent(g):
        wait_bytes(ag_send.at[g], sums[g][4].at[pl.ds(0, near - 1)])

    start_halo(FEAT)
    for name in ("w_enc", "w_mid", "w_dec", "w_out", "labels"):
        loads[name].wait()
    forward_weights(w_enc_f, w_enc)

    def enc_tiles(x, tiles):
        pre = conv(w_enc_f, F, x, tiles)
        s = sigmoid(pre)
        slope = s * (1.0 + pre * (1.0 - s))
        act = (pre * s).astype(bf16).astype(f32)
        for at, y in enumerate(tiles):
            lanes = slice(at * LANES, (at + 1) * LANES)
            enc_slope[x, :, lane_tile(y)] = slope[:, lanes]
            JE[x + 1, 32:64, lane_tile(y + 1)] = act[:, lanes].astype(bf16)

    def enc_inner(x, carry):
        for tiles in inner_pairs(ny):
            enc_tiles(x, tiles)
        return carry

    each(1, nx - 1, enc_inner, 0)
    turned_weights(w_mid_f, w_mid)
    window_weights(skip_weights, w_dec, 64, 96)
    window_weights(up_weights, w_dec, 0, 64)
    out_total[...] = jnp.zeros(out_total.shape, f32)
    wait_halo(FEAT)
    finish_halo(F, nx, ny, 32, 32, 0, 1)

    def enc_sides(x, carry):
        enc_tiles(x, (0, ny - 1))
        return carry

    each(1, nx - 1, enc_sides, 0)

    def enc_ends(i, carry):
        for tiles in all_pairs(ny):
            enc_tiles(i * (nx - 1), tiles)
        return carry

    each(0, 2, enc_ends, 0)

    def pool_block(bx, carry):
        for by in range(cy):
            block = jnp.zeros((32, LANES), f32)
            for dx in range(2):
                for dy in range(2):
                    block += JE[2 * bx + dx + 1, 32:64, lane_tile(2 * by + dy + 1)].astype(f32)
            pooled = (pair_sum(block) * 0.125).astype(bf16).astype(f32)
            PP[bx + 1, :, lane_tile(by + 1)] = packed(pooled)
            PO[bx + 1, 32:64, lane_tile(by + 1)] = pooled.astype(bf16)
        return carry

    each(0, cx, pool_block, 0)
    start_halo(POOL)
    start_halo(SKIP)
    finish_inner(PO, cx, cy, 32, 2)
    finish_inner(JE, nx, ny, 32, 1)
    local_part(window_sums, skip_weights, JE, nx, ny, True)
    turned_weights(w_enc_b, w_enc)
    turned_weights(w_dec_b, w_dec)
    for low in range(0, 27, 2):
        high = min(low + 2, 27)
        w_mid_b[:, low * 64 : high * 64] = laid_lanes(w_mid, range(low, high))
    wait_halo(POOL)
    unpack_halo(PO, PP, cx, cy, 32)

    def mid_block(bx, carry):
        for by in range(0, cy, 2):
            pre = conv(w_mid_f, PO, bx, (by, by + 1))
            s = sigmoid(pre)
            mid_slope[bx, :, lane_tile(by, 2)] = s * (1.0 + pre * (1.0 - s))
            act = (pre * s).astype(bf16)
            for dy in range(2):
                tile = act[:, dy * LANES : (dy + 1) * LANES]
                UP[bx + 1, :, lane_tile(by + dy + 1)] = packed(tile.astype(f32))
                JU[2 * bx + 1, 64:128, lane_tile(2 * (by + dy) + 1)] = tile
        return carry

    each(0, cx, mid_block, 0)
    start_halo(MID)

    def spread(bx, by, tile):
        before, after = shifted(tile, 1)
        tile = tile.astype(bf16)
        for x in (2 * bx - 1, 2 * bx):
            for y in (2 * by - 1, 2 * by):
                if 0 <= x <= nx + 1 and 0 <= y <= ny + 1:
                    lanes = lane_tile(y)
                    JU[x, 0:64, lanes] = before
                    JU[x, 64:128, lanes] = tile
                    JU[x, 128:192, lanes] = after

    for bx in range(1, cx + 1):
        for by in range(1, cy + 1):
            spread(bx, by, JU[2 * bx - 1, 64:128, lane_tile(2 * by - 1)].astype(f32))
    local_part(window_sums, up_weights, JU, nx, ny, False)
    wait_halo(SKIP)
    finish_halo(JE, nx, ny, 32, 32, 0, 1)
    border_part(window_sums, skip_weights, JE, nx, ny, True)
    wait_halo(MID)
    for bx in range(cx + 2):
        for by in range(cy + 2):
            if bx in (0, cx + 1) or by in (0, cy + 1):
                spread(bx, by, unpacked(UP[bx, :, lane_tile(by)]))

    border_part(window_sums, up_weights, JU, nx, ny, False)

    def dec_row(x, carry):
        pre = (
            window_sums[x, 0:32, lane_tile(0, ny)]
            + window_sums[x, 32:64, lane_tile(1, ny)]
            + window_sums[x, 64:96, lane_tile(2, ny)]
        )
        s = sigmoid(pre)
        slope = s * (1.0 + pre * (1.0 - s))
        act = (pre * s).astype(bf16)
        logits = jnp.dot(w_out[...], act, preferred_element_type=f32)
        expo = jnp.exp(logits)
        prob = expo / jnp.sum(expo, axis=0, keepdims=True)
        ids = lax.broadcasted_iota(jnp.int32, prob.shape, 0)
        these = jnp.concatenate([labels[x, y : y + 1, :] for y in range(ny)], axis=1)
        onehot = (these == ids).astype(f32)
        logit_grad = (loss_scale * (prob - onehot)).astype(bf16)
        out_total[...] += lax.dot_general(
            logit_grad, act, (((1,), (1,)), ((), ())), preferred_element_type=f32
        )
        act_grad = lax.dot_general(
            w_out[...], logit_grad, (((0,), (0,)), ((), ())), preferred_element_type=f32
        )
        grads = (act_grad * slope).astype(bf16).astype(f32)
        for y in range(ny):
            tile = grads[:, y * LANES : (y + 1) * LANES]
            D[x + 1, 32:64, lane_tile(y + 1)] = tile.astype(bf16)
        return carry

    each(0, nx, dec_row, 0)
    start_halo(DECG)
    finish_inner(D, nx, ny, 32, 1, back=True)

    def dec_back(x, tiles):
        grads = conv(w_dec_b, D, x, tiles, back=True)
        for at, y in enumerate(tiles):
            joined_grad[x, :, lane_tile(y)] = grads[:, at * LANES : (at + 1) * LANES]

    def dec_back_inner(x, carry):
        for tiles in inner_pairs(ny):
            dec_back(x, tiles)
        return carry

    each(1, nx - 1, dec_back_inner, 0)
    joined = [(JU, 64, 64), (JE, 32, 32)]
    weight_grad(total_dec, lambda x: D[x + 1, :, lane_tile(1, ny)], joined, nx, ny)
    total_dec[0:4, 864:896] = out_total[...]
    start_scatter(DEC)

    wait_halo(DECG)
    finish_halo(D, nx, ny, 32, 32, 0, 1, back=True)

    def dec_back_sides(x, carry):
        dec_back(x, (0, ny - 1))
        return carry

    each(1, nx - 1, dec_back_sides, 0)

    def dec_back_ends(i, carry):
        for tiles in all_pairs(ny):
            dec_back(i * (nx - 1), tiles)
        return carry

    each(0, 2, dec_back_ends, 0)

    def mid_grads(bx, carry):
        for by in range(cy):
            block = jnp.zeros((64, LANES), f32)
            for dx in range(2):
                for dy in range(2):
                    block += joined_grad[2 * bx + dx, 0:64, lane_tile(2 * by + dy)]
            grads = pair_sum(block) * mid_slope[bx, :, lane_tile(by)]
            grads = grads.astype(bf16).astype(f32)
            MGP[bx + 1, :, lane_tile(by + 1)] = packed(grads)
            MG[bx + 1, 64:128, lane_tile(by + 1)] = grads.astype(bf16)
        return carry

    each(0, cx, mid_grads, 0)
    start_halo(MIDG)
    finish_inner(MG, cx, cy, 64, 2, back=True)

    weight_grad(total_mid, lambda x: MG[x + 1, 64:128, lane_tile(1, cy)], [(PO, 0, 96)], cx, cy)
    start_scatter(MIDW)
    start_exchange(DEC)

    wait_halo(MIDG)
    start_exchange(MIDW)
    unpack_halo(MG, MGP, cx, cy, 64, back=True)

    def mid_back(bx, carry):
        for by in range(0, cy, 2):
            pooled = conv(w_mid_b, MG, bx, (by, by + 1), back=True) * 0.125
            for dx in range(2):
                x = 2 * bx + dx
                for dy in range(4):
                    y = 2 * by + dy
                    up = pooled[:, (dy // 2) * LANES : (dy // 2 + 1) * LANES]
                    tile = (joined_grad[x, 64:96, lane_tile(y)] + up) * enc_slope[x, :, lane_tile(y)]
                    put_stack(EG, x + 1, y + 1, tile, 32, 0, 1, back=True)
        return carry

    each(0, cx, mid_back, 0)
    start_halo(ENCG)

    weight_grad(total_enc, lambda x: EG[x + 1, :, lane_tile(1, ny)], [(F, 32, 32)], nx, ny)
    start_scatter(ENC)

    def enc_back(x, tiles):
        grads = conv(w_enc_b, EG, x, tiles, back=True)
        for at, y in enumerate(tiles):
            rows32[x, pl.ds(y, 32, stride=ny), :] = grads[:, at * LANES : (at + 1) * LANES]

    def enc_back_inner(x, carry):
        for tiles in inner_pairs(ny):
            enc_back(x, tiles)
        return carry

    each(1, nx - 1, enc_back_inner, 0)
    start_exchange(ENC)
    wait_halo(ENCG)
    finish_halo(EG, nx, ny, 32, 32, 0, 1, back=True)

    def enc_back_sides(x, carry):
        enc_back(x, (0, ny - 1))
        return carry

    each(1, nx - 1, enc_back_sides, 0)

    def enc_back_ends(i, carry):
        for tiles in all_pairs(ny):
            enc_back(i * (nx - 1), tiles)
        return carry

    each(0, 2, enc_back_ends, 0)

    def lay_out(x, carry):
        feature_grad[:, x] = rows32[x].reshape(32, ny, LANES).astype(bf16)
        return carry

    each(0, nx, lay_out, 0)
    stores = [
        pltpu.make_async_copy(source, dest, store_sem.at[at])
        for at, (source, dest) in enumerate(
            (
                (feature_grad, feature_grad_hbm),
                (ag_dec, sum_dec),
                (ag_mid, sum_mid),
                (ag_enc, sum_enc),
            )
        )
    ]
    stores[0].start()
    start_gather(DEC)
    start_gather(MIDW)
    for field in range(7):
        wait_halo_sent(field)
    for g in (DEC, MIDW, ENC):
        wait_scatter_sent(g)
    start_gather(ENC)
    wait_gather(DEC)
    stores[1].start()
    wait_gather(MIDW)
    stores[2].start()
    for g in (DEC, MIDW, ENC):
        wait_exchange_sent(g)
    for g in (DEC, MIDW):
        wait_gather_sent(g)
    wait_gather(ENC)
    stores[3].start()
    wait_gather_sent(ENC)
    for store in stores:
        store.wait()


def outputs(
    scale,
    features_in,
    dec_in,
    mid_in,
    enc_in,
    features_out,
    enc_out,
    mid_out,
    dec_out,
    out_out,
    features,
    sum_dec,
    sum_mid,
    sum_enc,
    grad_enc,
    grad_mid,
    grad_dec,
    grad_out,
    sems,
):
    copies = [
        pltpu.make_async_copy(source, dest, sems.at[at])
        for at, (source, dest) in enumerate(
            (
                (dec_in, sum_dec),
                (mid_in, sum_mid),
                (enc_in, sum_enc),
                (features_in, features),
                (grad_dec, dec_out),
                (grad_out, out_out),
                (grad_mid, mid_out),
                (grad_enc, enc_out),
                (features, features_out),
            )
        )
    ]
    for copy in copies[:4]:
        copy.start()
    copies[0].wait()
    whole = jnp.concatenate([sum_dec[j].astype(f32) for j in range(8)], axis=1) * scale
    for t in range(27):
        window, c = divmod(t, 3)
        grad_dec[t] = whole[c * 32 : (c + 1) * 32, window * 96 : (window + 1) * 96]
    grad_out[...] = whole[0:4, 864:896]
    copies[4].start()
    copies[5].start()
    copies[3].wait()
    copies[8].start()
    copies[1].wait()
    for j in range(7):
        turned = (sum_mid[j].astype(f32) * (0.5 * scale)).T
        for t in range(4 * j, min(4 * j + 4, 27)):
            grad_mid[t] = turned[(t % 4) * 32 : (t % 4 + 1) * 32]
    copies[6].start()
    copies[2].wait()
    for window in range(9):
        j, at = divmod(window, 4)
        both = jnp.concatenate([sum_enc[2 * j], sum_enc[2 * j + 1]], axis=0)
        part = both[:, at * 32 : (at + 1) * 32].astype(f32) * scale
        for c in range(3):
            grad_enc[window * 3 + c] = part[c * 32 : (c + 1) * 32]
    copies[7].start()
    for copy in copies[4:]:
        copy.wait()


def shards(features, labels, w_enc, w_mid, w_dec, w_out):
    nb, nsx, nsy = lax.axis_size("batch"), lax.axis_size("sx"), lax.axis_size("sy")
    _, chans, nx, ny, nz = features.shape
    cx, cy = nx // 2, ny // 2
    scale = 1.0 / float(nb * nsx * nsy * nx * ny * nz)
    near, far = nb * (nsy // 2), nsx * 2

    def fine(depth):
        return pltpu.VMEM((nx + 2, depth, (ny + 2) * LANES), bf16)

    def coarse(depth):
        return pltpu.VMEM((cx + 2, depth, (cy + 2) * LANES), bf16)

    pieces = ((96, 128), (64, 128), (48, 128))
    scratch = [
        pltpu.VMEM((chans, nx, ny, nz), bf16),
        pltpu.VMEM((nx, ny, nz), jnp.int32),
        pltpu.VMEM((27, 32, 32), bf16),
        pltpu.VMEM((27, 32, 64), bf16),
        pltpu.VMEM((27, 32, 96), bf16),
        pltpu.VMEM((4, 32), bf16),
        pltpu.SemaphoreType.DMA((6,)),
        pltpu.VMEM((chans, nx, ny, nz), bf16),
        pltpu.SemaphoreType.DMA((4,)),
        pltpu.VMEM((32, 864), bf16),
        pltpu.VMEM((32, 864), bf16),
        pltpu.VMEM((64, 864), bf16),
        pltpu.VMEM((32, 1728), bf16),
        *[pltpu.VMEM((96, 96 * count), bf16) for count in (3, 2, 2, 1, 1)],
        *[pltpu.VMEM((96, 192 * count), bf16) for count in (3, 2, 2, 1, 1)],
        pltpu.VMEM((96, 864), bf16),
        pltpu.VMEM((nx, 32 * ny, LANES), f32),
        pltpu.VMEM((nx, 96, (ny + 2) * LANES), f32),
        fine(96),
        coarse(96),
        coarse(16),
        coarse(32),
        fine(192),
        fine(96),
        fine(96),
        coarse(192),
        coarse(32),
        fine(96),
        pltpu.VMEM((nx, 32, ny * LANES), f32),
        pltpu.VMEM((cx, 64, cy * LANES), f32),
        pltpu.VMEM((nx, 96, ny * LANES), f32),
        pltpu.VMEM((4, 32), f32),
        pltpu.VMEM((96, 1024), f32),
        pltpu.VMEM((64, 1024), f32),
        pltpu.VMEM((96, 384), f32),
    ]
    scratch += [pltpu.VMEM((near, rows, length), bf16) for rows, length in pieces]
    scratch += [pltpu.VMEM((near, rows, length), bf16) for rows, length in pieces]
    scratch += [pltpu.VMEM((far, rows, length), bf16) for rows, length in pieces]
    scratch += [pltpu.VMEM((near, rows, length), bf16) for rows, length in pieces]
    scratch += [pltpu.SemaphoreType.DMA((7, 8))] * 2
    scratch += [pltpu.SemaphoreType.DMA((3,))] * 2
    scratch += [pltpu.SemaphoreType.DMA((3,))] * 2
    scratch += [pltpu.SemaphoreType.DMA((3,))] * 2

    vmem = pl.BlockSpec(memory_space=pltpu.VMEM)
    partial_outputs = pl.pallas_call(
        functools.partial(kernel, (nb, nsx, nsy, nx, ny)),
        out_shape=(
            jax.ShapeDtypeStruct((chans, nx, ny, nz), bf16),
            *[jax.ShapeDtypeStruct((near, rows, length), bf16) for rows, length in pieces],
        ),
        in_specs=[pl.BlockSpec(memory_space=pl.ANY)] * 6,
        out_specs=[pl.BlockSpec(memory_space=pl.ANY)] * 4,
        scratch_shapes=scratch,
        compiler_params=pltpu.CompilerParams(
            collective_id=0, has_side_effects=True, vmem_limit_bytes=62 * 1024 * 1024
        ),
        name="unet_step",
    )(
        features[0],
        labels[0],
        w_enc.reshape(27, 32, 32),
        w_mid.swapaxes(3, 4).reshape(27, 32, 64),
        w_dec.reshape(27, 32, 96),
        w_out,
    )
    feature_grad, grad_enc, grad_mid, grad_dec, grad_out = pl.pallas_call(
        functools.partial(outputs, scale),
        out_shape=(
            jax.ShapeDtypeStruct((chans, nx, ny, nz), bf16),
            jax.ShapeDtypeStruct((27, 32, 32), f32),
            jax.ShapeDtypeStruct((27, 32, 64), f32),
            jax.ShapeDtypeStruct((27, 32, 96), f32),
            jax.ShapeDtypeStruct((4, 32), f32),
        ),
        in_specs=[pl.BlockSpec(memory_space=pl.ANY)] * 4,
        out_specs=[pl.BlockSpec(memory_space=pl.ANY)] * 5,
        scratch_shapes=[
            pltpu.VMEM((chans, nx, ny, nz), bf16),
            *[pltpu.VMEM((near, rows, length), bf16) for rows, length in pieces],
            pltpu.VMEM((27, 32, 32), f32),
            pltpu.VMEM((27, 32, 64), f32),
            pltpu.VMEM((27, 32, 96), f32),
            pltpu.VMEM((4, 32), f32),
            pltpu.SemaphoreType.DMA((9,)),
        ],
        compiler_params=pltpu.CompilerParams(vmem_limit_bytes=62 * 1024 * 1024),
        name="unet_outputs",
    )(*partial_outputs)
    return (
        feature_grad[None],
        grad_enc.reshape(w_enc.shape),
        grad_mid.reshape(3, 3, 3, 32, 64).swapaxes(3, 4),
        grad_dec.reshape(w_dec.shape),
        grad_out,
    )


def solution(mesh):
    placed = (P("batch", None, "sx", "sy", None), P("batch", "sx", "sy", None), P(), P(), P(), P())
    return jax.shard_map(
        shards,
        mesh=mesh,
        in_specs=placed,
        out_specs=(P("batch", None, "sx", "sy", None), P(), P(), P(), P()),
        check_vma=False,
    )
```

```python
import functools

import jax
import jax.numpy as jnp
from jax import lax
from jax.experimental import pallas as pl
from jax.experimental.pallas import tpu as pltpu
from jax.sharding import PartitionSpec as P

loss_scale = 32.0
LANES = 128
MESH = pl.DeviceIdType.MESH
f32 = jnp.float32
bf16 = jnp.bfloat16

DIRS = [(0, -1), (0, 1), (-1, -1), (-1, 1), (1, -1), (1, 1), (-1, 0), (1, 0)]
FEAT, POOL, SKIP, MID, DECG, MIDG, ENCG = range(7)
DEC, MIDW, ENC = range(3)


def lane_tile(y, count=1):
    if isinstance(y, int):
        return pl.ds(y * LANES, count * LANES)
    return pl.ds(pl.multiple_of(y * LANES, LANES), count * LANES)


def sigmoid(u):
    return 1.0 / (1.0 + jnp.exp(-u))


def shifted(tile, shift):
    lane = lax.broadcasted_iota(jnp.int32, tile.shape, 1)
    before = jnp.where(lane >= shift, pltpu.roll(tile, shift, axis=1), 0.0)
    after = jnp.where(lane < LANES - shift, pltpu.roll(tile, LANES - shift, axis=1), 0.0)
    return before.astype(bf16), after.astype(bf16)


def pair_sum(tile):
    lane = lax.broadcasted_iota(jnp.int32, tile.shape, 1)
    other = jnp.where(
        lane % 2 == 0, pltpu.roll(tile, LANES - 1, axis=1), pltpu.roll(tile, 1, axis=1)
    )
    return tile + other


def packed(tile):
    half = tile.shape[0] // 2
    lane = lax.broadcasted_iota(jnp.int32, (half, LANES), 1)
    return jnp.where(lane % 2 == 0, tile[:half], tile[half:]).astype(bf16)


def unpacked(tile):
    tile = tile.astype(f32)
    lane = lax.broadcasted_iota(jnp.int32, tile.shape, 1)
    first = jnp.where(lane % 2 == 0, tile, pltpu.roll(tile, 1, axis=1))
    second = jnp.where(lane % 2 == 1, tile, pltpu.roll(tile, LANES - 1, axis=1))
    return jnp.concatenate([first, second], axis=0)


def put_sides(buf, x, y, tile, period, offset, shift, back):
    chans = tile.shape[0]
    before, after = shifted(tile, shift)
    lanes = lane_tile(y)
    buf[x, offset : offset + chans, lanes] = after if back else before
    buf[x, 2 * period + offset : 2 * period + offset + chans, lanes] = before if back else after


def put_stack(buf, x, y, tile, period, offset, shift, back=False):
    chans = tile.shape[0]
    buf[x, period + offset : period + offset + chans, lane_tile(y)] = tile.astype(bf16)
    put_sides(buf, x, y, tile, period, offset, shift, back)


def each(first, last, step, carry):
    for at in range(first, last):
        step(at, carry)


def over_halo(nx, ny, step, part=None):
    for x in range(nx + 2):
        for y in range(ny + 2):
            side = y in (0, ny + 1)
            if (x in (0, nx + 1) or side) and (part is None or part != side):
                step(x, y)


def finish_halo(buf, nx, ny, chans, period, offset, shift, back=False, part=None):
    def step(x, y):
        tile = buf[x, period + offset : period + offset + chans, lane_tile(y)].astype(f32)
        put_sides(buf, x, y, tile, period, offset, shift, back)

    over_halo(nx, ny, step, part)


def finish_inner(buf, nx, ny, chans, shift, back=False):
    for x in range(1, nx + 1):
        for y in range(1, ny + 1):
            tile = buf[x, chans : 2 * chans, lane_tile(y)].astype(f32)
            put_sides(buf, x, y, tile, chans, 0, shift, back)


def unpack_halo(buf, landed, nx, ny, chans, back=False):
    def step(x, y):
        put_stack(buf, x, y, unpacked(landed[x, :, lane_tile(y)]), chans, 0, 2, back)

    over_halo(nx, ny, step)


def clear_halo(buf, nx, ny, low, high):
    width = (ny + 2) * LANES
    buf[0, low:high, :] = jnp.zeros((high - low, width), bf16)
    buf[nx + 1, low:high, :] = jnp.zeros((high - low, width), bf16)
    for x in range(1, nx + 1):
        buf[x, low:high, lane_tile(0)] = jnp.zeros((high - low, LANES), bf16)
        buf[x, low:high, lane_tile(ny + 1)] = jnp.zeros((high - low, LANES), bf16)


def taps(fields, x, y, count, low, high, back=False):
    depth = sum(rows for _, _, rows in fields)
    parts = []
    for window in range(9):
        a, b = divmod(8 - window if back else window, 3)
        start = window * depth
        for buf, base, rows in fields:
            first, last = max(low, start), min(high, start + rows)
            if first < last:
                where = slice(base + first - start, base + last - start)
                parts.append(buf[x + a, where, lane_tile(y + b, count)])
            start += rows
    return parts[0] if len(parts) == 1 else jnp.concatenate(parts, axis=0)


def conv(weight, buf, x, tiles, back=False):
    depth = buf.shape[1]
    fields = [(buf, 0, depth)]
    y, other = tiles
    if other == y + 1:
        window = taps(fields, x, y, 2, 0, 9 * depth, back)
    else:
        window = jnp.concatenate(
            [taps(fields, x, at, 1, 0, 9 * depth, back) for at in tiles], axis=1
        )
    return jnp.dot(weight[...], window, preferred_element_type=f32)


def inner_pairs(ny):
    return [(y, y + 1) for y in range(1, ny - 1, 2)]


def all_pairs(ny):
    return [(y, y + 1) for y in range(0, ny, 2)]


def ranges_of(nx):
    return [(1, 3) if x == 0 else (0, 2) if x == nx - 1 else (0, 3) for x in range(nx)]


def local_part(sums, weights, buf, nx, ny, first):
    for x, (low, high) in enumerate(ranges_of(nx)):
        for y in range(1, ny + 1, 2):
            lanes = lane_tile(y, 2)
            window = jnp.concatenate([buf[x + a, :, lanes] for a in range(low, high)], axis=0)
            term = jnp.dot(weights[low, high][...], window, preferred_element_type=f32)
            if first:
                sums[x, :, lanes] = term
            else:
                sums[x, :, lanes] += term


def border_sides(sums, weights, buf, nx, ny, first):
    sides = (lane_tile(0), lane_tile(ny + 1))
    for x in range(nx):
        window = jnp.concatenate(
            [jnp.concatenate([buf[x + a, :, s] for s in sides], axis=1) for a in range(3)], axis=0
        )
        term = jnp.dot(weights[0, 3][...], window, preferred_element_type=f32)
        for at, lanes in enumerate(sides):
            part = term[:, at * LANES : (at + 1) * LANES]
            if first:
                sums[x, :, lanes] = part
            else:
                sums[x, :, lanes] += part


def border_rows(sums, weights, buf, nx, ny):
    for x, a in ((0, 0), (nx - 1, 2)):
        for y in range(1, ny + 1, 2):
            lanes = lane_tile(y, 2)
            sums[x, :, lanes] += jnp.dot(
                weights[a, a + 1][...], buf[x + a, :, lanes], preferred_element_type=f32
            )


def weight_grad(total, grads, fields, size_x, count):
    width = 9 * sum(rows for _, _, rows in fields)
    for low in range(0, width, 256):
        high = min(low + 256, width)
        acc = None
        for x in range(size_x):
            term = lax.dot_general(
                grads(x),
                taps(fields, x, 0, count, low, high),
                (((1,), (1,)), ((), ())),
                preferred_element_type=f32,
            )
            acc = term if acc is None else acc + term
        total[:, low:high] = acc
    rest = total.shape[1] - width
    total[:, width:] = jnp.zeros((total.shape[0], rest), f32)


def laid_lanes(w, order):
    return jnp.concatenate([w[t] for t in order], axis=1)


def forward_weights(dest, w):
    for low in range(0, 27, 4):
        high = min(low + 4, 27)
        dest[:, low * 32 : high * 32] = laid_lanes(w, range(low, high))


def window_weights(dests, w, first, last):
    for (low, high), dest in dests.items():
        for b in range(3):
            parts = [
                w[(a * 3 + b) * 3 + c, :, first:last] for a in range(low, high) for c in range(3)
            ]
            dest[b * 32 : (b + 1) * 32, :] = jnp.concatenate(parts, axis=1)


def turned_weights(dest, w):
    count, outs, ins = w.shape
    flat = w[...].astype(f32).reshape(count * outs, ins)
    dest[...] = flat.T.astype(bf16)


def kernel(
    sizes,
    feat_hbm,
    labels_hbm,
    w_enc_hbm,
    w_mid_hbm,
    w_dec_hbm,
    w_out_hbm,
    feature_grad_hbm,
    sum_dec,
    sum_mid,
    sum_enc,
    feat,
    labels,
    w_enc,
    w_mid,
    w_dec,
    w_out,
    load_sem,
    feature_grad,
    store_sem,
    w_enc_f,
    w_enc_b,
    w_mid_f,
    w_mid_b,
    w_skip_03,
    w_skip_13,
    w_skip_02,
    w_skip_01,
    w_skip_23,
    w_up_03,
    w_up_13,
    w_up_02,
    w_up_01,
    w_up_23,
    w_dec_b,
    rows32,
    window_sums,
    F,
    PO,
    PP,
    UP,
    JU,
    JE,
    D,
    MG,
    MGP,
    EG,
    enc_slope,
    mid_slope,
    joined_grad,
    out_total,
    total_dec,
    total_mid,
    total_enc,
    part_dec,
    part_mid,
    part_enc,
    rs_dec,
    rs_mid,
    rs_enc,
    ar_dec,
    ar_mid,
    ar_enc,
    ag_dec,
    ag_mid,
    ag_enc,
    halo_send,
    halo_recv,
    rs_send,
    rs_recv,
    ar_send,
    ar_recv,
    ag_send,
    ag_recv,
):
    nb, nsx, nsy, nx, ny = sizes
    cx, cy = nx // 2, ny // 2
    half = nsy // 2
    near, far = nb * half, nsx * 2
    bt, sx, sy = lax.axis_index("batch"), lax.axis_index("sx"), lax.axis_index("sy")
    here, there = bt * half + lax.rem(sy, half), sx * 2 + sy // half
    skip_weights = {
        (0, 3): w_skip_03,
        (1, 3): w_skip_13,
        (0, 2): w_skip_02,
        (0, 1): w_skip_01,
        (2, 3): w_skip_23,
    }
    up_weights = {
        (0, 3): w_up_03,
        (1, 3): w_up_13,
        (0, 2): w_up_02,
        (0, 1): w_up_01,
        (2, 3): w_up_23,
    }

    loads = {
        name: pltpu.make_async_copy(source, dest, load_sem.at[at])
        for at, (name, source, dest) in enumerate(
            (
                ("feat", feat_hbm, feat),
                ("w_enc", w_enc_hbm, w_enc),
                ("w_mid", w_mid_hbm, w_mid),
                ("w_dec", w_dec_hbm, w_dec),
                ("w_out", w_out_hbm, w_out),
                ("labels", labels_hbm, labels),
            )
        )
    }
    for load in loads.values():
        load.start()

    clear_halo(F, nx, ny, 32, 64)
    clear_halo(PP, cx, cy, 0, 16)
    clear_halo(JE, nx, ny, 32, 64)
    clear_halo(UP, cx, cy, 0, 32)
    clear_halo(D, nx, ny, 32, 64)
    clear_halo(MGP, cx, cy, 0, 32)
    clear_halo(EG, nx, ny, 32, 64)

    def near_peer(k):
        return lax.rem(here + k, near)

    def near_id(p):
        return (p // half, sx, (sy // half) * half + lax.rem(p, half))

    def far_peer(k):
        return lax.rem(there + k, far)

    def far_id(q):
        return (bt, q // 2, lax.rem(q, 2) * half + lax.rem(sy, half))

    barrier = pltpu.get_barrier_semaphore()
    for dx, dy in DIRS:
        pl.semaphore_signal(
            barrier,
            inc=1,
            device_id=(bt, lax.rem(sx + dx + nsx, nsx), lax.rem(sy + dy + nsy, nsy)),
            device_id_type=MESH,
        )
    for k in range(1, far):
        pl.semaphore_signal(barrier, inc=1, device_id=far_id(far_peer(k)), device_id_type=MESH)
    for k in range(1, near):
        pl.semaphore_signal(barrier, inc=1, device_id=near_id(near_peer(k)), device_id_type=MESH)

    loads["feat"].wait()

    def load_features(x, carry):
        rows32[x] = feat[:, x].astype(f32).reshape(32 * ny, LANES)
        for y in range(ny):
            put_stack(F, x + 1, y + 1, rows32[x, pl.ds(y, 32, stride=ny), :], 32, 0, 1)
        return carry

    each(0, nx, load_features, 0)

    pl.semaphore_wait(barrier, near - 1 + far - 1 + 8)

    fields = {
        FEAT: (F, nx, ny, 32, 64),
        POOL: (PP, cx, cy, 0, 16),
        SKIP: (JE, nx, ny, 32, 64),
        MID: (UP, cx, cy, 0, 32),
        DECG: (D, nx, ny, 32, 64),
        MIDG: (MGP, cx, cy, 0, 32),
        ENCG: (EG, nx, ny, 32, 64),
    }

    def halo_copy(field, index):
        buf, sizex, sizey, low, high = fields[field]
        dx, dy = DIRS[index]

        def source(step, size):
            return {-1: (1, 1), 0: (1, size), 1: (size, 1)}[step]

        def target(step, size):
            return {-1: (size + 1, 1), 0: (1, size), 1: (0, 1)}[step]

        (x0, xn), (y0, yn) = source(dx, sizex), source(dy, sizey)
        (tx0, _), (ty0, _) = target(dx, sizex), target(dy, sizey)
        return pltpu.make_async_remote_copy(
            src_ref=buf.at[pl.ds(x0, xn), low:high, lane_tile(y0, yn)],
            dst_ref=buf.at[pl.ds(tx0, xn), low:high, lane_tile(ty0, yn)],
            send_sem=halo_send.at[field, index],
            recv_sem=halo_recv.at[field, index],
            device_id=(bt, lax.rem(sx + dx + nsx, nsx), lax.rem(sy + dy + nsy, nsy)),
            device_id_type=MESH,
        )

    def inside(dx, dy):
        ok = None
        for step, at, size in ((dx, sx, nsx), (dy, sy, nsy)):
            if step:
                this = at > 0 if step < 0 else at < size - 1
                ok = this if ok is None else jnp.logical_and(ok, this)
        return ok

    def start_halo(field):
        for index, (dx, dy) in enumerate(DIRS):

            @pl.when(inside(dx, dy))
            def _():
                halo_copy(field, index).start()

    def wait_halo(field, part=None):
        for index, (dx, dy) in enumerate(DIRS):
            if part is not None and part != (dy == 0):
                continue

            @pl.when(inside(-dx, -dy))
            def _():
                halo_copy(field, index).wait_recv()

    def wait_halo_sent(field):
        for index, (dx, dy) in enumerate(DIRS):

            @pl.when(inside(dx, dy))
            def _():
                halo_copy(field, index).wait_send()

    cut_dec = [(0, 96, 128 * j, 128) for j in range(8)]
    cut_mid = [(0, 64, 128 * j, 128) for j in range(8)]
    cut_enc = [(48 * (j % 2), 48, 128 * (j // 2), 128) for j in range(6)] + [None] * 2
    sums = {
        DEC: (total_dec, part_dec, rs_dec, ar_dec, ag_dec, cut_dec),
        MIDW: (total_mid, part_mid, rs_mid, ar_mid, ag_mid, cut_mid),
        ENC: (total_enc, part_enc, rs_enc, ar_enc, ag_enc, cut_enc),
    }

    def rs_copy(g, k):
        _, part, landing, _, _, _ = sums[g]
        return pltpu.make_async_remote_copy(
            src_ref=part.at[near_peer(k)],
            dst_ref=landing.at[here],
            send_sem=rs_send.at[g],
            recv_sem=rs_recv.at[g],
            device_id=near_id(near_peer(k)),
            device_id_type=MESH,
        )

    def ar_copy(g, k):
        landing = sums[g][3]
        return pltpu.make_async_remote_copy(
            src_ref=landing.at[there],
            dst_ref=landing.at[there],
            send_sem=ar_send.at[g],
            recv_sem=ar_recv.at[g],
            device_id=far_id(far_peer(k)),
            device_id_type=MESH,
        )

    def ag_copy(g, k):
        landing = sums[g][4]
        return pltpu.make_async_remote_copy(
            src_ref=landing.at[here],
            dst_ref=landing.at[here],
            send_sem=ag_send.at[g],
            recv_sem=ag_recv.at[g],
            device_id=near_id(near_peer(k)),
            device_id_type=MESH,
        )

    def wait_bytes(sem, pieces):
        pltpu.make_async_copy(pieces, pieces, sem).wait()

    def start_scatter(g):
        total, part, _, _, _, cut = sums[g]
        for j in range(near):
            if cut[j] is None:
                part[j] = jnp.zeros(part.shape[1:], bf16)
            else:
                row, rows, lane, lanes = cut[j]
                part[j] = total[row : row + rows, lane : lane + lanes].astype(bf16)
        for k in range(1, near):
            rs_copy(g, k).start()

    def start_exchange(g):
        _, part, landing, mine, _, _ = sums[g]
        wait_bytes(rs_recv.at[g], landing.at[pl.ds(0, near - 1)])
        acc = part[here].astype(f32)
        for k in range(1, near):
            acc = acc + landing[near_peer(k)].astype(f32)
        mine[there] = acc.astype(bf16)
        for k in range(1, far):
            ar_copy(g, k).start()

    def start_gather(g):
        _, _, _, landing, result, _ = sums[g]
        wait_bytes(ar_recv.at[g], landing.at[pl.ds(0, far - 1)])
        acc = landing[0].astype(f32)
        for q in range(1, far):
            acc = acc + landing[q].astype(f32)
        result[here] = acc.astype(bf16)
        for k in range(1, near):
            ag_copy(g, k).start()

    def wait_gather(g):
        wait_bytes(ag_recv.at[g], sums[g][4].at[pl.ds(0, near - 1)])

    def wait_scatter_sent(g):
        wait_bytes(rs_send.at[g], sums[g][1].at[pl.ds(0, near - 1)])

    def wait_exchange_sent(g):
        wait_bytes(ar_send.at[g], sums[g][3].at[pl.ds(0, far - 1)])

    def wait_gather_sent(g):
        wait_bytes(ag_send.at[g], sums[g][4].at[pl.ds(0, near - 1)])

    start_halo(FEAT)
    for name in ("w_enc", "w_mid", "w_dec", "w_out", "labels"):
        loads[name].wait()
    forward_weights(w_enc_f, w_enc)

    def enc_tiles(x, tiles):
        pre = conv(w_enc_f, F, x, tiles)
        s = sigmoid(pre)
        slope = s * (1.0 + pre * (1.0 - s))
        act = (pre * s).astype(bf16).astype(f32)
        for at, y in enumerate(tiles):
            lanes = slice(at * LANES, (at + 1) * LANES)
            enc_slope[x, :, lane_tile(y)] = slope[:, lanes]
            JE[x + 1, 32:64, lane_tile(y + 1)] = act[:, lanes].astype(bf16)

    def enc_inner(x, carry):
        for tiles in inner_pairs(ny):
            enc_tiles(x, tiles)
        return carry

    each(1, nx - 1, enc_inner, 0)
    turned_weights(w_mid_f, w_mid)
    window_weights(skip_weights, w_dec, 64, 96)
    window_weights(up_weights, w_dec, 0, 64)
    out_total[...] = jnp.zeros(out_total.shape, f32)
    wait_halo(FEAT, False)
    finish_halo(F, nx, ny, 32, 32, 0, 1, part=False)
    for x in range(1, nx - 1):
        enc_tiles(x, (0, ny - 1))
    wait_halo(FEAT, True)
    finish_halo(F, nx, ny, 32, 32, 0, 1, part=True)
    for x in (0, nx - 1):
        for tiles in all_pairs(ny):
            enc_tiles(x, tiles)

    def pool_block(bx, carry):
        for by in range(cy):
            block = jnp.zeros((32, LANES), f32)
            for dx in range(2):
                for dy in range(2):
                    block += JE[2 * bx + dx + 1, 32:64, lane_tile(2 * by + dy + 1)].astype(f32)
            pooled = (pair_sum(block) * 0.125).astype(bf16).astype(f32)
            PP[bx + 1, :, lane_tile(by + 1)] = packed(pooled)
            PO[bx + 1, 32:64, lane_tile(by + 1)] = pooled.astype(bf16)
        return carry

    each(0, cx, pool_block, 0)
    start_halo(POOL)
    start_halo(SKIP)
    finish_inner(PO, cx, cy, 32, 2)
    finish_inner(JE, nx, ny, 32, 1)
    local_part(window_sums, skip_weights, JE, nx, ny, True)
    turned_weights(w_enc_b, w_enc)
    turned_weights(w_dec_b, w_dec)
    for low in range(0, 27, 2):
        high = min(low + 2, 27)
        w_mid_b[:, low * 64 : high * 64] = laid_lanes(w_mid, range(low, high))
    wait_halo(POOL)
    unpack_halo(PO, PP, cx, cy, 32)

    def mid_block(bx, carry):
        for by in range(0, cy, 2):
            pre = conv(w_mid_f, PO, bx, (by, by + 1))
            s = sigmoid(pre)
            mid_slope[bx, :, lane_tile(by, 2)] = s * (1.0 + pre * (1.0 - s))
            act = (pre * s).astype(bf16)
            for dy in range(2):
                tile = act[:, dy * LANES : (dy + 1) * LANES]
                UP[bx + 1, :, lane_tile(by + dy + 1)] = packed(tile.astype(f32))
                JU[2 * bx + 1, 64:128, lane_tile(2 * (by + dy) + 1)] = tile
        return carry

    each(0, cx, mid_block, 0)
    start_halo(MID)

    def spread(bx, by, tile):
        before, after = shifted(tile, 1)
        tile = tile.astype(bf16)
        for x in (2 * bx - 1, 2 * bx):
            for y in (2 * by - 1, 2 * by):
                if 0 <= x <= nx + 1 and 0 <= y <= ny + 1:
                    lanes = lane_tile(y)
                    JU[x, 0:64, lanes] = before
                    JU[x, 64:128, lanes] = tile
                    JU[x, 128:192, lanes] = after

    for bx in range(1, cx + 1):
        for by in range(1, cy + 1):
            spread(bx, by, JU[2 * bx - 1, 64:128, lane_tile(2 * by - 1)].astype(f32))
    local_part(window_sums, up_weights, JU, nx, ny, False)
    wait_halo(SKIP)
    finish_halo(JE, nx, ny, 32, 32, 0, 1)
    border_sides(window_sums, skip_weights, JE, nx, ny, True)
    border_rows(window_sums, skip_weights, JE, nx, ny)
    for part in (False, True):
        wait_halo(MID, part)
        over_halo(cx, cy, lambda bx, by: spread(bx, by, unpacked(UP[bx, :, lane_tile(by)])), part)
        if part:
            border_rows(window_sums, up_weights, JU, nx, ny)
        else:
            border_sides(window_sums, up_weights, JU, nx, ny, False)

    def dec_row(x, carry):
        pre = (
            window_sums[x, 0:32, lane_tile(0, ny)]
            + window_sums[x, 32:64, lane_tile(1, ny)]
            + window_sums[x, 64:96, lane_tile(2, ny)]
        )
        s = sigmoid(pre)
        slope = s * (1.0 + pre * (1.0 - s))
        act = (pre * s).astype(bf16)
        logits = jnp.dot(w_out[...], act, preferred_element_type=f32)
        expo = jnp.exp(logits)
        prob = expo / jnp.sum(expo, axis=0, keepdims=True)
        ids = lax.broadcasted_iota(jnp.int32, prob.shape, 0)
        these = jnp.concatenate([labels[x, y : y + 1, :] for y in range(ny)], axis=1)
        onehot = (these == ids).astype(f32)
        logit_grad = (loss_scale * (prob - onehot)).astype(bf16)
        out_total[...] += lax.dot_general(
            logit_grad, act, (((1,), (1,)), ((), ())), preferred_element_type=f32
        )
        act_grad = lax.dot_general(
            w_out[...], logit_grad, (((0,), (0,)), ((), ())), preferred_element_type=f32
        )
        grads = (act_grad * slope).astype(bf16).astype(f32)
        for y in range(ny):
            tile = grads[:, y * LANES : (y + 1) * LANES]
            D[x + 1, 32:64, lane_tile(y + 1)] = tile.astype(bf16)
        return carry

    each(0, nx, dec_row, 0)
    start_halo(DECG)
    finish_inner(D, nx, ny, 32, 1, back=True)

    def dec_back(x, tiles):
        grads = conv(w_dec_b, D, x, tiles, back=True)
        for at, y in enumerate(tiles):
            joined_grad[x, :, lane_tile(y)] = grads[:, at * LANES : (at + 1) * LANES]

    def dec_back_inner(x, carry):
        for tiles in inner_pairs(ny):
            dec_back(x, tiles)
        return carry

    each(1, nx - 1, dec_back_inner, 0)
    joined = [(JU, 64, 64), (JE, 32, 32)]
    weight_grad(total_dec, lambda x: D[x + 1, :, lane_tile(1, ny)], joined, nx, ny)
    total_dec[0:4, 864:896] = out_total[...]
    start_scatter(DEC)

    wait_halo(DECG, False)
    finish_halo(D, nx, ny, 32, 32, 0, 1, back=True, part=False)
    for x in range(1, nx - 1):
        dec_back(x, (0, ny - 1))
    wait_halo(DECG, True)
    finish_halo(D, nx, ny, 32, 32, 0, 1, back=True, part=True)
    for x in (0, nx - 1):
        for tiles in all_pairs(ny):
            dec_back(x, tiles)

    def mid_grads(bx, carry):
        for by in range(cy):
            block = jnp.zeros((64, LANES), f32)
            for dx in range(2):
                for dy in range(2):
                    block += joined_grad[2 * bx + dx, 0:64, lane_tile(2 * by + dy)]
            grads = pair_sum(block) * mid_slope[bx, :, lane_tile(by)]
            grads = grads.astype(bf16).astype(f32)
            MGP[bx + 1, :, lane_tile(by + 1)] = packed(grads)
            MG[bx + 1, 64:128, lane_tile(by + 1)] = grads.astype(bf16)
        return carry

    each(0, cx, mid_grads, 0)
    start_halo(MIDG)
    finish_inner(MG, cx, cy, 64, 2, back=True)

    weight_grad(total_mid, lambda x: MG[x + 1, 64:128, lane_tile(1, cy)], [(PO, 0, 96)], cx, cy)
    start_scatter(MIDW)
    start_exchange(DEC)

    wait_halo(MIDG)
    start_exchange(MIDW)
    unpack_halo(MG, MGP, cx, cy, 64, back=True)

    def mid_back(bx, carry):
        for by in range(0, cy, 2):
            pooled = conv(w_mid_b, MG, bx, (by, by + 1), back=True) * 0.125
            for dx in range(2):
                x = 2 * bx + dx
                for dy in range(4):
                    y = 2 * by + dy
                    up = pooled[:, (dy // 2) * LANES : (dy // 2 + 1) * LANES]
                    tile = (joined_grad[x, 64:96, lane_tile(y)] + up) * enc_slope[x, :, lane_tile(y)]
                    put_stack(EG, x + 1, y + 1, tile, 32, 0, 1, back=True)
        return carry

    each(0, cx, mid_back, 0)
    start_halo(ENCG)

    weight_grad(total_enc, lambda x: EG[x + 1, :, lane_tile(1, ny)], [(F, 32, 32)], nx, ny)
    start_scatter(ENC)

    def enc_back(x, tiles):
        grads = conv(w_enc_b, EG, x, tiles, back=True)
        for at, y in enumerate(tiles):
            rows32[x, pl.ds(y, 32, stride=ny), :] = grads[:, at * LANES : (at + 1) * LANES]

    def enc_back_inner(x, carry):
        for tiles in inner_pairs(ny):
            enc_back(x, tiles)
        return carry

    each(1, nx - 1, enc_back_inner, 0)
    start_exchange(ENC)
    wait_halo(ENCG)
    finish_halo(EG, nx, ny, 32, 32, 0, 1, back=True)

    def enc_back_sides(x, carry):
        enc_back(x, (0, ny - 1))
        return carry

    each(1, nx - 1, enc_back_sides, 0)

    def enc_back_ends(i, carry):
        for tiles in all_pairs(ny):
            enc_back(i * (nx - 1), tiles)
        return carry

    each(0, 2, enc_back_ends, 0)

    def lay_out(x, carry):
        feature_grad[:, x] = rows32[x].reshape(32, ny, LANES).astype(bf16)
        return carry

    each(0, nx, lay_out, 0)
    stores = [
        pltpu.make_async_copy(source, dest, store_sem.at[at])
        for at, (source, dest) in enumerate(
            (
                (feature_grad, feature_grad_hbm),
                (ag_dec, sum_dec),
                (ag_mid, sum_mid),
                (ag_enc, sum_enc),
            )
        )
    ]
    stores[0].start()
    start_gather(DEC)
    start_gather(MIDW)
    for field in range(7):
        wait_halo_sent(field)
    for g in (DEC, MIDW, ENC):
        wait_scatter_sent(g)
    start_gather(ENC)
    wait_gather(DEC)
    stores[1].start()
    wait_gather(MIDW)
    stores[2].start()
    for g in (DEC, MIDW, ENC):
        wait_exchange_sent(g)
    for g in (DEC, MIDW):
        wait_gather_sent(g)
    wait_gather(ENC)
    stores[3].start()
    wait_gather_sent(ENC)
    for store in stores:
        store.wait()


def outputs(
    scale,
    features_in,
    dec_in,
    mid_in,
    enc_in,
    features_out,
    enc_out,
    mid_out,
    dec_out,
    out_out,
    features,
    sum_dec,
    sum_mid,
    sum_enc,
    grad_enc,
    grad_mid,
    grad_dec,
    grad_out,
    sems,
):
    copies = [
        pltpu.make_async_copy(source, dest, sems.at[at])
        for at, (source, dest) in enumerate(
            (
                (dec_in, sum_dec),
                (mid_in, sum_mid),
                (enc_in, sum_enc),
                (features_in, features),
                (grad_dec, dec_out),
                (grad_out, out_out),
                (grad_mid, mid_out),
                (grad_enc, enc_out),
                (features, features_out),
            )
        )
    ]
    for copy in copies[:4]:
        copy.start()
    copies[0].wait()
    whole = jnp.concatenate([sum_dec[j].astype(f32) for j in range(8)], axis=1) * scale
    for t in range(27):
        window, c = divmod(t, 3)
        grad_dec[t] = whole[c * 32 : (c + 1) * 32, window * 96 : (window + 1) * 96]
    grad_out[...] = whole[0:4, 864:896]
    copies[4].start()
    copies[5].start()
    copies[3].wait()
    copies[8].start()
    copies[1].wait()
    for j in range(7):
        turned = (sum_mid[j].astype(f32) * (0.5 * scale)).T
        for t in range(4 * j, min(4 * j + 4, 27)):
            grad_mid[t] = turned[(t % 4) * 32 : (t % 4 + 1) * 32]
    copies[6].start()
    copies[2].wait()
    for window in range(9):
        j, at = divmod(window, 4)
        both = jnp.concatenate([sum_enc[2 * j], sum_enc[2 * j + 1]], axis=0)
        part = both[:, at * 32 : (at + 1) * 32].astype(f32) * scale
        for c in range(3):
            grad_enc[window * 3 + c] = part[c * 32 : (c + 1) * 32]
    copies[7].start()
    for copy in copies[4:]:
        copy.wait()


def shards(features, labels, w_enc, w_mid, w_dec, w_out):
    nb, nsx, nsy = lax.axis_size("batch"), lax.axis_size("sx"), lax.axis_size("sy")
    _, chans, nx, ny, nz = features.shape
    cx, cy = nx // 2, ny // 2
    scale = 1.0 / float(nb * nsx * nsy * nx * ny * nz)
    near, far = nb * (nsy // 2), nsx * 2

    def fine(depth):
        return pltpu.VMEM((nx + 2, depth, (ny + 2) * LANES), bf16)

    def coarse(depth):
        return pltpu.VMEM((cx + 2, depth, (cy + 2) * LANES), bf16)

    pieces = ((96, 128), (64, 128), (48, 128))
    scratch = [
        pltpu.VMEM((chans, nx, ny, nz), bf16),
        pltpu.VMEM((nx, ny, nz), jnp.int32),
        pltpu.VMEM((27, 32, 32), bf16),
        pltpu.VMEM((27, 32, 64), bf16),
        pltpu.VMEM((27, 32, 96), bf16),
        pltpu.VMEM((4, 32), bf16),
        pltpu.SemaphoreType.DMA((6,)),
        pltpu.VMEM((chans, nx, ny, nz), bf16),
        pltpu.SemaphoreType.DMA((4,)),
        pltpu.VMEM((32, 864), bf16),
        pltpu.VMEM((32, 864), bf16),
        pltpu.VMEM((64, 864), bf16),
        pltpu.VMEM((32, 1728), bf16),
        *[pltpu.VMEM((96, 96 * count), bf16) for count in (3, 2, 2, 1, 1)],
        *[pltpu.VMEM((96, 192 * count), bf16) for count in (3, 2, 2, 1, 1)],
        pltpu.VMEM((96, 864), bf16),
        pltpu.VMEM((nx, 32 * ny, LANES), f32),
        pltpu.VMEM((nx, 96, (ny + 2) * LANES), f32),
        fine(96),
        coarse(96),
        coarse(16),
        coarse(32),
        fine(192),
        fine(96),
        fine(96),
        coarse(192),
        coarse(32),
        fine(96),
        pltpu.VMEM((nx, 32, ny * LANES), f32),
        pltpu.VMEM((cx, 64, cy * LANES), f32),
        pltpu.VMEM((nx, 96, ny * LANES), f32),
        pltpu.VMEM((4, 32), f32),
        pltpu.VMEM((96, 1024), f32),
        pltpu.VMEM((64, 1024), f32),
        pltpu.VMEM((96, 384), f32),
    ]
    scratch += [pltpu.VMEM((near, rows, length), bf16) for rows, length in pieces]
    scratch += [pltpu.VMEM((near, rows, length), bf16) for rows, length in pieces]
    scratch += [pltpu.VMEM((far, rows, length), bf16) for rows, length in pieces]
    scratch += [pltpu.VMEM((near, rows, length), bf16) for rows, length in pieces]
    scratch += [pltpu.SemaphoreType.DMA((7, 8))] * 2
    scratch += [pltpu.SemaphoreType.DMA((3,))] * 2
    scratch += [pltpu.SemaphoreType.DMA((3,))] * 2
    scratch += [pltpu.SemaphoreType.DMA((3,))] * 2

    vmem = pl.BlockSpec(memory_space=pltpu.VMEM)
    partial_outputs = pl.pallas_call(
        functools.partial(kernel, (nb, nsx, nsy, nx, ny)),
        out_shape=(
            jax.ShapeDtypeStruct((chans, nx, ny, nz), bf16),
            *[jax.ShapeDtypeStruct((near, rows, length), bf16) for rows, length in pieces],
        ),
        in_specs=[pl.BlockSpec(memory_space=pl.ANY)] * 6,
        out_specs=[pl.BlockSpec(memory_space=pl.ANY)] * 4,
        scratch_shapes=scratch,
        compiler_params=pltpu.CompilerParams(
            collective_id=0, has_side_effects=True, vmem_limit_bytes=62 * 1024 * 1024
        ),
        name="unet_step",
    )(
        features[0],
        labels[0],
        w_enc.reshape(27, 32, 32),
        w_mid.swapaxes(3, 4).reshape(27, 32, 64),
        w_dec.reshape(27, 32, 96),
        w_out,
    )
    feature_grad, grad_enc, grad_mid, grad_dec, grad_out = pl.pallas_call(
        functools.partial(outputs, scale),
        out_shape=(
            jax.ShapeDtypeStruct((chans, nx, ny, nz), bf16),
            jax.ShapeDtypeStruct((27, 32, 32), f32),
            jax.ShapeDtypeStruct((27, 32, 64), f32),
            jax.ShapeDtypeStruct((27, 32, 96), f32),
            jax.ShapeDtypeStruct((4, 32), f32),
        ),
        in_specs=[pl.BlockSpec(memory_space=pl.ANY)] * 4,
        out_specs=[pl.BlockSpec(memory_space=pl.ANY)] * 5,
        scratch_shapes=[
            pltpu.VMEM((chans, nx, ny, nz), bf16),
            *[pltpu.VMEM((near, rows, length), bf16) for rows, length in pieces],
            pltpu.VMEM((27, 32, 32), f32),
            pltpu.VMEM((27, 32, 64), f32),
            pltpu.VMEM((27, 32, 96), f32),
            pltpu.VMEM((4, 32), f32),
            pltpu.SemaphoreType.DMA((9,)),
        ],
        compiler_params=pltpu.CompilerParams(vmem_limit_bytes=62 * 1024 * 1024),
        name="unet_outputs",
    )(*partial_outputs)
    return (
        feature_grad[None],
        grad_enc.reshape(w_enc.shape),
        grad_mid.reshape(3, 3, 3, 32, 64).swapaxes(3, 4),
        grad_dec.reshape(w_dec.shape),
        grad_out,
    )


def solution(mesh):
    placed = (P("batch", None, "sx", "sy", None), P("batch", "sx", "sy", None), P(), P(), P(), P())
    return jax.shard_map(
        shards,
        mesh=mesh,
        in_specs=placed,
        out_specs=(P("batch", None, "sx", "sy", None), P(), P(), P(), P()),
        check_vma=False,
    )
```

```python
import functools

import jax
import jax.numpy as jnp
from jax import lax
from jax.experimental import pallas as pl
from jax.experimental.pallas import tpu as pltpu
from jax.sharding import PartitionSpec as P

loss_scale = 32.0
LANES = 128
MESH = pl.DeviceIdType.MESH
f32 = jnp.float32
bf16 = jnp.bfloat16

DIRS = [(0, -1), (0, 1), (-1, -1), (-1, 1), (1, -1), (1, 1), (-1, 0), (1, 0)]
FEAT, POOL, SKIP, MID, DECG, MIDG, ENCG = range(7)
DEC, MIDW, ENC = range(3)


def lane_tile(y, count=1):
    if isinstance(y, int):
        return pl.ds(y * LANES, count * LANES)
    return pl.ds(pl.multiple_of(y * LANES, LANES), count * LANES)


def sigmoid(u):
    return 1.0 / (1.0 + jnp.exp(-u))


def shifted(tile, shift):
    lane = lax.broadcasted_iota(jnp.int32, tile.shape, 1)
    before = jnp.where(lane >= shift, pltpu.roll(tile, shift, axis=1), 0.0)
    after = jnp.where(lane < LANES - shift, pltpu.roll(tile, LANES - shift, axis=1), 0.0)
    return before.astype(bf16), after.astype(bf16)


def pair_sum(tile):
    lane = lax.broadcasted_iota(jnp.int32, tile.shape, 1)
    other = jnp.where(
        lane % 2 == 0, pltpu.roll(tile, LANES - 1, axis=1), pltpu.roll(tile, 1, axis=1)
    )
    return tile + other


def packed(tile):
    half = tile.shape[0] // 2
    lane = lax.broadcasted_iota(jnp.int32, (half, LANES), 1)
    return jnp.where(lane % 2 == 0, tile[:half], tile[half:]).astype(bf16)


def unpacked(tile):
    tile = tile.astype(f32)
    lane = lax.broadcasted_iota(jnp.int32, tile.shape, 1)
    first = jnp.where(lane % 2 == 0, tile, pltpu.roll(tile, 1, axis=1))
    second = jnp.where(lane % 2 == 1, tile, pltpu.roll(tile, LANES - 1, axis=1))
    return jnp.concatenate([first, second], axis=0)


def put_sides(buf, x, y, tile, period, offset, shift, back):
    chans = tile.shape[0]
    before, after = shifted(tile, shift)
    lanes = lane_tile(y)
    buf[x, offset : offset + chans, lanes] = after if back else before
    buf[x, 2 * period + offset : 2 * period + offset + chans, lanes] = before if back else after


def put_stack(buf, x, y, tile, period, offset, shift, back=False):
    chans = tile.shape[0]
    buf[x, period + offset : period + offset + chans, lane_tile(y)] = tile.astype(bf16)
    put_sides(buf, x, y, tile, period, offset, shift, back)


def each(first, last, step, carry):
    for at in range(first, last):
        step(at, carry)


def over_halo(nx, ny, step, part=None):
    for x in range(nx + 2):
        for y in range(ny + 2):
            side = y in (0, ny + 1)
            if (x in (0, nx + 1) or side) and (part is None or part != side):
                step(x, y)


def finish_halo(buf, nx, ny, chans, period, offset, shift, back=False, part=None):
    def step(x, y):
        tile = buf[x, period + offset : period + offset + chans, lane_tile(y)].astype(f32)
        put_sides(buf, x, y, tile, period, offset, shift, back)

    over_halo(nx, ny, step, part)


def finish_inner(buf, nx, ny, chans, shift, back=False):
    for x in range(1, nx + 1):
        for y in range(1, ny + 1):
            tile = buf[x, chans : 2 * chans, lane_tile(y)].astype(f32)
            put_sides(buf, x, y, tile, chans, 0, shift, back)


def unpack_halo(buf, landed, nx, ny, chans, back=False):
    def step(x, y):
        put_stack(buf, x, y, unpacked(landed[x, :, lane_tile(y)]), chans, 0, 2, back)

    over_halo(nx, ny, step)


def clear_halo(buf, nx, ny, low, high):
    width = (ny + 2) * LANES
    buf[0, low:high, :] = jnp.zeros((high - low, width), bf16)
    buf[nx + 1, low:high, :] = jnp.zeros((high - low, width), bf16)
    for x in range(1, nx + 1):
        buf[x, low:high, lane_tile(0)] = jnp.zeros((high - low, LANES), bf16)
        buf[x, low:high, lane_tile(ny + 1)] = jnp.zeros((high - low, LANES), bf16)


def taps(fields, x, y, count, low, high, back=False):
    depth = sum(rows for _, _, rows in fields)
    parts = []
    for window in range(9):
        a, b = divmod(8 - window if back else window, 3)
        start = window * depth
        for buf, base, rows in fields:
            first, last = max(low, start), min(high, start + rows)
            if first < last:
                where = slice(base + first - start, base + last - start)
                parts.append(buf[x + a, where, lane_tile(y + b, count)])
            start += rows
    return parts[0] if len(parts) == 1 else jnp.concatenate(parts, axis=0)


def conv(weight, buf, x, tiles, back=False):
    depth = buf.shape[1]
    fields = [(buf, 0, depth)]
    y, other = tiles
    if other == y + 1:
        window = taps(fields, x, y, 2, 0, 9 * depth, back)
    else:
        window = jnp.concatenate(
            [taps(fields, x, at, 1, 0, 9 * depth, back) for at in tiles], axis=1
        )
    return jnp.dot(weight[...], window, preferred_element_type=f32)


def inner_pairs(ny):
    return [(y, y + 1) for y in range(1, ny - 1, 2)]


def all_pairs(ny):
    return [(y, y + 1) for y in range(0, ny, 2)]


def ranges_of(nx):
    return [(1, 3) if x == 0 else (0, 2) if x == nx - 1 else (0, 3) for x in range(nx)]


def local_part(sums, weights, buf, nx, ny, first):
    for x, (low, high) in enumerate(ranges_of(nx)):
        for y in range(1, ny + 1, 2):
            lanes = lane_tile(y, 2)
            window = jnp.concatenate([buf[x + a, :, lanes] for a in range(low, high)], axis=0)
            term = jnp.dot(weights[low, high][...], window, preferred_element_type=f32)
            if first:
                sums[x, :, lanes] = term
            else:
                sums[x, :, lanes] += term


def border_sides(sums, weights, buf, nx, ny, first):
    sides = (lane_tile(0), lane_tile(ny + 1))
    for x in range(nx):
        window = jnp.concatenate(
            [jnp.concatenate([buf[x + a, :, s] for s in sides], axis=1) for a in range(3)], axis=0
        )
        term = jnp.dot(weights[0, 3][...], window, preferred_element_type=f32)
        for at, lanes in enumerate(sides):
            part = term[:, at * LANES : (at + 1) * LANES]
            if first:
                sums[x, :, lanes] = part
            else:
                sums[x, :, lanes] += part


def border_rows(sums, weights, buf, nx, ny):
    for x, a in ((0, 0), (nx - 1, 2)):
        for y in range(1, ny + 1, 2):
            lanes = lane_tile(y, 2)
            sums[x, :, lanes] += jnp.dot(
                weights[a, a + 1][...], buf[x + a, :, lanes], preferred_element_type=f32
            )


def weight_grad(total, grads, fields, size_x, count):
    width = 9 * sum(rows for _, _, rows in fields)
    for low in range(0, width, 256):
        high = min(low + 256, width)
        acc = None
        for x in range(size_x):
            term = lax.dot_general(
                grads(x),
                taps(fields, x, 0, count, low, high),
                (((1,), (1,)), ((), ())),
                preferred_element_type=f32,
            )
            acc = term if acc is None else acc + term
        total[:, low:high] = acc
    rest = total.shape[1] - width
    total[:, width:] = jnp.zeros((total.shape[0], rest), f32)


def laid_lanes(w, order):
    return jnp.concatenate([w[t] for t in order], axis=1)


def forward_weights(dest, w):
    for low in range(0, 27, 4):
        high = min(low + 4, 27)
        dest[:, low * 32 : high * 32] = laid_lanes(w, range(low, high))


def window_weights(dests, w, first, last):
    for (low, high), dest in dests.items():
        for b in range(3):
            parts = [
                w[(a * 3 + b) * 3 + c, :, first:last] for a in range(low, high) for c in range(3)
            ]
            dest[b * 32 : (b + 1) * 32, :] = jnp.concatenate(parts, axis=1)


def turned_weights(dest, w):
    count, outs, ins = w.shape
    flat = w[...].astype(f32).reshape(count * outs, ins)
    dest[...] = flat.T.astype(bf16)


def kernel(
    sizes,
    feat_hbm,
    labels_hbm,
    w_enc_hbm,
    w_mid_hbm,
    w_dec_hbm,
    w_out_hbm,
    feature_grad_hbm,
    sum_dec,
    sum_mid,
    sum_enc,
    feat,
    labels,
    w_enc,
    w_mid,
    w_dec,
    w_out,
    load_sem,
    feature_grad,
    store_sem,
    w_enc_f,
    w_enc_b,
    w_mid_f,
    w_mid_b,
    w_skip_03,
    w_skip_13,
    w_skip_02,
    w_skip_01,
    w_skip_23,
    w_up_03,
    w_up_13,
    w_up_02,
    w_up_01,
    w_up_23,
    w_dec_b,
    rows32,
    window_sums,
    F,
    PO,
    PP,
    UP,
    JU,
    JE,
    D,
    MG,
    MGP,
    EG,
    enc_slope,
    mid_slope,
    joined_grad,
    out_total,
    total_dec,
    total_mid,
    total_enc,
    part_dec,
    part_mid,
    part_enc,
    rs_dec,
    rs_mid,
    rs_enc,
    ar_dec,
    ar_mid,
    ar_enc,
    ag_dec,
    ag_mid,
    ag_enc,
    halo_send,
    halo_recv,
    rs_send,
    rs_recv,
    ar_send,
    ar_recv,
    ag_send,
    ag_recv,
):
    nb, nsx, nsy, nx, ny = sizes
    cx, cy = nx // 2, ny // 2
    half = nsy // 2
    near, far = nb * half, nsx * 2
    bt, sx, sy = lax.axis_index("batch"), lax.axis_index("sx"), lax.axis_index("sy")
    here, there = bt * half + lax.rem(sy, half), sx * 2 + sy // half
    skip_weights = {
        (0, 3): w_skip_03,
        (1, 3): w_skip_13,
        (0, 2): w_skip_02,
        (0, 1): w_skip_01,
        (2, 3): w_skip_23,
    }
    up_weights = {
        (0, 3): w_up_03,
        (1, 3): w_up_13,
        (0, 2): w_up_02,
        (0, 1): w_up_01,
        (2, 3): w_up_23,
    }

    loads = {
        name: pltpu.make_async_copy(source, dest, load_sem.at[at])
        for at, (name, source, dest) in enumerate(
            (
                ("feat", feat_hbm, feat),
                ("w_enc", w_enc_hbm, w_enc),
                ("w_mid", w_mid_hbm, w_mid),
                ("w_dec", w_dec_hbm, w_dec),
                ("w_out", w_out_hbm, w_out),
                ("labels", labels_hbm, labels),
            )
        )
    }
    for load in loads.values():
        load.start()

    clear_halo(F, nx, ny, 32, 64)
    clear_halo(PP, cx, cy, 0, 16)
    clear_halo(JE, nx, ny, 32, 64)
    clear_halo(UP, cx, cy, 0, 32)
    clear_halo(D, nx, ny, 32, 64)
    clear_halo(MGP, cx, cy, 0, 32)
    clear_halo(EG, nx, ny, 32, 64)

    def near_peer(k):
        return lax.rem(here + k, near)

    def near_id(p):
        return (p // half, sx, (sy // half) * half + lax.rem(p, half))

    def far_peer(k):
        return lax.rem(there + k, far)

    def far_id(q):
        return (bt, q // 2, lax.rem(q, 2) * half + lax.rem(sy, half))

    barrier = pltpu.get_barrier_semaphore()
    for dx, dy in DIRS:
        pl.semaphore_signal(
            barrier,
            inc=1,
            device_id=(bt, lax.rem(sx + dx + nsx, nsx), lax.rem(sy + dy + nsy, nsy)),
            device_id_type=MESH,
        )
    for k in range(1, far):
        pl.semaphore_signal(barrier, inc=1, device_id=far_id(far_peer(k)), device_id_type=MESH)
    for k in range(1, near):
        pl.semaphore_signal(barrier, inc=1, device_id=near_id(near_peer(k)), device_id_type=MESH)

    loads["feat"].wait()

    def load_features(x, carry):
        rows32[x] = feat[:, x].astype(f32).reshape(32 * ny, LANES)
        for y in range(ny):
            put_stack(F, x + 1, y + 1, rows32[x, pl.ds(y, 32, stride=ny), :], 32, 0, 1)
        return carry

    each(0, nx, load_features, 0)

    pl.semaphore_wait(barrier, near - 1 + far - 1 + 8)

    fields = {
        FEAT: (F, nx, ny, 32, 64),
        POOL: (PP, cx, cy, 0, 16),
        SKIP: (JE, nx, ny, 32, 64),
        MID: (UP, cx, cy, 0, 32),
        DECG: (D, nx, ny, 32, 64),
        MIDG: (MGP, cx, cy, 0, 32),
        ENCG: (EG, nx, ny, 32, 64),
    }

    def halo_copy(field, index):
        buf, sizex, sizey, low, high = fields[field]
        dx, dy = DIRS[index]

        def source(step, size):
            return {-1: (1, 1), 0: (1, size), 1: (size, 1)}[step]

        def target(step, size):
            return {-1: (size + 1, 1), 0: (1, size), 1: (0, 1)}[step]

        (x0, xn), (y0, yn) = source(dx, sizex), source(dy, sizey)
        (tx0, _), (ty0, _) = target(dx, sizex), target(dy, sizey)
        return pltpu.make_async_remote_copy(
            src_ref=buf.at[pl.ds(x0, xn), low:high, lane_tile(y0, yn)],
            dst_ref=buf.at[pl.ds(tx0, xn), low:high, lane_tile(ty0, yn)],
            send_sem=halo_send.at[field, index],
            recv_sem=halo_recv.at[field, index],
            device_id=(bt, lax.rem(sx + dx + nsx, nsx), lax.rem(sy + dy + nsy, nsy)),
            device_id_type=MESH,
        )

    def inside(dx, dy):
        ok = None
        for step, at, size in ((dx, sx, nsx), (dy, sy, nsy)):
            if step:
                this = at > 0 if step < 0 else at < size - 1
                ok = this if ok is None else jnp.logical_and(ok, this)
        return ok

    def start_halo(field):
        for index, (dx, dy) in enumerate(DIRS):

            @pl.when(inside(dx, dy))
            def _():
                halo_copy(field, index).start()

    def wait_halo(field, part=None):
        for index, (dx, dy) in enumerate(DIRS):
            if part is not None and part != (dy == 0):
                continue

            @pl.when(inside(-dx, -dy))
            def _():
                halo_copy(field, index).wait_recv()

    def wait_halo_sent(field):
        for index, (dx, dy) in enumerate(DIRS):

            @pl.when(inside(dx, dy))
            def _():
                halo_copy(field, index).wait_send()

    cut_dec = [(0, 96, 128 * j, 128) for j in range(8)]
    cut_mid = [(0, 64, 128 * j, 128) for j in range(8)]
    cut_enc = [(48 * (j % 2), 48, 128 * (j // 2), 128) for j in range(6)] + [None] * 2
    sums = {
        DEC: (total_dec, part_dec, rs_dec, ar_dec, ag_dec, cut_dec),
        MIDW: (total_mid, part_mid, rs_mid, ar_mid, ag_mid, cut_mid),
        ENC: (total_enc, part_enc, rs_enc, ar_enc, ag_enc, cut_enc),
    }

    def rs_copy(g, k):
        _, part, landing, _, _, _ = sums[g]
        return pltpu.make_async_remote_copy(
            src_ref=part.at[near_peer(k)],
            dst_ref=landing.at[here],
            send_sem=rs_send.at[g],
            recv_sem=rs_recv.at[g],
            device_id=near_id(near_peer(k)),
            device_id_type=MESH,
        )

    def ar_copy(g, k):
        landing = sums[g][3]
        return pltpu.make_async_remote_copy(
            src_ref=landing.at[there],
            dst_ref=landing.at[there],
            send_sem=ar_send.at[g],
            recv_sem=ar_recv.at[g],
            device_id=far_id(far_peer(k)),
            device_id_type=MESH,
        )

    def ag_copy(g, k):
        landing = sums[g][4]
        return pltpu.make_async_remote_copy(
            src_ref=landing.at[here],
            dst_ref=landing.at[here],
            send_sem=ag_send.at[g],
            recv_sem=ag_recv.at[g],
            device_id=near_id(near_peer(k)),
            device_id_type=MESH,
        )

    def wait_bytes(sem, pieces):
        pltpu.make_async_copy(pieces, pieces, sem).wait()

    def start_scatter(g):
        total, part, _, _, _, cut = sums[g]
        for j in range(near):
            if cut[j] is None:
                part[j] = jnp.zeros(part.shape[1:], bf16)
            else:
                row, rows, lane, lanes = cut[j]
                part[j] = total[row : row + rows, lane : lane + lanes].astype(bf16)
        for k in range(1, near):
            rs_copy(g, k).start()

    def start_exchange(g):
        _, part, landing, mine, _, _ = sums[g]
        wait_bytes(rs_recv.at[g], landing.at[pl.ds(0, near - 1)])
        acc = part[here].astype(f32)
        for k in range(1, near):
            acc = acc + landing[near_peer(k)].astype(f32)
        mine[there] = acc.astype(bf16)
        for k in range(1, far):
            ar_copy(g, k).start()

    def start_gather(g):
        _, _, _, landing, result, _ = sums[g]
        wait_bytes(ar_recv.at[g], landing.at[pl.ds(0, far - 1)])
        acc = landing[0].astype(f32)
        for q in range(1, far):
            acc = acc + landing[q].astype(f32)
        result[here] = acc.astype(bf16)
        for k in range(1, near):
            ag_copy(g, k).start()

    def wait_gather(g):
        wait_bytes(ag_recv.at[g], sums[g][4].at[pl.ds(0, near - 1)])

    def wait_scatter_sent(g):
        wait_bytes(rs_send.at[g], sums[g][1].at[pl.ds(0, near - 1)])

    def wait_exchange_sent(g):
        wait_bytes(ar_send.at[g], sums[g][3].at[pl.ds(0, far - 1)])

    def wait_gather_sent(g):
        wait_bytes(ag_send.at[g], sums[g][4].at[pl.ds(0, near - 1)])

    start_halo(FEAT)
    for name in ("w_enc", "w_mid", "w_dec", "w_out", "labels"):
        loads[name].wait()
    forward_weights(w_enc_f, w_enc)

    def enc_tiles(x, tiles):
        pre = conv(w_enc_f, F, x, tiles)
        s = sigmoid(pre)
        slope = s * (1.0 + pre * (1.0 - s))
        act = (pre * s).astype(bf16).astype(f32)
        for at, y in enumerate(tiles):
            lanes = slice(at * LANES, (at + 1) * LANES)
            enc_slope[x, :, lane_tile(y)] = slope[:, lanes]
            JE[x + 1, 32:64, lane_tile(y + 1)] = act[:, lanes].astype(bf16)

    def enc_inner(x, carry):
        for tiles in inner_pairs(ny):
            enc_tiles(x, tiles)
        return carry

    each(1, nx - 1, enc_inner, 0)
    turned_weights(w_mid_f, w_mid)
    window_weights(skip_weights, w_dec, 64, 96)
    window_weights(up_weights, w_dec, 0, 64)
    out_total[...] = jnp.zeros(out_total.shape, f32)
    wait_halo(FEAT, False)
    finish_halo(F, nx, ny, 32, 32, 0, 1, part=False)
    for x in range(1, nx - 1):
        enc_tiles(x, (0, ny - 1))
    wait_halo(FEAT, True)
    finish_halo(F, nx, ny, 32, 32, 0, 1, part=True)
    for x in (0, nx - 1):
        for tiles in all_pairs(ny):
            enc_tiles(x, tiles)

    def pool_block(bx, carry):
        for by in range(cy):
            block = jnp.zeros((32, LANES), f32)
            for dx in range(2):
                for dy in range(2):
                    block += JE[2 * bx + dx + 1, 32:64, lane_tile(2 * by + dy + 1)].astype(f32)
            pooled = (pair_sum(block) * 0.125).astype(bf16).astype(f32)
            PP[bx + 1, :, lane_tile(by + 1)] = packed(pooled)
            PO[bx + 1, 32:64, lane_tile(by + 1)] = pooled.astype(bf16)
        return carry

    each(0, cx, pool_block, 0)
    start_halo(POOL)
    start_halo(SKIP)
    finish_inner(PO, cx, cy, 32, 2)
    finish_inner(JE, nx, ny, 32, 1)
    local_part(window_sums, skip_weights, JE, nx, ny, True)
    turned_weights(w_enc_b, w_enc)
    turned_weights(w_dec_b, w_dec)
    for low in range(0, 27, 2):
        high = min(low + 2, 27)
        w_mid_b[:, low * 64 : high * 64] = laid_lanes(w_mid, range(low, high))
    wait_halo(POOL)
    unpack_halo(PO, PP, cx, cy, 32)

    def mid_block(bx, carry):
        for by in range(0, cy, 2):
            pre = conv(w_mid_f, PO, bx, (by, by + 1))
            s = sigmoid(pre)
            mid_slope[bx, :, lane_tile(by, 2)] = s * (1.0 + pre * (1.0 - s))
            act = (pre * s).astype(bf16)
            for dy in range(2):
                tile = act[:, dy * LANES : (dy + 1) * LANES]
                UP[bx + 1, :, lane_tile(by + dy + 1)] = packed(tile.astype(f32))
                JU[2 * bx + 1, 64:128, lane_tile(2 * (by + dy) + 1)] = tile
        return carry

    each(0, cx, mid_block, 0)
    start_halo(MID)

    def spread(bx, by, tile):
        before, after = shifted(tile, 1)
        tile = tile.astype(bf16)
        for x in (2 * bx - 1, 2 * bx):
            for y in (2 * by - 1, 2 * by):
                if 0 <= x <= nx + 1 and 0 <= y <= ny + 1:
                    lanes = lane_tile(y)
                    JU[x, 0:64, lanes] = before
                    JU[x, 64:128, lanes] = tile
                    JU[x, 128:192, lanes] = after

    for bx in range(1, cx + 1):
        for by in range(1, cy + 1):
            spread(bx, by, JU[2 * bx - 1, 64:128, lane_tile(2 * by - 1)].astype(f32))
    local_part(window_sums, up_weights, JU, nx, ny, False)
    wait_halo(SKIP)
    finish_halo(JE, nx, ny, 32, 32, 0, 1)
    border_sides(window_sums, skip_weights, JE, nx, ny, True)
    border_rows(window_sums, skip_weights, JE, nx, ny)
    for part in (False, True):
        wait_halo(MID, part)
        over_halo(cx, cy, lambda bx, by: spread(bx, by, unpacked(UP[bx, :, lane_tile(by)])), part)
        if part:
            border_rows(window_sums, up_weights, JU, nx, ny)
        else:
            border_sides(window_sums, up_weights, JU, nx, ny, False)

    def dec_row(x, carry):
        pre = (
            window_sums[x, 0:32, lane_tile(0, ny)]
            + window_sums[x, 32:64, lane_tile(1, ny)]
            + window_sums[x, 64:96, lane_tile(2, ny)]
        )
        s = sigmoid(pre)
        slope = s * (1.0 + pre * (1.0 - s))
        act = (pre * s).astype(bf16)
        logits = jnp.dot(w_out[...], act, preferred_element_type=f32)
        expo = jnp.exp(logits)
        prob = expo / jnp.sum(expo, axis=0, keepdims=True)
        ids = lax.broadcasted_iota(jnp.int32, prob.shape, 0)
        these = jnp.concatenate([labels[x, y : y + 1, :] for y in range(ny)], axis=1)
        onehot = (these == ids).astype(f32)
        logit_grad = (loss_scale * (prob - onehot)).astype(bf16)
        out_total[...] += lax.dot_general(
            logit_grad, act, (((1,), (1,)), ((), ())), preferred_element_type=f32
        )
        act_grad = lax.dot_general(
            w_out[...], logit_grad, (((0,), (0,)), ((), ())), preferred_element_type=f32
        )
        grads = (act_grad * slope).astype(bf16).astype(f32)
        for y in range(ny):
            tile = grads[:, y * LANES : (y + 1) * LANES]
            D[x + 1, 32:64, lane_tile(y + 1)] = tile.astype(bf16)
        return carry

    each(0, nx, dec_row, 0)
    start_halo(DECG)
    finish_inner(D, nx, ny, 32, 1, back=True)

    def dec_back(x, tiles):
        grads = conv(w_dec_b, D, x, tiles, back=True)
        for at, y in enumerate(tiles):
            joined_grad[x, :, lane_tile(y)] = grads[:, at * LANES : (at + 1) * LANES]

    def dec_back_inner(x, carry):
        for tiles in inner_pairs(ny):
            dec_back(x, tiles)
        return carry

    each(1, nx - 1, dec_back_inner, 0)
    joined = [(JU, 64, 64), (JE, 32, 32)]
    weight_grad(total_dec, lambda x: D[x + 1, :, lane_tile(1, ny)], joined, nx, ny)
    total_dec[0:4, 864:896] = out_total[...]
    start_scatter(DEC)

    wait_halo(DECG, False)
    finish_halo(D, nx, ny, 32, 32, 0, 1, back=True, part=False)
    for x in range(1, nx - 1):
        dec_back(x, (0, ny - 1))
    wait_halo(DECG, True)
    finish_halo(D, nx, ny, 32, 32, 0, 1, back=True, part=True)
    for x in (0, nx - 1):
        for tiles in all_pairs(ny):
            dec_back(x, tiles)

    def mid_grads(bx, carry):
        for by in range(cy):
            block = jnp.zeros((64, LANES), f32)
            for dx in range(2):
                for dy in range(2):
                    block += joined_grad[2 * bx + dx, 0:64, lane_tile(2 * by + dy)]
            grads = pair_sum(block) * mid_slope[bx, :, lane_tile(by)]
            grads = grads.astype(bf16).astype(f32)
            MGP[bx + 1, :, lane_tile(by + 1)] = packed(grads)
            MG[bx + 1, 64:128, lane_tile(by + 1)] = grads.astype(bf16)
        return carry

    each(0, cx, mid_grads, 0)
    start_halo(MIDG)
    finish_inner(MG, cx, cy, 64, 2, back=True)

    weight_grad(total_mid, lambda x: MG[x + 1, 64:128, lane_tile(1, cy)], [(PO, 0, 96)], cx, cy)
    start_scatter(MIDW)
    start_exchange(DEC)

    wait_halo(MIDG)
    start_exchange(MIDW)
    unpack_halo(MG, MGP, cx, cy, 64, back=True)

    def mid_back(bx, carry):
        for by in range(0, cy, 2):
            pooled = conv(w_mid_b, MG, bx, (by, by + 1), back=True) * 0.125
            for dx in range(2):
                x = 2 * bx + dx
                for dy in range(4):
                    y = 2 * by + dy
                    up = pooled[:, (dy // 2) * LANES : (dy // 2 + 1) * LANES]
                    tile = (joined_grad[x, 64:96, lane_tile(y)] + up) * enc_slope[x, :, lane_tile(y)]
                    put_stack(EG, x + 1, y + 1, tile, 32, 0, 1, back=True)
        return carry

    each(0, cx, mid_back, 0)

    weight_grad(total_enc, lambda x: EG[x + 1, :, lane_tile(1, ny)], [(F, 32, 32)], nx, ny)
    start_scatter(ENC)
    start_halo(ENCG)

    def enc_back(x, tiles):
        grads = conv(w_enc_b, EG, x, tiles, back=True)
        for at, y in enumerate(tiles):
            rows32[x, pl.ds(y, 32, stride=ny), :] = grads[:, at * LANES : (at + 1) * LANES]

    def enc_back_inner(x, carry):
        for tiles in inner_pairs(ny):
            enc_back(x, tiles)
        return carry

    each(1, nx - 1, enc_back_inner, 0)
    start_exchange(ENC)
    wait_halo(ENCG)
    finish_halo(EG, nx, ny, 32, 32, 0, 1, back=True)

    def enc_back_sides(x, carry):
        enc_back(x, (0, ny - 1))
        return carry

    each(1, nx - 1, enc_back_sides, 0)

    def enc_back_ends(i, carry):
        for tiles in all_pairs(ny):
            enc_back(i * (nx - 1), tiles)
        return carry

    each(0, 2, enc_back_ends, 0)

    def lay_out(x, carry):
        feature_grad[:, x] = rows32[x].reshape(32, ny, LANES).astype(bf16)
        return carry

    each(0, nx, lay_out, 0)
    stores = [
        pltpu.make_async_copy(source, dest, store_sem.at[at])
        for at, (source, dest) in enumerate(
            (
                (feature_grad, feature_grad_hbm),
                (ag_dec, sum_dec),
                (ag_mid, sum_mid),
                (ag_enc, sum_enc),
            )
        )
    ]
    stores[0].start()
    start_gather(DEC)
    start_gather(MIDW)
    for field in range(7):
        wait_halo_sent(field)
    for g in (DEC, MIDW, ENC):
        wait_scatter_sent(g)
    start_gather(ENC)
    wait_gather(DEC)
    stores[1].start()
    wait_gather(MIDW)
    stores[2].start()
    for g in (DEC, MIDW, ENC):
        wait_exchange_sent(g)
    for g in (DEC, MIDW):
        wait_gather_sent(g)
    wait_gather(ENC)
    stores[3].start()
    wait_gather_sent(ENC)
    for store in stores:
        store.wait()


def outputs(
    scale,
    features_in,
    dec_in,
    mid_in,
    enc_in,
    features_out,
    enc_out,
    mid_out,
    dec_out,
    out_out,
    features,
    sum_dec,
    sum_mid,
    sum_enc,
    grad_enc,
    grad_mid,
    grad_dec,
    grad_out,
    sems,
):
    copies = [
        pltpu.make_async_copy(source, dest, sems.at[at])
        for at, (source, dest) in enumerate(
            (
                (dec_in, sum_dec),
                (mid_in, sum_mid),
                (enc_in, sum_enc),
                (features_in, features),
                (grad_dec, dec_out),
                (grad_out, out_out),
                (grad_mid, mid_out),
                (grad_enc, enc_out),
                (features, features_out),
            )
        )
    ]
    for copy in copies[:4]:
        copy.start()
    copies[0].wait()
    whole = jnp.concatenate([sum_dec[j].astype(f32) for j in range(8)], axis=1) * scale
    for t in range(27):
        window, c = divmod(t, 3)
        grad_dec[t] = whole[c * 32 : (c + 1) * 32, window * 96 : (window + 1) * 96]
    grad_out[...] = whole[0:4, 864:896]
    copies[4].start()
    copies[5].start()
    copies[3].wait()
    copies[8].start()
    copies[1].wait()
    for j in range(7):
        turned = (sum_mid[j].astype(f32) * (0.5 * scale)).T
        for t in range(4 * j, min(4 * j + 4, 27)):
            grad_mid[t] = turned[(t % 4) * 32 : (t % 4 + 1) * 32]
    copies[6].start()
    copies[2].wait()
    for window in range(9):
        j, at = divmod(window, 4)
        both = jnp.concatenate([sum_enc[2 * j], sum_enc[2 * j + 1]], axis=0)
        part = both[:, at * 32 : (at + 1) * 32].astype(f32) * scale
        for c in range(3):
            grad_enc[window * 3 + c] = part[c * 32 : (c + 1) * 32]
    copies[7].start()
    for copy in copies[4:]:
        copy.wait()


def shards(features, labels, w_enc, w_mid, w_dec, w_out):
    nb, nsx, nsy = lax.axis_size("batch"), lax.axis_size("sx"), lax.axis_size("sy")
    _, chans, nx, ny, nz = features.shape
    cx, cy = nx // 2, ny // 2
    scale = 1.0 / float(nb * nsx * nsy * nx * ny * nz)
    near, far = nb * (nsy // 2), nsx * 2

    def fine(depth):
        return pltpu.VMEM((nx + 2, depth, (ny + 2) * LANES), bf16)

    def coarse(depth):
        return pltpu.VMEM((cx + 2, depth, (cy + 2) * LANES), bf16)

    pieces = ((96, 128), (64, 128), (48, 128))
    scratch = [
        pltpu.VMEM((chans, nx, ny, nz), bf16),
        pltpu.VMEM((nx, ny, nz), jnp.int32),
        pltpu.VMEM((27, 32, 32), bf16),
        pltpu.VMEM((27, 32, 64), bf16),
        pltpu.VMEM((27, 32, 96), bf16),
        pltpu.VMEM((4, 32), bf16),
        pltpu.SemaphoreType.DMA((6,)),
        pltpu.VMEM((chans, nx, ny, nz), bf16),
        pltpu.SemaphoreType.DMA((4,)),
        pltpu.VMEM((32, 864), bf16),
        pltpu.VMEM((32, 864), bf16),
        pltpu.VMEM((64, 864), bf16),
        pltpu.VMEM((32, 1728), bf16),
        *[pltpu.VMEM((96, 96 * count), bf16) for count in (3, 2, 2, 1, 1)],
        *[pltpu.VMEM((96, 192 * count), bf16) for count in (3, 2, 2, 1, 1)],
        pltpu.VMEM((96, 864), bf16),
        pltpu.VMEM((nx, 32 * ny, LANES), f32),
        pltpu.VMEM((nx, 96, (ny + 2) * LANES), f32),
        fine(96),
        coarse(96),
        coarse(16),
        coarse(32),
        fine(192),
        fine(96),
        fine(96),
        coarse(192),
        coarse(32),
        fine(96),
        pltpu.VMEM((nx, 32, ny * LANES), f32),
        pltpu.VMEM((cx, 64, cy * LANES), f32),
        pltpu.VMEM((nx, 96, ny * LANES), f32),
        pltpu.VMEM((4, 32), f32),
        pltpu.VMEM((96, 1024), f32),
        pltpu.VMEM((64, 1024), f32),
        pltpu.VMEM((96, 384), f32),
    ]
    scratch += [pltpu.VMEM((near, rows, length), bf16) for rows, length in pieces]
    scratch += [pltpu.VMEM((near, rows, length), bf16) for rows, length in pieces]
    scratch += [pltpu.VMEM((far, rows, length), bf16) for rows, length in pieces]
    scratch += [pltpu.VMEM((near, rows, length), bf16) for rows, length in pieces]
    scratch += [pltpu.SemaphoreType.DMA((7, 8))] * 2
    scratch += [pltpu.SemaphoreType.DMA((3,))] * 2
    scratch += [pltpu.SemaphoreType.DMA((3,))] * 2
    scratch += [pltpu.SemaphoreType.DMA((3,))] * 2

    vmem = pl.BlockSpec(memory_space=pltpu.VMEM)
    partial_outputs = pl.pallas_call(
        functools.partial(kernel, (nb, nsx, nsy, nx, ny)),
        out_shape=(
            jax.ShapeDtypeStruct((chans, nx, ny, nz), bf16),
            *[jax.ShapeDtypeStruct((near, rows, length), bf16) for rows, length in pieces],
        ),
        in_specs=[pl.BlockSpec(memory_space=pl.ANY)] * 6,
        out_specs=[pl.BlockSpec(memory_space=pl.ANY)] * 4,
        scratch_shapes=scratch,
        compiler_params=pltpu.CompilerParams(
            collective_id=0, has_side_effects=True, vmem_limit_bytes=62 * 1024 * 1024
        ),
        name="unet_step",
    )(
        features[0],
        labels[0],
        w_enc.reshape(27, 32, 32),
        w_mid.swapaxes(3, 4).reshape(27, 32, 64),
        w_dec.reshape(27, 32, 96),
        w_out,
    )
    feature_grad, grad_enc, grad_mid, grad_dec, grad_out = pl.pallas_call(
        functools.partial(outputs, scale),
        out_shape=(
            jax.ShapeDtypeStruct((chans, nx, ny, nz), bf16),
            jax.ShapeDtypeStruct((27, 32, 32), f32),
            jax.ShapeDtypeStruct((27, 32, 64), f32),
            jax.ShapeDtypeStruct((27, 32, 96), f32),
            jax.ShapeDtypeStruct((4, 32), f32),
        ),
        in_specs=[pl.BlockSpec(memory_space=pl.ANY)] * 4,
        out_specs=[pl.BlockSpec(memory_space=pl.ANY)] * 5,
        scratch_shapes=[
            pltpu.VMEM((chans, nx, ny, nz), bf16),
            *[pltpu.VMEM((near, rows, length), bf16) for rows, length in pieces],
            pltpu.VMEM((27, 32, 32), f32),
            pltpu.VMEM((27, 32, 64), f32),
            pltpu.VMEM((27, 32, 96), f32),
            pltpu.VMEM((4, 32), f32),
            pltpu.SemaphoreType.DMA((9,)),
        ],
        compiler_params=pltpu.CompilerParams(vmem_limit_bytes=62 * 1024 * 1024),
        name="unet_outputs",
    )(*partial_outputs)
    return (
        feature_grad[None],
        grad_enc.reshape(w_enc.shape),
        grad_mid.reshape(3, 3, 3, 32, 64).swapaxes(3, 4),
        grad_dec.reshape(w_dec.shape),
        grad_out,
    )


def solution(mesh):
    placed = (P("batch", None, "sx", "sy", None), P("batch", "sx", "sy", None), P(), P(), P(), P())
    return jax.shard_map(
        shards,
        mesh=mesh,
        in_specs=placed,
        out_specs=(P("batch", None, "sx", "sy", None), P(), P(), P(), P()),
        check_vma=False,
    )
```
